32 devices in a mesh: row: 4 (over z), col: 8 (over y, x, core).
Axes of the slice: x: 2, y: 2, z: 4, core: 2. Of those that a mesh axis runs over, the one named last changes fastest.
Arguments:
- tokens: bfloat16 [512, 4096], P('row', 'col'), may hold values from -6 to 6
- upstream: bfloat16 [512, 4096], P('row', 'col'), may hold values from -6 to 6
- w_in: bfloat16 [8, 64, 256, 256], P('col', 'row'), may hold values from -0.1875 to 0.1875
- in_codes: int32 [8, 64], P('col'), may hold values from -1 to 127, as said below
- w_out: bfloat16 [8, 64, 256, 256], P('col', 'row'), may hold values from -0.09375 to 0.09375
- out_codes: int32 [8, 64], P('col'), may hold values from -1 to 127, as said below
Outputs:
- layer_out: bfloat16 [512, 4096], P('row', 'col')
- grad_tokens: bfloat16 [512, 4096], P('row', 'col')
- grad_w_in: bfloat16 [8, 64, 256, 256], P('col', 'row')
- grad_w_out: bfloat16 [8, 64, 256, 256], P('col', 'row')
The draws below stay inside these ranges and needn't reach their ends.
Inputs may be any that keep to these rules, and one draw needn't show every extreme that they name: `in_codes`: row c describes panel c's 64 slots: a code k names input tile row k // 8 and local hidden tile column k % 8; -1 marks an empty slot. Codes of a row are distinct, every row has one filled slot or more, and some row has all 64 slots filled. `out_codes`: row c describes panel c's 64 slots: a code k names output tile column k // 8 and local hidden tile row k % 8; -1 marks an empty slot. Codes of a row are distinct, every row has one filled slot or more, and some row has all 64 slots filled.
All inputs are finite; a program needn't handle non-finite values.
Results may differ from the reference program's by a relative error of at most 0.015.
Values may be sent and summed in bfloat16 or wider, within the bound.
No kernel may reach another device: no remote copies, remote signals or barrier semaphores. Data moves between devices by JAX's collectives and lax.ppermute only.
A program may use at most 128 MiB of HBM per device.

```python
import jax
import jax.numpy as jnp
from jax import lax

D = 4096
FF = 16384
TILE = 256
TOKENS = 512
PANELS = 8
CAP = 64


def draw_codes(key, salt_value):
    base_key = jax.random.fold_in(key, salt_value)
    tiles_all = D // TILE * (FF // (TILE * PANELS))
    full_panel = jax.random.randint(jax.random.fold_in(base_key, 1), (), 0, PANELS)

    def one_panel(panel_id):
        panel_key = jax.random.fold_in(base_key, panel_id + 7)
        chosen = jax.random.permutation(jax.random.fold_in(panel_key, 1), tiles_all)[:CAP].astype(jnp.int32)
        slot_rank = jax.random.permutation(jax.random.fold_in(panel_key, 2), CAP).astype(jnp.int32)
        filled = jax.random.randint(jax.random.fold_in(panel_key, 3), (), 1, CAP + 1)
        is_full = panel_id == full_panel
        filled = jnp.where(is_full, CAP, filled)
        shifted = (chosen + (tiles_all - 1 - chosen[0])) % tiles_all
        chosen = jnp.where(is_full, shifted, chosen)
        return jnp.where(slot_rank < filled, chosen, -1).astype(jnp.int32)
    return jax.vmap(one_panel)(jnp.arange(PANELS, dtype=jnp.int32))


def draw_in_codes(key, part):
    return draw_codes(key, 11)


def draw_out_codes(key, part):
    return draw_codes(key, 23)


def levels(key, extent, shards, smallest, high):
    level, own = 1.0, jax.random.fold_in(key, 6)
    for axis_at, blocks in shards:
        draws = jnp.exp(jax.random.uniform(jax.random.fold_in(own, axis_at), (blocks,), jnp.float32, smallest / len(shards), high / len(shards)))
        level = level * jnp.repeat(draws, extent[axis_at] // blocks).reshape([-1 if axis == axis_at else 1 for axis in range(len(extent))])
    return level


def gaussian(stream_key, shape, deviation, bound, cuts=(), held_as=jnp.bfloat16):
    gain = levels(stream_key, shape, cuts, -0.22, 0.18) if cuts else 1.0
    values = jax.random.normal(stream_key, shape, jnp.float32) * deviation * gain
    return jnp.minimum(jnp.maximum(values, -bound), bound).astype(held_as)


def setup_inputs(seed: int = 0) -> dict:
    seeds = jax.random.split(jax.random.key(seed), 7)
    tokens = gaussian(seeds[0], (TOKENS, D), 1.0, 6.0, ((0, 4), (1, 8)))
    upstream = gaussian(seeds[1], (TOKENS, D), 1.0, 6.0, ((0, 4), (1, 8)))
    w_in = gaussian(seeds[2], (PANELS, CAP, TILE, TILE), (D // 4) ** -0.5, 0.1875, ((0, 8), (1, 4)))
    in_codes = draw_in_codes(jax.random.fold_in(seeds[6], 71), 0)
    w_out = gaussian(seeds[4], (PANELS, CAP, TILE, TILE), (FF // 4) ** -0.5, 0.09375, ((0, 8), (1, 4)))
    out_codes = draw_out_codes(jax.random.fold_in(seeds[6], 71), 0)
    return {"tokens": tokens, "upstream": upstream, "w_in": w_in, "in_codes": in_codes, "w_out": w_out, "out_codes": out_codes}


def silu_slope(hidden):
    sigmoid_value = jax.nn.sigmoid(hidden)
    return sigmoid_value * (1.0 + hidden * (1.0 - sigmoid_value))


def split_codes(slot_codes, tile_cols):
    filled = slot_codes >= 0
    clipped = jnp.maximum(slot_codes, 0)
    return (clipped // tile_cols).astype(jnp.int32), (clipped % tile_cols).astype(jnp.int32), filled


def selector(position, filled, classes):
    matches = position[:, None] == jnp.arange(classes, dtype=jnp.int32)[None, :]
    return (matches & filled[:, None]).astype(jnp.float32)


def reference(tokens, upstream, w_in, in_codes, w_out, out_codes):
    tile_rows = D // TILE
    tile_cols = FF // (TILE * PANELS)
    token_tiles = tokens.reshape(TOKENS, tile_rows, TILE)
    up_tiles = upstream.reshape(TOKENS, tile_rows, TILE)
    highest = lax.Precision.HIGHEST

    def panel_step(carry, panel_data):
        layer_total, input_total = carry
        codes_in, tiles_in, codes_out, tiles_out = panel_data
        in_row, in_col, in_filled = split_codes(codes_in, tile_cols)
        out_row, out_col, out_filled = split_codes(codes_out, tile_cols)
        tiles_in32 = tiles_in.astype(jnp.float32)
        tiles_out32 = tiles_out.astype(jnp.float32)
        picked_tokens = jnp.take(token_tiles, in_row, axis=1).astype(jnp.float32)
        products = jnp.einsum('tkd,kdn->tkn', picked_tokens, tiles_in32)
        hidden = jnp.einsum('tkn,kj->tjn', products, selector(in_col, in_filled, tile_cols), precision=highest)
        activ = jax.nn.silu(hidden).astype(jnp.bfloat16)
        picked_activ = jnp.take(activ, out_col, axis=1).astype(jnp.float32)
        out_products = jnp.einsum('tkf,kfd->tkd', picked_activ, tiles_out32)
        layer_part = jnp.einsum('tkd,ki->tid', out_products, selector(out_row, out_filled, tile_rows), precision=highest)
        layer_part = lax.optimization_barrier(layer_part.reshape(TOKENS, D).astype(jnp.bfloat16)).astype(jnp.float32)
        picked_up = jnp.take(up_tiles, out_row, axis=1).astype(jnp.float32)
        back_products = jnp.einsum('tkd,kfd->tkf', picked_up, tiles_out32)
        grad_activ = jnp.einsum('tkf,kj->tjf', back_products, selector(out_col, out_filled, tile_cols), precision=highest)
        grad_hidden = (grad_activ * silu_slope(hidden)).astype(jnp.bfloat16)
        picked_grad = jnp.take(grad_hidden, in_col, axis=1).astype(jnp.float32)
        in_products = jnp.einsum('tkf,kdf->tkd', picked_grad, tiles_in32)
        input_part = jnp.einsum('tkd,ki->tid', in_products, selector(in_row, in_filled, tile_rows), precision=highest)
        input_part = lax.optimization_barrier(input_part.reshape(TOKENS, D).astype(jnp.bfloat16)).astype(jnp.float32)
        grad_in = jnp.einsum('tkd,tkn->kdn', picked_tokens, picked_grad)
        grad_in = jnp.where(in_filled[:, None, None], grad_in, 0.0).astype(jnp.bfloat16)
        grad_out = jnp.einsum('tkf,tkd->kfd', picked_activ, picked_up)
        grad_out = jnp.where(out_filled[:, None, None], grad_out, 0.0).astype(jnp.bfloat16)
        return (layer_total + layer_part, input_total + input_part), (grad_in, grad_out)

    zeros = jnp.zeros((TOKENS, D), jnp.float32)
    totals, grads = lax.scan(panel_step, (zeros, zeros), (in_codes, w_in, out_codes, w_out))
    return totals[0].astype(jnp.bfloat16), totals[1].astype(jnp.bfloat16), grads[0], grads[1]
```

```python
import functools

import jax
import jax.numpy as jnp
from jax import lax
from jax.experimental import pallas as pl
from jax.experimental.pallas import tpu as pltpu
from jax.sharding import PartitionSpec as P

D = 4096
FF = 16384
VMEM = 56 * 1024 * 1024


def params():
    return pltpu.CompilerParams(
        dimension_semantics=("arbitrary",), vmem_limit_bytes=VMEM
    )


def matmul(a, b, a_dim, b_dim):
    return lax.dot_general(
        a, b, (((a_dim,), (b_dim,)), ((), ())), preferred_element_type=jnp.float32
    )


def rows_of(ref, at):
    block = ref[:, at]
    return block.reshape(block.shape[0] * block.shape[1], block.shape[2])


def place(code, cols, forward):
    wide, hidden = code // cols, code % cols
    return (wide, hidden) if forward else (hidden, wide)


def to_hidden_kernel(cols, flip, codes, x_ref, w_ref, o_ref, acc):
    group, _, rows, tile = x_ref.shape
    acc[...] = jnp.zeros_like(acc)

    def slot(s, carry):
        code = codes[s]

        @pl.when(code >= 0)
        def _():
            source, target = place(code, cols, True)
            acc[target] += matmul(rows_of(x_ref, source), w_ref[s], 1, 1 if flip else 0)

        return carry

    lax.fori_loop(0, w_ref.shape[0], slot, 0)
    for part in range(group):
        o_ref[part] = acc[:, part * rows:(part + 1) * rows].astype(o_ref.dtype)


def to_hidden(x, w, codes, cols, flip):
    blocks, wide, rows, tile = x.shape
    group = min(blocks, 4)
    slots = w.shape[0]
    return pl.pallas_call(
        functools.partial(to_hidden_kernel, cols, flip),
        grid_spec=pltpu.PrefetchScalarGridSpec(
            num_scalar_prefetch=1,
            grid=(blocks // group,),
            in_specs=[
                pl.BlockSpec((group, wide, rows, tile), lambda b, codes: (b, 0, 0, 0)),
                pl.BlockSpec((slots, tile, tile), lambda b, codes: (0, 0, 0)),
            ],
            out_specs=pl.BlockSpec((group, cols, rows, tile), lambda b, codes: (b, 0, 0, 0)),
            scratch_shapes=[pltpu.VMEM((cols, group * rows, tile), jnp.float32)],
        ),
        out_shape=jax.ShapeDtypeStruct((blocks, cols, rows, tile), jnp.bfloat16),
        compiler_params=params(),
    )(codes, x, w)


def from_hidden_kernel(cols, flip, codes, h_ref, x_ref, w_ref, o_ref, g_ref, acc, grad):
    group, _, rows, tile = x_ref.shape
    acc[...] = jnp.zeros_like(acc)

    @pl.when(pl.program_id(0) == 0)
    def _():
        grad[...] = jnp.zeros_like(grad)

    def slot(s, carry):
        code = codes[s]

        @pl.when(code >= 0)
        def _():
            source, target = place(code, cols, False)
            h, x = rows_of(h_ref, source), rows_of(x_ref, target)
            acc[target] += matmul(h, w_ref[s], 1, 1 if flip else 0)
            grad[s] += matmul(x, h, 0, 0) if flip else matmul(h, x, 0, 0)

        return carry

    lax.fori_loop(0, w_ref.shape[0], slot, 0)
    for part in range(group):
        o_ref[part] = acc[:, part * rows:(part + 1) * rows].astype(o_ref.dtype)

    @pl.when(pl.program_id(0) == pl.num_programs(0) - 1)
    def _():
        g_ref[...] = grad[...].astype(g_ref.dtype)


def from_hidden(h, x, w, codes, flip, held):
    blocks, cols, rows, tile = h.shape
    wide = x.shape[1]
    group = min(blocks, 4)
    slots = w.shape[0]
    return pl.pallas_call(
        functools.partial(from_hidden_kernel, cols, flip),
        grid_spec=pltpu.PrefetchScalarGridSpec(
            num_scalar_prefetch=1,
            grid=(blocks // group,),
            in_specs=[
                pl.BlockSpec((group, cols, rows, tile), lambda b, codes: (b, 0, 0, 0)),
                pl.BlockSpec((group, wide, rows, tile), lambda b, codes: (b, 0, 0, 0)),
                pl.BlockSpec((slots, tile, tile), lambda b, codes: (0, 0, 0)),
            ],
            out_specs=[
                pl.BlockSpec((group, wide, rows, tile), lambda b, codes: (b, 0, 0, 0)),
                pl.BlockSpec((slots, tile, tile), lambda b, codes: (0, 0, 0)),
            ],
            scratch_shapes=[
                pltpu.VMEM((wide, group * rows, tile), jnp.float32),
                pltpu.VMEM((slots, tile, tile), jnp.float32),
            ],
        ),
        out_shape=[
            jax.ShapeDtypeStruct((blocks, wide, rows, tile), jnp.bfloat16),
            jax.ShapeDtypeStruct((slots, tile, tile), held),
        ],
        compiler_params=params(),
    )(codes, h, x, w)


def to_pieces(x, tile):
    rows, width = x.shape
    unit = min(width, tile)
    return jnp.swapaxes(x.reshape(rows, width // unit, unit), 0, 1)


def join_pieces(x, tile):
    blocks, devices, pieces, rows, unit = x.shape
    parts = tile // unit
    x = x.reshape(blocks, devices * pieces // parts, parts, rows, unit)
    return jnp.swapaxes(x, 2, 3).reshape(blocks, -1, rows, tile)


def cut_pieces(x, devices):
    blocks, tiles, rows, tile = x.shape
    unit = min(tile, tiles * tile // devices)
    x = jnp.swapaxes(x.reshape(blocks, tiles, rows, tile // unit, unit), 2, 3)
    x = x.reshape(blocks, devices, -1, rows, unit)
    return jnp.swapaxes(x, 0, 1)


def finish(hidden_side, x, w, codes, flip, devices):
    blocks = x.shape[0]
    group = min(blocks, 4)
    held = jnp.bfloat16 if group == blocks else jnp.float32
    sums, grad = [], None
    for at in range(0, blocks, group):
        h, wide = hidden_side[at:at + group], x[at:at + group]
        if sums:
            h, wide, _ = lax.optimization_barrier((h, wide, sums[-1]))
        part, slots_grad = from_hidden(h, wide, w, codes, flip, held)
        grad = slots_grad if grad is None else grad + slots_grad
        sums.append(lax.psum_scatter(cut_pieces(part, devices), "col", scatter_dimension=0))
    own = lax.psum_scatter(jnp.concatenate(sums), "row", scatter_dimension=0)
    return jnp.swapaxes(own, 0, 1).reshape(own.shape[1], -1), grad.astype(jnp.bfloat16)


def per_device(tokens, upstream, w_in, in_codes, w_out, out_codes):
    tile = w_in.shape[3]
    slots = w_in.shape[1]
    devices = lax.axis_size("col")
    blocks = lax.axis_size("row")
    cols = FF // (tile * devices)
    first = lax.axis_index("row") * slots
    codes_in = lax.dynamic_slice_in_dim(in_codes[0], first, slots)
    codes_out = lax.dynamic_slice_in_dim(out_codes[0], first, slots)

    def everywhere(x):
        pieces = lax.all_gather(to_pieces(x, tile), ("row", "col"))
        return join_pieces(pieces.reshape(blocks, devices, *pieces.shape[1:]), tile)

    all_tokens = everywhere(tokens)
    hidden = to_hidden(all_tokens, w_in[0], codes_in, cols, False)
    if blocks > 4:
        upstream, hidden = lax.optimization_barrier((upstream, hidden))
    all_up = everywhere(upstream)
    hidden = lax.psum_scatter(hidden, "row", scatter_dimension=0).astype(jnp.float32)
    grad_activ = to_hidden(all_up, w_out[0], codes_out, cols, True)
    grad_activ = lax.psum_scatter(grad_activ, "row", scatter_dimension=0).astype(jnp.float32)
    sigmoid = jax.nn.sigmoid(hidden)
    activ = (hidden * sigmoid).astype(jnp.bfloat16)
    grad_hidden = grad_activ * sigmoid * (1.0 + hidden * (1.0 - sigmoid))
    grad_hidden = grad_hidden.astype(jnp.bfloat16)
    all_activ = lax.all_gather(activ, "row")
    all_grad = lax.all_gather(grad_hidden, "row")
    layer_out, grad_w_out = finish(all_activ, all_up, w_out[0], codes_out, False, devices)
    if blocks > 4:
        all_grad, layer_out = lax.optimization_barrier((all_grad, layer_out))
    grad_tokens, grad_w_in = finish(all_grad, all_tokens, w_in[0], codes_in, True, devices)
    return layer_out, grad_tokens, grad_w_in[None], grad_w_out[None]


def solution(mesh):
    placed = (
        P("row", "col"),
        P("row", "col"),
        P("col", "row", None, None),
        P("col", None),
        P("col", "row", None, None),
        P("col", None),
    )
    return jax.shard_map(
        per_device,
        mesh=mesh,
        in_specs=placed,
        out_specs=(
            P("row", "col"),
            P("row", "col"),
            P("col", "row", None, None),
            P("col", "row", None, None),
        ),
        check_vma=False,
    )
```

```python
import functools

import jax
import jax.numpy as jnp
from jax import lax
from jax.experimental import pallas as pl
from jax.experimental.pallas import tpu as pltpu
from jax.sharding import PartitionSpec as P

D = 4096
FF = 16384
VMEM = 56 * 1024 * 1024
GROUP = 4
ANY = pl.BlockSpec(memory_space=pl.ANY)


def matmul(a, b, a_dim, b_dim):
    return lax.dot_general(
        a, b, (((a_dim,), (b_dim,)), ((), ())), preferred_element_type=jnp.float32
    )


def flat(block):
    return block.reshape(block.shape[0] * block.shape[1], block.shape[2])


def chunks(blocks):
    group = min(blocks, GROUP)
    return [slice(at, at + group) for at in range(0, blocks, group)]


def wide_copies(refs, held, sems, col):
    tile = held.shape[3]
    if len(refs[0].shape) == 5:
        refs = [refs[0].at[m] for m in range(refs[0].shape[0])]
    pieces, unit = refs[0].shape[1], refs[0].shape[3]
    copies = []
    for m, ref in enumerate(refs):
        owner = lax.bitwise_xor(col, m)
        for q in range(pieces):
            if unit == tile:
                target = held.at[owner * pieces + q]
            else:
                parts = tile // unit
                lane = pl.multiple_of(lax.rem(owner, parts) * unit, unit)
                target = held.at[lax.div(owner, parts), :, :, pl.ds(lane, unit)]
            copies.append(pltpu.make_async_copy(ref.at[:, q], target, sems.at[len(copies)]))
    for copy in copies:
        copy.start()
    return copies


def hidden_copies(refs, held, sems, row, at, blocks):
    copies = []
    for g in range(held.shape[1]):
        j = at + g
        target, sem = held.at[:, g], sems.at[g]
        if j == 0:
            copy = pltpu.make_async_copy(refs[0], target, sem)
            copy.start()
        else:
            copy = pltpu.make_async_copy(refs[blocks - 1 + j], target, sem)
            other = pltpu.make_async_copy(refs[blocks - j], target, sem)

            @pl.when(row + j < blocks)
            def _():
                copy.start()

            @pl.when(row + j >= blocks)
            def _():
                other.start()

        copies.append(copy)
    return copies


def over_slots(info, slots, cols, body):
    def slot(s, carry):
        code = info[2 + s]

        @pl.when(code >= 0)
        def _():
            body(s, lax.div(code, cols), lax.rem(code, cols))

        return carry

    lax.fori_loop(0, slots, slot, 0)


def to_hidden_kernel(cols, flip, wides, info, w_ref, *refs):
    x_refs, refs = refs[:wides], refs[wides:]
    *outs, x, acc, sems = refs
    copies = wide_copies(x_refs, x, sems, info[1])
    acc[...] = jnp.zeros_like(acc)
    for copy in copies:
        copy.wait()

    def add(s, wide, hidden):
        for chunk in chunks(x.shape[1]):
            product = matmul(flat(x[wide, chunk]), w_ref[s], 1, 1 if flip else 0)
            acc[hidden, chunk] += product.reshape(-1, *acc.shape[2:])

    over_slots(info, w_ref.shape[0], cols, add)
    for part, out in enumerate(outs):
        out[...] = acc[:, part].astype(out.dtype)


def from_hidden_kernel(cols, flip, at, blocks, info, w_ref, *refs):
    h_refs, refs = refs[:2 * blocks - 1], refs[2 * blocks - 1:]
    *outs, h, acc, sems = refs
    if len(outs[0].shape) == 5:
        outs = [outs[0].at[m] for m in range(outs[0].shape[0])]
    copies = hidden_copies(h_refs, h, sems, info[0], at, blocks)
    acc[...] = jnp.zeros_like(acc)
    for copy in copies:
        copy.wait()

    def add(s, wide, hidden):
        acc[wide] += matmul(flat(h[hidden]), w_ref[s], 1, 1 if flip else 0)

    over_slots(info, w_ref.shape[0], cols, add)
    tile = w_ref.shape[2]
    group, pieces, rows, unit = outs[0].shape
    for m, out in enumerate(outs):
        owner = lax.bitwise_xor(info[1], m)
        for q in range(pieces):
            if unit == tile:
                block = acc[owner * pieces + q]
            else:
                parts = tile // unit
                lane = pl.multiple_of(lax.rem(owner, parts) * unit, unit)
                block = acc[lax.div(owner, parts), :, pl.ds(lane, unit)]
            out[:, q] = block.astype(out.dtype).reshape(group, rows, unit)


def grad_kernel(cols, flip, wides, info, *refs):
    x_refs, h_refs, refs = refs[:wides], refs[wides:-5], refs[-5:]
    out, x, h, x_sems, h_sems = refs
    copies = wide_copies(x_refs, x, x_sems, info[1])
    copies += hidden_copies(h_refs, h, h_sems, info[0], 0, x.shape[1])
    out[...] = jnp.zeros_like(out)
    for copy in copies:
        copy.wait()

    def add(s, wide, hidden):
        total = 0.0
        for chunk in chunks(x.shape[1]):
            a, b = flat(x[wide, chunk]), flat(h[hidden, chunk])
            a, b = (a, b) if flip else (b, a)
            total += matmul(a, b, 0, 0)
        out[s] = total.astype(out.dtype)

    over_slots(info, out.shape[0], cols, add)


def call(kernel, out_shape, scratch, flops, moved, *args):
    return pl.pallas_call(
        kernel,
        out_shape=out_shape,
        in_specs=[pl.BlockSpec(memory_space=pltpu.SMEM)] + args[1],
        out_specs=jax.tree.map(lambda _: pl.BlockSpec(memory_space=pltpu.VMEM), out_shape),
        scratch_shapes=scratch,
        compiler_params=pltpu.CompilerParams(vmem_limit_bytes=VMEM),
        cost_estimate=pl.CostEstimate(flops=flops, bytes_accessed=moved, transcendentals=0),
    )(args[0], *args[2])


def to_hidden(info, xs, w, cols, flip):
    blocks, pieces, rows, unit = xs[0].shape[-4:]
    slots, tile, _ = w.shape
    outs = [jax.ShapeDtypeStruct((cols, rows, tile), jnp.bfloat16)] * blocks
    scratch = [
        pltpu.VMEM((D // tile, blocks, rows, tile), jnp.bfloat16),
        pltpu.VMEM((cols, blocks, rows, tile), jnp.float32),
        pltpu.SemaphoreType.DMA((D // unit,)),
    ]
    kernel = functools.partial(to_hidden_kernel, cols, flip, len(xs))
    specs = [pl.BlockSpec(memory_space=pltpu.VMEM)] + [ANY] * len(xs)
    flops = 2 * slots * blocks * rows * tile * tile
    return call(kernel, outs, scratch, flops, 8 << 20, info, specs, [w, *xs])


def from_hidden(info, hs, w, cols, flip, at, group, devices):
    _, rows, tile = hs[0].shape
    slots = w.shape[0]
    unit = min(tile, D // devices)
    pieces = D // devices // unit
    outs = [jax.ShapeDtypeStruct((group, pieces, rows, unit), jnp.bfloat16)] * devices
    if long_row():
        outs = [jax.ShapeDtypeStruct((devices, *outs[0].shape), jnp.bfloat16)]
    scratch = [
        pltpu.VMEM((cols, group, rows, tile), jnp.bfloat16),
        pltpu.VMEM((D // tile, group * rows, tile), jnp.float32),
        pltpu.SemaphoreType.DMA((group,)),
    ]
    blocks = (len(hs) + 1) // 2
    kernel = functools.partial(from_hidden_kernel, cols, flip, at, blocks)
    specs = [pl.BlockSpec(memory_space=pltpu.VMEM)] + [ANY] * len(hs)
    flops = 2 * slots * group * rows * tile * tile
    return call(kernel, outs, scratch, flops, 8 << 20, info, specs, [w, *hs])


def slot_grads(info, xs, hs, slots, cols, flip):
    blocks, pieces, rows, unit = xs[0].shape[-4:]
    tile = hs[0].shape[2]
    out = jax.ShapeDtypeStruct((slots, tile, tile), jnp.bfloat16)
    scratch = [
        pltpu.VMEM((D // tile, blocks, rows, tile), jnp.bfloat16),
        pltpu.VMEM((cols, blocks, rows, tile), jnp.bfloat16),
        pltpu.SemaphoreType.DMA((D // unit,)),
        pltpu.SemaphoreType.DMA((blocks,)),
    ]
    kernel = functools.partial(grad_kernel, cols, flip, len(xs))
    specs = [ANY] * (len(xs) + len(hs))
    flops = 2 * slots * blocks * rows * tile * tile
    return call(kernel, out, scratch, flops, 8 << 20, info, specs, [*xs, *hs])


def long_row():
    return lax.axis_size("row") > GROUP


def swap_col(x, m):
    count = lax.axis_size("col")
    return lax.ppermute(x, "col", [(s, s ^ m) for s in range(count)])


def shift_row(x, step):
    count = lax.axis_size("row")
    return lax.ppermute(x, "row", [(s, (s + step) % count) for s in range(count)])


def step_row(x, step, first, last):
    return lax.ppermute(x, "row", [(s, s + step) for s in range(first, last + 1)])


def spread(x, tile):
    rows, width = x.shape
    unit = min(width, tile)
    own = jnp.swapaxes(x.reshape(rows, width // unit, unit), 0, 1)
    if long_row():
        everything = lax.all_gather(lax.all_gather(own, "row"), "col")
        return [everything]
    mine = jnp.stack([own] + [shift_row(own, -j) for j in range(1, lax.axis_size("row"))])
    held = []
    for m in range(0, lax.axis_size("col"), 2):
        held.append(swap_col(mine, m) if m else mine)
        held.append(swap_col(held[m], 1))
    return held


def add(*terms):
    total = sum(term.astype(jnp.float32) for term in terms)
    return total


def line_reduce(parts):
    if long_row():
        return lax.psum_scatter(jnp.stack(parts), "row", scatter_dimension=0).astype(jnp.float32)
    count = len(parts)
    right = left = None
    for k in range(1, count):
        out_right, out_left = parts[count - k], parts[k]
        if k > 1:
            out_right = add(out_right, right).astype(jnp.bfloat16)
            out_left = add(out_left, left).astype(jnp.bfloat16)
        right = step_row(out_right, 1, 0, k - 1)
        left = step_row(out_left, -1, count - k, count - 1)
    return add(parts[0], right, left)


def line_gather(x):
    count = lax.axis_size("row")
    if long_row():
        everything = lax.all_gather(x, "row")
        return [everything[0]] * count + [everything[j] for j in range(1, count)]
    right, left = [x], [x]
    for k in range(1, count):
        right.append(step_row(right[-1], 1, k - 1, count - 2))
        left.append(step_row(left[-1], -1, 1, count - k))
    return right + left[1:]


def finish_col(parts):
    if long_row():
        return lax.psum_scatter(parts[0], "col", scatter_dimension=0)
    sums = []
    for m in range(0, len(parts), 2):
        pair = add(parts[m], swap_col(parts[m + 1], 1)).astype(jnp.bfloat16)
        sums.append(swap_col(pair, m) if m else pair)
    return add(*sums).astype(jnp.bfloat16)


def finish_row(blocks):
    if long_row():
        total = lax.psum_scatter(jnp.stack(blocks), "row", scatter_dimension=0)
        return jnp.swapaxes(total, 0, 1).reshape(total.shape[1], -1)
    total = add(blocks[0], *[shift_row(blocks[j], j) for j in range(1, len(blocks))])
    _, rows, _ = total.shape
    return jnp.swapaxes(total, 0, 1).reshape(rows, -1).astype(jnp.bfloat16)


def per_device(tokens, upstream, w_in, in_codes, w_out, out_codes):
    tile = w_in.shape[3]
    slots = w_in.shape[1]
    devices = lax.axis_size("col")
    blocks = lax.axis_size("row")
    cols = FF // (tile * devices)
    group = min(blocks, GROUP)
    starts = range(0, blocks, group)
    row, col = lax.axis_index("row"), lax.axis_index("col")

    def slot_info(codes):
        own = lax.dynamic_slice_in_dim(codes[0], row * slots, slots)
        place = jnp.stack([row, col]).astype(jnp.int32)
        if long_row():
            place = jnp.zeros_like(place)
        return jnp.concatenate([place, own])

    info_in, info_out = slot_info(in_codes), slot_info(out_codes)
    w_in, w_out = w_in[0], w_out[0]

    def hidden_side(info, xs, w, flip):
        return line_reduce(to_hidden(info, xs, w, cols, flip))

    def wide_side(info, hs, w, flip):
        sums = []
        for at in starts:
            if sums:
                hs, _ = lax.optimization_barrier((hs, sums[-1]))
            parts = from_hidden(info, hs, w, cols, flip, at, group, devices)
            sums.append(finish_col(parts))
        return finish_row([part[g] for part in sums for g in range(group)])

    all_tokens = spread(tokens, tile)
    hidden = hidden_side(info_in, all_tokens, w_in, False)
    if len(starts) > 1:
        upstream, hidden = lax.optimization_barrier((upstream, hidden))
    all_up = spread(upstream, tile)
    grad_activ = hidden_side(info_out, all_up, w_out, True)
    sigmoid = jax.nn.sigmoid(hidden)
    activ = (hidden * sigmoid).astype(jnp.bfloat16)
    grad_hidden = grad_activ * sigmoid * (1.0 + hidden * (1.0 - sigmoid))
    grad_hidden = grad_hidden.astype(jnp.bfloat16)
    all_activ, all_grad = line_gather(activ), line_gather(grad_hidden)
    layer_out = wide_side(info_out, all_activ, w_out, False)
    grad_w_out = slot_grads(info_out, all_up, all_activ, slots, cols, False)
    if len(starts) > 1:
        held = (all_grad, tokens, layer_out, grad_w_out)
        all_grad, tokens, layer_out, grad_w_out = lax.optimization_barrier(held)
        all_tokens = spread(tokens, tile)
    grad_tokens = wide_side(info_in, all_grad, w_in, True)
    grad_w_in = slot_grads(info_in, all_tokens, all_grad, slots, cols, True)
    return layer_out, grad_tokens, grad_w_in[None], grad_w_out[None]


def solution(mesh):
    placed = (
        P("row", "col"),
        P("row", "col"),
        P("col", "row", None, None),
        P("col", None),
        P("col", "row", None, None),
        P("col", None),
    )
    return jax.shard_map(
        per_device,
        mesh=mesh,
        in_specs=placed,
        out_specs=(
            P("row", "col"),
            P("row", "col"),
            P("col", "row", None, None),
            P("col", "row", None, None),
        ),
        check_vma=False,
    )
```

```python
import functools

import jax
import jax.numpy as jnp
from jax import lax
from jax.experimental import pallas as pl
from jax.experimental.pallas import tpu as pltpu
from jax.sharding import PartitionSpec as P

D = 4096
FF = 16384
VMEM = 56 * 1024 * 1024
GROUP = 4
REACH = {0: (0,), 1: (-1, 1), 2: (-2, 2), 3: (-3, -1, 1, 3)}
ANY = pl.BlockSpec(memory_space=pl.ANY)


def matmul(a, b, a_dim, b_dim):
    return lax.dot_general(
        a, b, (((a_dim,), (b_dim,)), ((), ())), preferred_element_type=jnp.float32
    )


def flat(block):
    return block.reshape(block.shape[0] * block.shape[1], block.shape[2])


def chunks(blocks):
    group = min(blocks, GROUP)
    return [slice(at, at + group) for at in range(0, blocks, group)]


def tile_part(held, owner, q, pieces, unit):
    tile = held.shape[-1]
    if unit == tile:
        return owner * pieces + q, slice(None)
    parts = tile // unit
    lane = pl.multiple_of(lax.rem(owner, parts) * unit, unit)
    return lax.div(owner, parts), pl.ds(lane, unit)


def wide_copies(refs, held, sems, col):
    copies = []

    def copy(source, owner, q, pieces, block):
        unit = source.shape[-1]
        at, lanes = tile_part(held, owner, q, pieces, unit)
        target = held.at[at, block, :, lanes]
        copies.append(pltpu.make_async_copy(source, target, sems.at[len(copies)]))
        copies[-1].start()

    if len(refs) == 1:
        devices, _, pieces, _, _ = refs[0].shape
        for owner in range(devices):
            for q in range(pieces):
                copy(refs[0].at[owner, :, q], owner, q, pieces, slice(None))
        return copies
    for at, ref in enumerate(refs):
        half, pieces, _, _ = ref.shape
        for m in range(half):
            owner = lax.bitwise_xor(col, 2 * m + at % 2)
            for q in range(pieces):
                copy(ref.at[m, q], owner, q, pieces, at // 2)
    return copies


def hidden_copies(refs, names, labels, held, sems, row):
    copies = []
    if names is None:
        for g, block in enumerate(labels):
            copies.append(pltpu.make_async_copy(refs[0].at[block], held.at[:, g], sems.at[g]))
            copies[-1].start()
        return copies
    for g, t in enumerate(labels):
        distance = lax.bitwise_xor(row, t) - row
        for name, ref in zip(names, refs):
            if name in REACH[t]:
                copy = pltpu.make_async_copy(ref, held.at[:, g], sems.at[g])
                pl.when(distance == name)(copy.start)
        copies.append(copy)
    return copies


def over_slots(info, slots, cols, body):
    def slot(s, carry):
        code = info[2 + s]

        @pl.when(code >= 0)
        def _():
            body(s, lax.div(code, cols), lax.rem(code, cols))

        return carry

    lax.fori_loop(0, slots, slot, 0)


def to_hidden_kernel(cols, flip, wides, info, w_ref, *refs):
    x_refs, refs = refs[:wides], refs[wides:]
    *outs, x, acc, sems = refs
    copies = wide_copies(x_refs, x, sems, info[1])
    acc[...] = jnp.zeros_like(acc)
    for copy in copies:
        copy.wait()

    def add(s, wide, hidden):
        for chunk in chunks(x.shape[1]):
            product = matmul(flat(x[wide, chunk]), w_ref[s], 1, 1 if flip else 0)
            acc[hidden, chunk] += product.reshape(-1, *acc.shape[2:])

    over_slots(info, w_ref.shape[0], cols, add)
    for part, out in enumerate(outs):
        out[...] = acc[:, part].astype(out.dtype)


def from_hidden_kernel(cols, flip, names, labels, info, w_ref, *refs):
    count = 1 if names is None else 2 * len(labels)
    h_refs, outs, (h, acc, sems) = refs[:-3 - count], refs[-3 - count:-3], refs[-3:]
    copies = hidden_copies(h_refs, names, labels, h, sems, info[0])
    acc[...] = jnp.zeros_like(acc)
    for copy in copies:
        copy.wait()

    def add(s, wide, hidden):
        for chunk in chunks(h.shape[1]):
            product = matmul(flat(h[hidden, chunk]), w_ref[s], 1, 1 if flip else 0)
            acc[wide, chunk] += product.reshape(-1, *acc.shape[2:])

    over_slots(info, w_ref.shape[0], cols, add)
    for at, out in enumerate(outs):
        pieces, unit = out.shape[-3], out.shape[-1]
        for m in range(out.shape[0]):
            for q in range(pieces):
                if names is None:
                    tile, lanes = tile_part(acc, m, q, pieces, unit)
                    out[m, :, q] = acc[tile, :, :, lanes].astype(out.dtype)
                else:
                    owner = lax.bitwise_xor(info[1], 2 * m + at % 2)
                    tile, lanes = tile_part(acc, owner, q, pieces, unit)
                    out[m, q] = acc[tile, at // 2, :, lanes].astype(out.dtype)


def grad_kernel(cols, flip, wides, names, labels, info, *refs):
    x_refs, h_refs, refs = refs[:wides], refs[wides:-5], refs[-5:]
    out, x, h, x_sems, h_sems = refs
    copies = wide_copies(x_refs, x, x_sems, info[1])
    copies += hidden_copies(h_refs, names, labels, h, h_sems, info[0])
    out[...] = jnp.zeros_like(out)
    for copy in copies:
        copy.wait()

    def add(s, wide, hidden):
        total = 0.0
        for chunk in chunks(x.shape[1]):
            a, b = flat(x[wide, chunk]), flat(h[hidden, chunk])
            a, b = (a, b) if flip else (b, a)
            total += matmul(a, b, 0, 0)
        out[s] = total.astype(out.dtype)

    over_slots(info, out.shape[0], cols, add)


def call(kernel, out_shape, scratch, flops, moved, *args):
    return pl.pallas_call(
        kernel,
        out_shape=out_shape,
        in_specs=[pl.BlockSpec(memory_space=pltpu.SMEM)] + args[1],
        out_specs=jax.tree.map(lambda _: pl.BlockSpec(memory_space=pltpu.VMEM), out_shape),
        scratch_shapes=scratch,
        compiler_params=pltpu.CompilerParams(vmem_limit_bytes=VMEM),
        cost_estimate=pl.CostEstimate(flops=flops, bytes_accessed=moved, transcendentals=0),
    )(args[0], *args[2])


def wide_scratch(blocks, rows, tile, unit):
    pieces = D // unit
    count = pieces if long_row() else pieces * blocks
    held = pltpu.VMEM((D // tile, blocks, rows, tile), jnp.bfloat16)
    return [held, pltpu.SemaphoreType.DMA((count,))]


def to_hidden(info, xs, w, cols, flip):
    rows, unit = xs[0].shape[-2:]
    slots, tile, _ = w.shape
    blocks = lax.axis_size("row")
    outs = [jax.ShapeDtypeStruct((cols, rows, tile), jnp.bfloat16)] * blocks
    held, sems = wide_scratch(blocks, rows, tile, unit)
    scratch = [held, pltpu.VMEM((cols, blocks, rows, tile), jnp.float32), sems]
    kernel = functools.partial(to_hidden_kernel, cols, flip, len(xs))
    specs = [pl.BlockSpec(memory_space=pltpu.VMEM)] + [ANY] * len(xs)
    flops = 2 * slots * blocks * rows * tile * tile
    return call(kernel, outs, scratch, flops, 8 << 20, info, specs, [w, *xs])


def sources(hs, labels):
    if not isinstance(hs, dict):
        return None, [hs]
    names = sorted({name for t in labels for name in REACH[t]})
    return names, [hs[name] for name in names]


def from_hidden(info, hs, w, cols, flip, labels, devices):
    names, hs = sources(hs, labels)
    rows, tile = hs[0].shape[-2:]
    slots, group = w.shape[0], len(labels)
    unit = min(tile, D // devices)
    pieces = D // devices // unit
    if names is None:
        outs = [jax.ShapeDtypeStruct((devices, group, pieces, rows, unit), jnp.bfloat16)]
    else:
        outs = [jax.ShapeDtypeStruct((devices // 2, pieces, rows, unit), jnp.bfloat16)] * (2 * group)
    scratch = [
        pltpu.VMEM((cols, group, rows, tile), jnp.bfloat16),
        pltpu.VMEM((D // tile, group, rows, tile), jnp.float32),
        pltpu.SemaphoreType.DMA((group,)),
    ]
    kernel = functools.partial(from_hidden_kernel, cols, flip, names, labels)
    specs = [pl.BlockSpec(memory_space=pltpu.VMEM)] + [ANY] * len(hs)
    flops = 2 * slots * group * rows * tile * tile
    return call(kernel, outs, scratch, flops, 8 << 20, info, specs, [w, *hs])


def slot_grads(info, xs, hs, slots, cols, flip):
    blocks = lax.axis_size("row")
    labels = range(blocks)
    names, hs = sources(hs, labels)
    rows, unit = xs[0].shape[-2:]
    tile = hs[0].shape[-1]
    out = jax.ShapeDtypeStruct((slots, tile, tile), jnp.bfloat16)
    held, sems = wide_scratch(blocks, rows, tile, unit)
    scratch = [
        held,
        pltpu.VMEM((cols, blocks, rows, tile), jnp.bfloat16),
        sems,
        pltpu.SemaphoreType.DMA((blocks,)),
    ]
    kernel = functools.partial(grad_kernel, cols, flip, len(xs), names, labels)
    specs = [ANY] * (len(xs) + len(hs))
    flops = 2 * slots * blocks * rows * tile * tile
    return call(kernel, out, scratch, flops, 8 << 20, info, specs, [*xs, *hs])


def long_row():
    return lax.axis_size("row") != 4


def swap_col(x, m):
    count = lax.axis_size("col")
    return lax.ppermute(x, "col", [(s, s ^ m) for s in range(count)])


def swap_row(x, t):
    return lax.ppermute(x, "row", [(s, s ^ t) for s in range(4)])


def step_row(x, step, first, last):
    return lax.ppermute(x, "row", [(s, s + step) for s in range(first, last + 1)])


def own_pieces(x, tile):
    rows, width = x.shape
    unit = min(width, tile)
    return jnp.swapaxes(x.reshape(rows, width // unit, unit), 0, 1)


def spread(blocks):
    held = []
    for own in blocks:
        even = [swap_col(own, m) if m else own for m in range(0, lax.axis_size("col"), 2)]
        held.append(jnp.stack(even))
        held.append(swap_col(held[-1], 1))
    return held


def add(*terms):
    return sum(term.astype(jnp.float32) for term in terms)


def line_reduce(parts, row):
    right = step_row(parts[3], 1, 0, 0)
    left = step_row(parts[3], -1, 3, 3)
    right = step_row(add(parts[2], right).astype(jnp.bfloat16), 1, 0, 1)
    left = step_row(add(parts[2], left).astype(jnp.bfloat16), -1, 2, 3)
    last_right = add(jnp.where(row == 1, parts[3], parts[1]), right).astype(jnp.bfloat16)
    last_left = add(jnp.where(row == 2, parts[3], parts[1]), left).astype(jnp.bfloat16)
    right = step_row(last_right, 1, 0, 2)
    left = step_row(last_left, -1, 1, 3)
    return add(parts[0], right, left), (last_right, last_left)


def line_gather(x):
    held = {0: x}
    for k in range(1, 4):
        held[-k] = step_row(held[1 - k], 1, k - 1, 2)
        held[k] = step_row(held[k - 1], -1, 1, 4 - k)
    return held


def finish_col(even, odd):
    pairs = add(even, swap_col(odd, 1)).astype(jnp.bfloat16)
    sums = [pairs[0]] + [swap_col(pairs[m], 2 * m) for m in range(1, even.shape[0])]
    return add(*sums).astype(jnp.bfloat16)


def rows_first(total):
    return jnp.swapaxes(total, 0, 1).reshape(total.shape[1], -1).astype(jnp.bfloat16)


def finish_row(sums):
    return rows_first(add(sums[0], *[swap_row(sums[t], t) for t in range(1, 4)]))


def activations(hidden, grad_activ):
    sigmoid = jax.nn.sigmoid(hidden)
    slope = sigmoid * (1.0 + hidden * (1.0 - sigmoid))
    return (grad_activ * slope).astype(jnp.bfloat16)


def silu(hidden):
    return (hidden * jax.nn.sigmoid(hidden)).astype(jnp.bfloat16)


def per_device(tokens, upstream, w_in, in_codes, w_out, out_codes):
    tile = w_in.shape[3]
    slots = w_in.shape[1]
    devices = lax.axis_size("col")
    cols = FF // (tile * devices)
    row, col = lax.axis_index("row"), lax.axis_index("col")

    def slot_info(codes):
        own = lax.dynamic_slice_in_dim(codes[0], row * slots, slots)
        place = jnp.stack([row, col]).astype(jnp.int32)
        return jnp.concatenate([place, own])

    info_in, info_out = slot_info(in_codes), slot_info(out_codes)
    w_in, w_out = w_in[0], w_out[0]
    tokens, upstream = own_pieces(tokens, tile), own_pieces(upstream, tile)
    args = (info_in, info_out, tokens, upstream, w_in, w_out, cols, devices)
    results = on_long_row(*args) if long_row() else on_line(*args)
    layer_out, grad_tokens, grad_w_in, grad_w_out = results
    return layer_out, grad_tokens, grad_w_in[None], grad_w_out[None]


def on_line(info_in, info_out, tokens, upstream, w_in, w_out, cols, devices):
    row, slots = info_in[0], w_in.shape[0]
    token_blocks = [tokens] + [swap_row(tokens, t) for t in range(1, 4)]
    up_blocks = [upstream] + [swap_row(upstream, t) for t in range(1, 4)]
    all_tokens = spread(token_blocks)
    up_blocks, all_tokens[-2] = lax.optimization_barrier((up_blocks, all_tokens[-2]))
    all_up = spread(up_blocks)
    parts = to_hidden(info_in, all_tokens, w_in, cols, False)
    hidden, last = line_reduce(parts, row)
    parts = to_hidden(info_out, all_up, w_out, cols, True)
    parts, _ = lax.optimization_barrier((parts, last))
    grad_activ, _ = line_reduce(parts, row)
    all_activ = line_gather(silu(hidden))
    all_grad = line_gather(activations(hidden, grad_activ))

    def wide_side(info, hs, w, flip, groups):
        sums = []
        for labels in groups:
            outs = from_hidden(info, hs, w, cols, flip, labels, devices)
            sums += [finish_col(*outs[2 * g:2 * g + 2]) for g in range(len(labels))]
        return finish_row(sums)

    layer_out = wide_side(info_out, all_activ, w_out, False, [(0, 1, 2, 3)])
    grad_w_out = slot_grads(info_out, all_up, all_activ, slots, cols, False)
    grad_tokens = wide_side(info_in, all_grad, w_in, True, [(0, 1), (2,), (3,)])
    grad_w_in = slot_grads(info_in, all_tokens, all_grad, slots, cols, True)
    return layer_out, grad_tokens, grad_w_in, grad_w_out


def on_long_row(info_in, info_out, tokens, upstream, w_in, w_out, cols, devices):
    slots, blocks = w_in.shape[0], lax.axis_size("row")

    def everywhere(x):
        return [lax.all_gather(lax.all_gather(x, "row"), "col")]

    def hidden_side(info, xs, w, flip):
        parts = jnp.stack(to_hidden(info, xs, w, cols, flip))
        return lax.psum_scatter(parts, "row", scatter_dimension=0).astype(jnp.float32)

    def wide_side(info, hs, w, flip):
        sums = []
        for chunk in chunks(blocks):
            if sums:
                hs, _ = lax.optimization_barrier((hs, sums[-1]))
            labels = range(blocks)[chunk]
            [parts] = from_hidden(info, hs, w, cols, flip, labels, devices)
            sums.append(lax.psum_scatter(parts, "col", scatter_dimension=0))
        total = lax.psum_scatter(jnp.concatenate(sums), "row", scatter_dimension=0)
        return rows_first(total)

    hidden = hidden_side(info_in, everywhere(tokens), w_in, False)
    upstream, hidden = lax.optimization_barrier((upstream, hidden))
    all_up = everywhere(upstream)
    grad_activ = hidden_side(info_out, all_up, w_out, True)
    all_activ = lax.all_gather(silu(hidden), "row")
    layer_out = wide_side(info_out, all_activ, w_out, False)
    grad_w_out = slot_grads(info_out, all_up, all_activ, slots, cols, False)
    held = (activations(hidden, grad_activ), tokens, layer_out, grad_w_out)
    grad_hidden, tokens, layer_out, grad_w_out = lax.optimization_barrier(held)
    all_grad = lax.all_gather(grad_hidden, "row")
    grad_tokens = wide_side(info_in, all_grad, w_in, True)
    grad_w_in = slot_grads(info_in, everywhere(tokens), all_grad, slots, cols, True)
    return layer_out, grad_tokens, grad_w_in, grad_w_out


def solution(mesh):
    placed = (
        P("row", "col"),
        P("row", "col"),
        P("col", "row", None, None),
        P("col", None),
        P("col", "row", None, None),
        P("col", None),
    )
    return jax.shard_map(
        per_device,
        mesh=mesh,
        in_specs=placed,
        out_specs=(
            P("row", "col"),
            P("row", "col"),
            P("col", "row", None, None),
            P("col", "row", None, None),
        ),
        check_vma=False,
    )
```

```python
import functools

import jax
import jax.numpy as jnp
from jax import lax
from jax.experimental import pallas as pl
from jax.experimental.pallas import tpu as pltpu
from jax.sharding import PartitionSpec as P

D = 4096
FF = 16384
VMEM = 56 * 1024 * 1024
GROUP = 4
REACH = {0: (0,), 1: (-1, 1), 2: (-2, 2), 3: (-3, -1, 1, 3)}
ANY = pl.BlockSpec(memory_space=pl.ANY)


def matmul(a, b, a_dim, b_dim):
    return lax.dot_general(
        a, b, (((a_dim,), (b_dim,)), ((), ())), preferred_element_type=jnp.float32
    )


def flat(block):
    return block.reshape(block.shape[0] * block.shape[1], block.shape[2])


def chunks(blocks):
    group = min(blocks, GROUP)
    return [slice(at, at + group) for at in range(0, blocks, group)]


def tile_part(held, owner, q, pieces, unit):
    tile = held.shape[-1]
    if unit == tile:
        return owner * pieces + q, slice(None)
    parts = tile // unit
    lane = pl.multiple_of(lax.rem(owner, parts) * unit, unit)
    return lax.div(owner, parts), pl.ds(lane, unit)


def wide_copies(refs, held, sems, col):
    copies = []
    if len(refs) == 1:
        pairs = [(m, refs[0].at[m]) for m in range(refs[0].shape[0])]
    else:
        pairs = [(lax.bitwise_xor(col, m), ref) for m, ref in enumerate(refs)]
    for owner, ref in pairs:
        _, pieces, _, unit = ref.shape
        for q in range(pieces):
            tile, lanes = tile_part(held, owner, q, pieces, unit)
            target = held.at[tile, :, :, lanes]
            copies.append(pltpu.make_async_copy(ref.at[:, q], target, sems.at[len(copies)]))
            copies[-1].start()
    return copies


def hidden_copies(refs, names, labels, held, sems, row):
    copies = []
    if names is None:
        for g, block in enumerate(labels):
            copies.append(pltpu.make_async_copy(refs[0].at[block], held.at[:, g], sems.at[g]))
            copies[-1].start()
        return copies
    for g, t in enumerate(labels):
        distance = lax.bitwise_xor(row, t) - row
        for name, ref in zip(names, refs):
            if name in REACH[t]:
                copy = pltpu.make_async_copy(ref, held.at[:, g], sems.at[g])
                pl.when(distance == name)(copy.start)
        copies.append(copy)
    return copies


def over_slots(info, slots, cols, body):
    def slot(s, carry):
        code = info[2 + s]

        @pl.when(code >= 0)
        def _():
            body(s, lax.div(code, cols), lax.rem(code, cols))

        return carry

    lax.fori_loop(0, slots, slot, 0)


def to_hidden_kernel(cols, flip, wides, info, w_ref, *refs):
    x_refs, refs = refs[:wides], refs[wides:]
    *outs, x, acc, sems = refs
    copies = wide_copies(x_refs, x, sems, info[1])
    acc[...] = jnp.zeros_like(acc)
    for copy in copies:
        copy.wait()

    def add(s, wide, hidden):
        for chunk in chunks(x.shape[1]):
            product = matmul(flat(x[wide, chunk]), w_ref[s], 1, 1 if flip else 0)
            acc[hidden, chunk] += product.reshape(-1, *acc.shape[2:])

    over_slots(info, w_ref.shape[0], cols, add)
    for part, out in enumerate(outs):
        out[...] = acc[:, part].astype(out.dtype)


def from_hidden_kernel(cols, flip, names, labels, info, w_ref, *refs):
    count = 1 if names is None else 2
    h_refs, outs, (h, acc, sems) = refs[:-3 - count], refs[-3 - count:-3], refs[-3:]
    copies = hidden_copies(h_refs, names, labels, h, sems, info[0])
    acc[...] = jnp.zeros_like(acc)
    for copy in copies:
        copy.wait()

    def add(s, wide, hidden):
        for chunk in chunks(h.shape[1]):
            product = matmul(flat(h[hidden, chunk]), w_ref[s], 1, 1 if flip else 0)
            acc[wide, chunk] += product.reshape(-1, *acc.shape[2:])

    over_slots(info, w_ref.shape[0], cols, add)
    for at, out in enumerate(outs):
        pieces, unit = out.shape[-3], out.shape[-1]
        for m in range(out.shape[0]):
            owner = m if names is None else lax.bitwise_xor(info[1], 2 * m + at)
            for q in range(pieces):
                tile, lanes = tile_part(acc, owner, q, pieces, unit)
                out[m, :, q] = acc[tile, :, :, lanes].astype(out.dtype)


def grad_kernel(cols, flip, wides, names, labels, info, *refs):
    x_refs, h_refs, refs = refs[:wides], refs[wides:-5], refs[-5:]
    out, x, h, x_sems, h_sems = refs
    copies = wide_copies(x_refs, x, x_sems, info[1])
    copies += hidden_copies(h_refs, names, labels, h, h_sems, info[0])
    out[...] = jnp.zeros_like(out)
    for copy in copies:
        copy.wait()

    def add(s, wide, hidden):
        total = 0.0
        for chunk in chunks(x.shape[1]):
            a, b = flat(x[wide, chunk]), flat(h[hidden, chunk])
            a, b = (a, b) if flip else (b, a)
            total += matmul(a, b, 0, 0)
        out[s] = total.astype(out.dtype)

    over_slots(info, out.shape[0], cols, add)


def call(kernel, out_shape, scratch, flops, moved, *args):
    return pl.pallas_call(
        kernel,
        out_shape=out_shape,
        in_specs=[pl.BlockSpec(memory_space=pltpu.SMEM)] + args[1],
        out_specs=jax.tree.map(lambda _: pl.BlockSpec(memory_space=pltpu.VMEM), out_shape),
        scratch_shapes=scratch,
        compiler_params=pltpu.CompilerParams(vmem_limit_bytes=VMEM),
        cost_estimate=pl.CostEstimate(flops=flops, bytes_accessed=moved, transcendentals=0),
    )(args[0], *args[2])


def wide_scratch(blocks, rows, tile, unit):
    held = pltpu.VMEM((D // tile, blocks, rows, tile), jnp.bfloat16)
    return [held, pltpu.SemaphoreType.DMA((D // unit,))]


def to_hidden(info, xs, w, cols, flip):
    rows, unit = xs[0].shape[-2:]
    slots, tile, _ = w.shape
    blocks = lax.axis_size("row")
    outs = [jax.ShapeDtypeStruct((cols, rows, tile), jnp.bfloat16)] * blocks
    held, sems = wide_scratch(blocks, rows, tile, unit)
    scratch = [held, pltpu.VMEM((cols, blocks, rows, tile), jnp.float32), sems]
    kernel = functools.partial(to_hidden_kernel, cols, flip, len(xs))
    specs = [pl.BlockSpec(memory_space=pltpu.VMEM)] + [ANY] * len(xs)
    flops = 2 * slots * blocks * rows * tile * tile
    return call(kernel, outs, scratch, flops, 8 << 20, info, specs, [w, *xs])


def sources(hs, labels):
    if not isinstance(hs, dict):
        return None, [hs]
    names = sorted({name for t in labels for name in REACH[t]})
    return names, [hs[name] for name in names]


def from_hidden(info, hs, w, cols, flip, labels, devices):
    names, hs = sources(hs, labels)
    rows, tile = hs[0].shape[-2:]
    slots, group = w.shape[0], len(labels)
    unit = min(tile, D // devices)
    pieces = D // devices // unit
    shape = (group, pieces, rows, unit)
    if names is None:
        outs = [jax.ShapeDtypeStruct((devices, *shape), jnp.bfloat16)]
    else:
        outs = [jax.ShapeDtypeStruct((devices // 2, *shape), jnp.bfloat16)] * 2
    scratch = [
        pltpu.VMEM((cols, group, rows, tile), jnp.bfloat16),
        pltpu.VMEM((D // tile, group, rows, tile), jnp.float32),
        pltpu.SemaphoreType.DMA((group,)),
    ]
    kernel = functools.partial(from_hidden_kernel, cols, flip, names, labels)
    specs = [pl.BlockSpec(memory_space=pltpu.VMEM)] + [ANY] * len(hs)
    flops = 2 * slots * group * rows * tile * tile
    return call(kernel, outs, scratch, flops, 8 << 20, info, specs, [w, *hs])


def slot_grads(info, xs, hs, slots, cols, flip):
    blocks = lax.axis_size("row")
    labels = range(blocks)
    names, hs = sources(hs, labels)
    rows, unit = xs[0].shape[-2:]
    tile = hs[0].shape[-1]
    out = jax.ShapeDtypeStruct((slots, tile, tile), jnp.bfloat16)
    held, sems = wide_scratch(blocks, rows, tile, unit)
    scratch = [
        held,
        pltpu.VMEM((cols, blocks, rows, tile), jnp.bfloat16),
        sems,
        pltpu.SemaphoreType.DMA((blocks,)),
    ]
    kernel = functools.partial(grad_kernel, cols, flip, len(xs), names, labels)
    specs = [ANY] * (len(xs) + len(hs))
    flops = 2 * slots * blocks * rows * tile * tile
    return call(kernel, out, scratch, flops, 8 << 20, info, specs, [*xs, *hs])


def long_row():
    return lax.axis_size("row") != 4


def swap_col(x, m):
    count = lax.axis_size("col")
    return lax.ppermute(x, "col", [(s, s ^ m) for s in range(count)])


def swap_row(x, t):
    return lax.ppermute(x, "row", [(s, s ^ t) for s in range(4)])


def step_row(x, step, first, last):
    return lax.ppermute(x, "row", [(s, s + step) for s in range(first, last + 1)])


def own_pieces(x, tile):
    rows, width = x.shape
    unit = min(width, tile)
    return jnp.swapaxes(x.reshape(rows, width // unit, unit), 0, 1)


def spread(mine, after):
    mine = jnp.stack(mine)
    if after is not None:
        mine, _ = lax.optimization_barrier((mine, after))
    held = []
    for m in range(0, lax.axis_size("col"), 2):
        held.append(swap_col(mine, m) if m else mine)
        held.append(swap_col(held[m], 1))
    return held


def add(*terms):
    return sum(term.astype(jnp.float32) for term in terms)


def line_reduce(parts, row):
    right = step_row(parts[3], 1, 0, 0)
    left = step_row(parts[3], -1, 3, 3)
    right = step_row(add(parts[2], right).astype(jnp.bfloat16), 1, 0, 1)
    left = step_row(add(parts[2], left).astype(jnp.bfloat16), -1, 2, 3)
    last_right = add(jnp.where(row == 1, parts[3], parts[1]), right).astype(jnp.bfloat16)
    last_left = add(jnp.where(row == 2, parts[3], parts[1]), left).astype(jnp.bfloat16)
    right = step_row(last_right, 1, 0, 2)
    left = step_row(last_left, -1, 1, 3)
    return add(parts[0], right, left)


def line_gather(x):
    held = {0: x}
    for k in range(1, 4):
        held[-k] = step_row(held[1 - k], 1, k - 1, 2)
        held[k] = step_row(held[k - 1], -1, 1, 4 - k)
    return held


def finish_col(even, odd):
    pairs = add(even, swap_col(odd, 1)).astype(jnp.bfloat16)
    sums = [pairs[0]] + [swap_col(pairs[m], 2 * m) for m in range(1, even.shape[0])]
    return add(*sums).astype(jnp.bfloat16)


def rows_first(total):
    return jnp.swapaxes(total, 0, 1).reshape(total.shape[1], -1).astype(jnp.bfloat16)


def finish_row(sums):
    return rows_first(add(sums[0], *[swap_row(sums[t], t) for t in range(1, 4)]))


def activations(hidden, grad_activ):
    sigmoid = jax.nn.sigmoid(hidden)
    slope = sigmoid * (1.0 + hidden * (1.0 - sigmoid))
    return (grad_activ * slope).astype(jnp.bfloat16)


def silu(hidden):
    return (hidden * jax.nn.sigmoid(hidden)).astype(jnp.bfloat16)


def per_device(tokens, upstream, w_in, in_codes, w_out, out_codes):
    tile = w_in.shape[3]
    slots = w_in.shape[1]
    devices = lax.axis_size("col")
    cols = FF // (tile * devices)
    row, col = lax.axis_index("row"), lax.axis_index("col")

    def slot_info(codes):
        own = lax.dynamic_slice_in_dim(codes[0], row * slots, slots)
        place = jnp.stack([row, col]).astype(jnp.int32)
        return jnp.concatenate([place, own])

    info_in, info_out = slot_info(in_codes), slot_info(out_codes)
    w_in, w_out = w_in[0], w_out[0]
    tokens, upstream = own_pieces(tokens, tile), own_pieces(upstream, tile)
    args = (info_in, info_out, tokens, upstream, w_in, w_out, cols, devices)
    results = on_long_row(*args) if long_row() else on_line(*args)
    layer_out, grad_tokens, grad_w_in, grad_w_out = results
    return layer_out, grad_tokens, grad_w_in[None], grad_w_out[None]


def on_line(info_in, info_out, tokens, upstream, w_in, w_out, cols, devices):
    row, slots = info_in[0], w_in.shape[0]
    token_blocks = [tokens] + [swap_row(tokens, t) for t in range(1, 4)]
    up_blocks = [upstream] + [swap_row(upstream, t) for t in range(1, 4)]
    all_tokens = spread(token_blocks, None)
    all_up = spread(up_blocks, tuple(all_tokens[2::2]))
    parts = to_hidden(info_in, all_tokens, w_in, cols, False)
    hidden = line_reduce(parts, row)
    parts = to_hidden(info_out, all_up, w_out, cols, True)
    grad_activ = line_reduce(parts, row)
    all_activ = line_gather(silu(hidden))
    all_grad = line_gather(activations(hidden, grad_activ))

    def wide_side(info, hs, w, flip, groups):
        sums = []
        for labels in groups:
            total = finish_col(*from_hidden(info, hs, w, cols, flip, labels, devices))
            sums += [total[g] for g in range(len(labels))]
        return finish_row(sums)

    layer_out = wide_side(info_out, all_activ, w_out, False, [(0, 1, 2, 3)])
    grad_w_out = slot_grads(info_out, all_up, all_activ, slots, cols, False)
    grad_tokens = wide_side(info_in, all_grad, w_in, True, [(0, 1, 2, 3)])
    grad_w_in = slot_grads(info_in, all_tokens, all_grad, slots, cols, True)
    return layer_out, grad_tokens, grad_w_in, grad_w_out


def on_long_row(info_in, info_out, tokens, upstream, w_in, w_out, cols, devices):
    slots, blocks = w_in.shape[0], lax.axis_size("row")

    def everywhere(x):
        return [lax.all_gather(lax.all_gather(x, "row"), "col")]

    def hidden_side(info, xs, w, flip):
        parts = jnp.stack(to_hidden(info, xs, w, cols, flip))
        return lax.psum_scatter(parts, "row", scatter_dimension=0).astype(jnp.float32)

    def wide_side(info, hs, w, flip):
        sums = []
        for chunk in chunks(blocks):
            if sums:
                hs, _ = lax.optimization_barrier((hs, sums[-1]))
            labels = range(blocks)[chunk]
            [parts] = from_hidden(info, hs, w, cols, flip, labels, devices)
            sums.append(lax.psum_scatter(parts, "col", scatter_dimension=0))
        total = lax.psum_scatter(jnp.concatenate(sums), "row", scatter_dimension=0)
        return rows_first(total)

    hidden = hidden_side(info_in, everywhere(tokens), w_in, False)
    upstream, hidden = lax.optimization_barrier((upstream, hidden))
    all_up = everywhere(upstream)
    grad_activ = hidden_side(info_out, all_up, w_out, True)
    all_activ = lax.all_gather(silu(hidden), "row")
    layer_out = wide_side(info_out, all_activ, w_out, False)
    grad_w_out = slot_grads(info_out, all_up, all_activ, slots, cols, False)
    held = (activations(hidden, grad_activ), tokens, layer_out, grad_w_out)
    grad_hidden, tokens, layer_out, grad_w_out = lax.optimization_barrier(held)
    all_grad = lax.all_gather(grad_hidden, "row")
    grad_tokens = wide_side(info_in, all_grad, w_in, True)
    grad_w_in = slot_grads(info_in, everywhere(tokens), all_grad, slots, cols, True)
    return layer_out, grad_tokens, grad_w_in, grad_w_out


def solution(mesh):
    placed = (
        P("row", "col"),
        P("row", "col"),
        P("col", "row", None, None),
        P("col", None),
        P("col", "row", None, None),
        P("col", None),
    )
    return jax.shard_map(
        per_device,
        mesh=mesh,
        in_specs=placed,
        out_specs=(
            P("row", "col"),
            P("row", "col"),
            P("col", "row", None, None),
            P("col", "row", None, None),
        ),
        check_vma=False,
    )
```

```python
import functools

import jax
import jax.numpy as jnp
from jax import lax
from jax.experimental import pallas as pl
from jax.experimental.pallas import tpu as pltpu
from jax.sharding import PartitionSpec as P

D = 4096
FF = 16384
VMEM = 56 * 1024 * 1024
GROUP = 4
REACH = {0: (0,), 1: (-1, 1), 2: (-2, 2), 3: (-3, -1, 1, 3)}
ANY = pl.BlockSpec(memory_space=pl.ANY)


def matmul(a, b, a_dim, b_dim):
    return lax.dot_general(
        a, b, (((a_dim,), (b_dim,)), ((), ())), preferred_element_type=jnp.float32
    )


def flat(block):
    return block.reshape(block.shape[0] * block.shape[1], block.shape[2])


def chunks(blocks):
    group = min(blocks, GROUP)
    return [slice(at, at + group) for at in range(0, blocks, group)]


def tile_part(held, owner, q, pieces, unit):
    tile = held.shape[-1]
    if unit == tile:
        return owner * pieces + q, slice(None)
    parts = tile // unit
    lane = pl.multiple_of(lax.rem(owner, parts) * unit, unit)
    return lax.div(owner, parts), pl.ds(lane, unit)


def wide_copies(refs, held, sems, col):
    copies = []
    if len(refs) == 1:
        pairs = [(m, refs[0].at[m]) for m in range(refs[0].shape[0])]
    else:
        pairs = [(lax.bitwise_xor(col, m), ref) for m, ref in enumerate(refs)]
    for owner, ref in pairs:
        _, pieces, _, unit = ref.shape
        for q in range(pieces):
            tile, lanes = tile_part(held, owner, q, pieces, unit)
            target = held.at[tile, :, :, lanes]
            copies.append(pltpu.make_async_copy(ref.at[:, q], target, sems.at[len(copies)]))
            copies[-1].start()
    return copies


def hidden_copies(refs, names, labels, held, sems, row):
    copies = []
    if names is None:
        for g, block in enumerate(labels):
            copies.append(pltpu.make_async_copy(refs[0].at[block], held.at[:, g], sems.at[g]))
            copies[-1].start()
        return copies
    for g, t in enumerate(labels):
        distance = lax.bitwise_xor(row, t) - row
        for name, ref in zip(names, refs):
            if name in REACH[t]:
                copy = pltpu.make_async_copy(ref, held.at[:, g], sems.at[g])
                pl.when(distance == name)(copy.start)
        copies.append(copy)
    return copies


def over_slots(info, slots, cols, body):
    def slot(s, carry):
        code = info[2 + s]

        @pl.when(code >= 0)
        def _():
            body(s, lax.div(code, cols), lax.rem(code, cols))

        return carry

    lax.fori_loop(0, slots, slot, 0)


def to_hidden_kernel(cols, flip, wides, info, w_ref, *refs):
    x_refs, refs = refs[:wides], refs[wides:]
    *outs, x, acc, sems = refs
    copies = wide_copies(x_refs, x, sems, info[1])
    acc[...] = jnp.zeros_like(acc)
    for copy in copies:
        copy.wait()

    def add(s, wide, hidden):
        for chunk in chunks(x.shape[1]):
            product = matmul(flat(x[wide, chunk]), w_ref[s], 1, 1 if flip else 0)
            acc[hidden, chunk] += product.reshape(-1, *acc.shape[2:])

    over_slots(info, w_ref.shape[0], cols, add)
    for part, out in enumerate(outs):
        out[...] = acc[:, part].astype(out.dtype)


def from_hidden_kernel(cols, flip, names, labels, info, w_ref, *refs):
    count = 1 if names is None else 2
    h_refs, outs, (h, acc, sems) = refs[:-3 - count], refs[-3 - count:-3], refs[-3:]
    copies = hidden_copies(h_refs, names, labels, h, sems, info[0])
    acc[...] = jnp.zeros_like(acc)
    for copy in copies:
        copy.wait()

    def add(s, wide, hidden):
        for chunk in chunks(h.shape[1]):
            product = matmul(flat(h[hidden, chunk]), w_ref[s], 1, 1 if flip else 0)
            acc[wide, chunk] += product.reshape(-1, *acc.shape[2:])

    over_slots(info, w_ref.shape[0], cols, add)
    for at, out in enumerate(outs):
        pieces, unit = out.shape[-3], out.shape[-1]
        for m in range(out.shape[0]):
            owner = m if names is None else lax.bitwise_xor(info[1], 2 * m + at)
            for q in range(pieces):
                tile, lanes = tile_part(acc, owner, q, pieces, unit)
                out[m, :, q] = acc[tile, :, :, lanes].astype(out.dtype)


def grad_kernel(cols, flip, wides, names, labels, info, *refs):
    x_refs, h_refs, refs = refs[:wides], refs[wides:-5], refs[-5:]
    out, x, h, x_sems, h_sems = refs
    copies = wide_copies(x_refs, x, x_sems, info[1])
    copies += hidden_copies(h_refs, names, labels, h, h_sems, info[0])
    out[...] = jnp.zeros_like(out)
    for copy in copies:
        copy.wait()

    def add(s, wide, hidden):
        total = 0.0
        for chunk in chunks(x.shape[1]):
            a, b = flat(x[wide, chunk]), flat(h[hidden, chunk])
            a, b = (a, b) if flip else (b, a)
            total += matmul(a, b, 0, 0)
        out[s] = total.astype(out.dtype)

    over_slots(info, out.shape[0], cols, add)


def call(kernel, out_shape, scratch, flops, moved, *args):
    return pl.pallas_call(
        kernel,
        out_shape=out_shape,
        in_specs=[pl.BlockSpec(memory_space=pltpu.SMEM)] + args[1],
        out_specs=jax.tree.map(lambda _: pl.BlockSpec(memory_space=pltpu.VMEM), out_shape),
        scratch_shapes=scratch,
        compiler_params=pltpu.CompilerParams(vmem_limit_bytes=VMEM),
        cost_estimate=pl.CostEstimate(flops=flops, bytes_accessed=moved, transcendentals=0),
    )(args[0], *args[2])


def wide_scratch(blocks, rows, tile, unit):
    held = pltpu.VMEM((D // tile, blocks, rows, tile), jnp.bfloat16)
    return [held, pltpu.SemaphoreType.DMA((D // unit,))]


def to_hidden(info, xs, w, cols, flip):
    rows, unit = xs[0].shape[-2:]
    slots, tile, _ = w.shape
    blocks = lax.axis_size("row")
    outs = [jax.ShapeDtypeStruct((cols, rows, tile), jnp.bfloat16)] * blocks
    held, sems = wide_scratch(blocks, rows, tile, unit)
    scratch = [held, pltpu.VMEM((cols, blocks, rows, tile), jnp.float32), sems]
    kernel = functools.partial(to_hidden_kernel, cols, flip, len(xs))
    specs = [pl.BlockSpec(memory_space=pltpu.VMEM)] + [ANY] * len(xs)
    flops = 2 * slots * blocks * rows * tile * tile
    return call(kernel, outs, scratch, flops, 8 << 20, info, specs, [w, *xs])


def sources(hs, labels):
    if not isinstance(hs, dict):
        return None, [hs]
    names = sorted({name for t in labels for name in REACH[t]})
    return names, [hs[name] for name in names]


def from_hidden(info, hs, w, cols, flip, labels, devices):
    names, hs = sources(hs, labels)
    rows, tile = hs[0].shape[-2:]
    slots, group = w.shape[0], len(labels)
    unit = min(tile, D // devices)
    pieces = D // devices // unit
    shape = (group, pieces, rows, unit)
    if names is None:
        outs = [jax.ShapeDtypeStruct((devices, *shape), jnp.bfloat16)]
    else:
        outs = [jax.ShapeDtypeStruct((devices // 2, *shape), jnp.bfloat16)] * 2
    scratch = [
        pltpu.VMEM((cols, group, rows, tile), jnp.bfloat16),
        pltpu.VMEM((D // tile, group, rows, tile), jnp.float32),
        pltpu.SemaphoreType.DMA((group,)),
    ]
    kernel = functools.partial(from_hidden_kernel, cols, flip, names, labels)
    specs = [pl.BlockSpec(memory_space=pltpu.VMEM)] + [ANY] * len(hs)
    flops = 2 * slots * group * rows * tile * tile
    return call(kernel, outs, scratch, flops, 8 << 20, info, specs, [w, *hs])


def slot_grads(info, xs, hs, slots, cols, flip):
    blocks = lax.axis_size("row")
    labels = range(blocks)
    names, hs = sources(hs, labels)
    rows, unit = xs[0].shape[-2:]
    tile = hs[0].shape[-1]
    out = jax.ShapeDtypeStruct((slots, tile, tile), jnp.bfloat16)
    held, sems = wide_scratch(blocks, rows, tile, unit)
    scratch = [
        held,
        pltpu.VMEM((cols, blocks, rows, tile), jnp.bfloat16),
        sems,
        pltpu.SemaphoreType.DMA((blocks,)),
    ]
    kernel = functools.partial(grad_kernel, cols, flip, len(xs), names, labels)
    specs = [ANY] * (len(xs) + len(hs))
    flops = 2 * slots * blocks * rows * tile * tile
    return call(kernel, out, scratch, flops, 8 << 20, info, specs, [*xs, *hs])


def long_row():
    return lax.axis_size("row") != 4


def swap_col(x, m):
    count = lax.axis_size("col")
    return lax.ppermute(x, "col", [(s, s ^ m) for s in range(count)])


def swap_row(x, t):
    return lax.ppermute(x, "row", [(s, s ^ t) for s in range(4)])


def step_row(x, step, first, last):
    return lax.ppermute(x, "row", [(s, s + step) for s in range(first, last + 1)])


def own_pieces(x, tile):
    rows, width = x.shape
    unit = min(width, tile)
    return jnp.swapaxes(x.reshape(rows, width // unit, unit), 0, 1)


def after(values, *others):
    return lax.optimization_barrier((values, others))[0]


def across(mine):
    return [swap_col(mine, m) if m else mine for m in range(0, lax.axis_size("col"), 2)]


def with_odd(even):
    return [x for own in even for x in (own, swap_col(own, 1))]


def add(*terms):
    return sum(term.astype(jnp.float32) for term in terms)


def line_reduce(parts, row, second=(), third=()):
    right = step_row(parts[3], 1, 0, 0)
    left = step_row(parts[3], -1, 3, 3)
    right, left = first = after((right, left), second)
    right = step_row(add(parts[2], right).astype(jnp.bfloat16), 1, 0, 1)
    left = step_row(add(parts[2], left).astype(jnp.bfloat16), -1, 2, 3)
    right, left = again = after((right, left), third)
    last_right = add(jnp.where(row == 1, parts[3], parts[1]), right).astype(jnp.bfloat16)
    last_left = add(jnp.where(row == 2, parts[3], parts[1]), left).astype(jnp.bfloat16)
    right = step_row(last_right, 1, 0, 2)
    left = step_row(last_left, -1, 1, 3)
    return (parts[0], right, left), (first, again), (last_right, last_left)


def line_gather(x, waits=()):
    held = {0: x}
    for k in range(1, 4):
        held[-k] = step_row(held[1 - k], 1, k - 1, 2)
        held[k] = step_row(held[k - 1], -1, 1, 4 - k)
        if k <= len(waits):
            held[-k], held[k] = after((held[-k], held[k]), waits[k - 1])
    return held


def finish_col(even, odd):
    pairs = add(even, swap_col(odd, 1)).astype(jnp.bfloat16)
    sums = [pairs[0]] + [swap_col(pairs[m], 2 * m) for m in range(1, even.shape[0])]
    return add(*sums).astype(jnp.bfloat16)


def rows_first(total):
    return jnp.swapaxes(total, 0, 1).reshape(total.shape[1], -1).astype(jnp.bfloat16)


def finish_row(sums):
    return rows_first(add(sums[0], *[swap_row(sums[t], t) for t in range(1, 4)]))


def activations(hidden, grad_activ):
    sigmoid = jax.nn.sigmoid(hidden)
    slope = sigmoid * (1.0 + hidden * (1.0 - sigmoid))
    return (grad_activ * slope).astype(jnp.bfloat16)


def silu(hidden):
    return (hidden * jax.nn.sigmoid(hidden)).astype(jnp.bfloat16)


def per_device(tokens, upstream, w_in, in_codes, w_out, out_codes):
    tile = w_in.shape[3]
    slots = w_in.shape[1]
    devices = lax.axis_size("col")
    cols = FF // (tile * devices)
    row, col = lax.axis_index("row"), lax.axis_index("col")

    def slot_info(codes):
        own = lax.dynamic_slice_in_dim(codes[0], row * slots, slots)
        place = jnp.stack([row, col]).astype(jnp.int32)
        return jnp.concatenate([place, own])

    info_in, info_out = slot_info(in_codes), slot_info(out_codes)
    w_in, w_out = w_in[0], w_out[0]
    tokens, upstream = own_pieces(tokens, tile), own_pieces(upstream, tile)
    args = (info_in, info_out, tokens, upstream, w_in, w_out, cols, devices)
    results = on_long_row(*args) if long_row() else on_line(*args)
    layer_out, grad_tokens, grad_w_in, grad_w_out = results
    return layer_out, grad_tokens, grad_w_in[None], grad_w_out[None]


def on_line(info_in, info_out, tokens, upstream, w_in, w_out, cols, devices):
    row, slots = info_in[0], w_in.shape[0]
    token_blocks = [tokens] + [swap_row(tokens, t) for t in range(1, 4)]
    up_blocks = [upstream] + [swap_row(upstream, t) for t in range(1, 4)]
    token_even = across(jnp.stack(token_blocks))
    up_mine = jnp.stack(up_blocks)
    all_tokens = with_odd(after(token_even, up_mine))
    up_even = across(after(up_mine, token_even[1:]))
    parts = to_hidden(info_in, all_tokens, w_in, cols, False)
    all_up = with_odd(after(up_even, parts))
    terms, _, last = line_reduce(parts, row, up_even, all_up)
    parts = to_hidden(info_out, after(all_up, last), w_out, cols, True)
    hidden = add(*after(terms, parts))
    activ = silu(hidden)
    terms, steps, _ = line_reduce(after(parts, activ), row)
    all_activ = line_gather(activ, steps)
    all_grad = line_gather(activations(hidden, add(*terms)))
    labels = range(4)

    def column_sums(info, hs, w, flip):
        return finish_col(*from_hidden(info, hs, w, cols, flip, labels, devices))

    layer_sums = column_sums(info_out, all_activ, w_out, False)
    grad_w_out = slot_grads(info_out, all_up, all_activ, slots, cols, False)
    all_grad, layer_sums, grad_w_out = lax.optimization_barrier((all_grad, layer_sums, grad_w_out))
    input_sums = column_sums(info_in, all_grad, w_in, True)
    grad_w_in = slot_grads(info_in, all_tokens, all_grad, slots, cols, True)
    layer_out, grad_tokens = finish_row(layer_sums), finish_row(input_sums)
    return layer_out, grad_tokens, grad_w_in, grad_w_out


def on_long_row(info_in, info_out, tokens, upstream, w_in, w_out, cols, devices):
    slots, blocks = w_in.shape[0], lax.axis_size("row")

    def everywhere(x):
        return [lax.all_gather(lax.all_gather(x, "row"), "col")]

    def hidden_side(info, xs, w, flip):
        parts = jnp.stack(to_hidden(info, xs, w, cols, flip))
        return lax.psum_scatter(parts, "row", scatter_dimension=0).astype(jnp.float32)

    def wide_side(info, hs, w, flip):
        sums = []
        for chunk in chunks(blocks):
            if sums:
                hs, _ = lax.optimization_barrier((hs, sums[-1]))
            labels = range(blocks)[chunk]
            [parts] = from_hidden(info, hs, w, cols, flip, labels, devices)
            sums.append(lax.psum_scatter(parts, "col", scatter_dimension=0))
        total = lax.psum_scatter(jnp.concatenate(sums), "row", scatter_dimension=0)
        return rows_first(total)

    hidden = hidden_side(info_in, everywhere(tokens), w_in, False)
    upstream, hidden = lax.optimization_barrier((upstream, hidden))
    all_up = everywhere(upstream)
    grad_activ = hidden_side(info_out, all_up, w_out, True)
    all_activ = lax.all_gather(silu(hidden), "row")
    layer_out = wide_side(info_out, all_activ, w_out, False)
    grad_w_out = slot_grads(info_out, all_up, all_activ, slots, cols, False)
    held = (activations(hidden, grad_activ), tokens, layer_out, grad_w_out)
    grad_hidden, tokens, layer_out, grad_w_out = lax.optimization_barrier(held)
    all_grad = lax.all_gather(grad_hidden, "row")
    grad_tokens = wide_side(info_in, all_grad, w_in, True)
    grad_w_in = slot_grads(info_in, everywhere(tokens), all_grad, slots, cols, True)
    return layer_out, grad_tokens, grad_w_in, grad_w_out


def solution(mesh):
    placed = (
        P("row", "col"),
        P("row", "col"),
        P("col", "row", None, None),
        P("col", None),
        P("col", "row", None, None),
        P("col", None),
    )
    return jax.shard_map(
        per_device,
        mesh=mesh,
        in_specs=placed,
        out_specs=(
            P("row", "col"),
            P("row", "col"),
            P("col", "row", None, None),
            P("col", "row", None, None),
        ),
        check_vma=False,
    )
```

```python
import functools

import jax
import jax.numpy as jnp
from jax import lax
from jax.experimental import pallas as pl
from jax.experimental.pallas import tpu as pltpu
from jax.sharding import PartitionSpec as P

D = 4096
FF = 16384
VMEM = 56 * 1024 * 1024
GROUP = 4
ANY = pl.BlockSpec(memory_space=pl.ANY)


def matmul(a, b, a_dim, b_dim):
    return lax.dot_general(
        a, b, (((a_dim,), (b_dim,)), ((), ())), preferred_element_type=jnp.float32
    )


def flat(block):
    return block.reshape(block.shape[0] * block.shape[1], block.shape[2])


def chunks(blocks):
    group = min(blocks, GROUP)
    return [slice(at, at + group) for at in range(0, blocks, group)]


def tile_part(held, owner, q, pieces, unit):
    tile = held.shape[-1]
    if unit == tile:
        return owner * pieces + q, slice(None)
    parts = tile // unit
    lane = pl.multiple_of(lax.rem(owner, parts) * unit, unit)
    return lax.div(owner, parts), pl.ds(lane, unit)


def wide_copies(refs, held, sems, col):
    copies = []
    if len(refs) == 1:
        pairs = [(m, refs[0].at[m]) for m in range(refs[0].shape[0])]
    else:
        pairs = [(lax.bitwise_xor(col, m), ref) for m, ref in enumerate(refs)]
    for owner, ref in pairs:
        _, pieces, _, unit = ref.shape
        for q in range(pieces):
            tile, lanes = tile_part(held, owner, q, pieces, unit)
            target = held.at[tile, :, :, lanes]
            copies.append(pltpu.make_async_copy(ref.at[:, q], target, sems.at[len(copies)]))
            copies[-1].start()
    return copies


def hidden_copies(ref, labels, held, sems, row):
    copies = []
    for g, t in enumerate(labels):
        source = ref.at[lax.bitwise_xor(row, t)]
        copies.append(pltpu.make_async_copy(source, held.at[:, g], sems.at[g]))
        copies[-1].start()
    return copies


def over_slots(info, slots, cols, body):
    def slot(s, carry):
        code = info[2 + s]

        @pl.when(code >= 0)
        def _():
            body(s, lax.div(code, cols), lax.rem(code, cols))

        return carry

    lax.fori_loop(0, slots, slot, 0)


def to_hidden_kernel(cols, flip, wides, info, w_ref, *refs):
    x_refs, refs = refs[:wides], refs[wides:]
    *outs, x, acc, sems = refs
    copies = wide_copies(x_refs, x, sems, info[1])
    acc[...] = jnp.zeros_like(acc)
    for copy in copies:
        copy.wait()

    def add(s, wide, hidden):
        for chunk in chunks(x.shape[1]):
            product = matmul(flat(x[wide, chunk]), w_ref[s], 1, 1 if flip else 0)
            acc[hidden, chunk] += product.reshape(-1, *acc.shape[2:])

    over_slots(info, w_ref.shape[0], cols, add)
    for part, out in enumerate(outs):
        out[...] = acc[:, part].astype(out.dtype)


def from_hidden_kernel(cols, flip, labels, info, w_ref, *refs):
    h_ref, *outs, h, acc, sems = refs
    copies = hidden_copies(h_ref, labels, h, sems, info[0])
    acc[...] = jnp.zeros_like(acc)
    for copy in copies:
        copy.wait()

    def add(s, wide, hidden):
        for chunk in chunks(h.shape[1]):
            product = matmul(flat(h[hidden, chunk]), w_ref[s], 1, 1 if flip else 0)
            acc[wide, chunk] += product.reshape(-1, *acc.shape[2:])

    over_slots(info, w_ref.shape[0], cols, add)
    for at, out in enumerate(outs):
        pieces, unit = out.shape[-3], out.shape[-1]
        for m in range(out.shape[0]):
            owner = m if len(outs) == 1 else lax.bitwise_xor(info[1], 2 * m + at)
            for q in range(pieces):
                tile, lanes = tile_part(acc, owner, q, pieces, unit)
                out[m, :, q] = acc[tile, :, :, lanes].astype(out.dtype)


def grad_kernel(cols, flip, wides, labels, info, *refs):
    x_refs, (h_ref, out, x, h, x_sems, h_sems) = refs[:wides], refs[wides:]
    copies = wide_copies(x_refs, x, x_sems, info[1])
    copies += hidden_copies(h_ref, labels, h, h_sems, info[0])
    out[...] = jnp.zeros_like(out)
    for copy in copies:
        copy.wait()

    def add(s, wide, hidden):
        total = 0.0
        for chunk in chunks(x.shape[1]):
            a, b = flat(x[wide, chunk]), flat(h[hidden, chunk])
            a, b = (a, b) if flip else (b, a)
            total += matmul(a, b, 0, 0)
        out[s] = total.astype(out.dtype)

    over_slots(info, out.shape[0], cols, add)


def call(kernel, out_shape, scratch, flops, moved, *args):
    return pl.pallas_call(
        kernel,
        out_shape=out_shape,
        in_specs=[pl.BlockSpec(memory_space=pltpu.SMEM)] + args[1],
        out_specs=jax.tree.map(lambda _: pl.BlockSpec(memory_space=pltpu.VMEM), out_shape),
        scratch_shapes=scratch,
        compiler_params=pltpu.CompilerParams(vmem_limit_bytes=VMEM),
        cost_estimate=pl.CostEstimate(flops=flops, bytes_accessed=moved, transcendentals=0),
    )(args[0], *args[2])


def wide_scratch(blocks, rows, tile, unit):
    held = pltpu.VMEM((D // tile, blocks, rows, tile), jnp.bfloat16)
    return [held, pltpu.SemaphoreType.DMA((D // unit,))]


def to_hidden(info, xs, w, cols, flip):
    rows, unit = xs[0].shape[-2:]
    slots, tile, _ = w.shape
    blocks = lax.axis_size("row")
    outs = [jax.ShapeDtypeStruct((cols, rows, tile), jnp.bfloat16)] * blocks
    held, sems = wide_scratch(blocks, rows, tile, unit)
    scratch = [held, pltpu.VMEM((cols, blocks, rows, tile), jnp.float32), sems]
    kernel = functools.partial(to_hidden_kernel, cols, flip, len(xs))
    specs = [pl.BlockSpec(memory_space=pltpu.VMEM)] + [ANY] * len(xs)
    flops = 2 * slots * blocks * rows * tile * tile
    return call(kernel, outs, scratch, flops, 8 << 20, info, specs, [w, *xs])


def from_hidden(info, h, w, cols, flip, labels, devices):
    rows, tile = h.shape[-2:]
    slots, group = w.shape[0], len(labels)
    unit = min(tile, D // devices)
    pieces = D // devices // unit
    shape = (group, pieces, rows, unit)
    if long_row():
        outs = [jax.ShapeDtypeStruct((devices, *shape), jnp.bfloat16)]
    else:
        outs = [jax.ShapeDtypeStruct((devices // 2, *shape), jnp.bfloat16)] * 2
    scratch = [
        pltpu.VMEM((cols, group, rows, tile), jnp.bfloat16),
        pltpu.VMEM((D // tile, group, rows, tile), jnp.float32),
        pltpu.SemaphoreType.DMA((group,)),
    ]
    kernel = functools.partial(from_hidden_kernel, cols, flip, labels)
    specs = [pl.BlockSpec(memory_space=pltpu.VMEM), ANY]
    flops = 2 * slots * group * rows * tile * tile
    return call(kernel, outs, scratch, flops, 8 << 20, info, specs, [w, h])


def slot_grads(info, xs, h, slots, cols, flip):
    blocks = lax.axis_size("row")
    labels = range(blocks)
    rows, unit = xs[0].shape[-2:]
    tile = h.shape[-1]
    out = jax.ShapeDtypeStruct((slots, tile, tile), jnp.bfloat16)
    held, sems = wide_scratch(blocks, rows, tile, unit)
    scratch = [
        held,
        pltpu.VMEM((cols, blocks, rows, tile), jnp.bfloat16),
        sems,
        pltpu.SemaphoreType.DMA((blocks,)),
    ]
    kernel = functools.partial(grad_kernel, cols, flip, len(xs), labels)
    specs = [ANY] * (len(xs) + 1)
    flops = 2 * slots * blocks * rows * tile * tile
    return call(kernel, out, scratch, flops, 8 << 20, info, specs, [*xs, h])


def long_row():
    return lax.axis_size("row") != 4


def swap_col(x, m):
    count = lax.axis_size("col")
    return lax.ppermute(x, "col", [(s, s ^ m) for s in range(count)])


def swap_row(x, t):
    return lax.ppermute(x, "row", [(s, s ^ t) for s in range(4)])


def send_row(x, *pairs):
    return lax.ppermute(x, "row", pairs)


def own_pieces(x, tile):
    rows, width = x.shape
    unit = min(width, tile)
    return jnp.swapaxes(x.reshape(rows, width // unit, unit), 0, 1)


def after(values, *others):
    return lax.optimization_barrier((values, others))[0]


def across(mine):
    return [swap_col(mine, m) if m else mine for m in range(0, lax.axis_size("col"), 2)]


def with_odd(even):
    return [x for own in even for x in (own, swap_col(own, 1))]


def add(*terms):
    return sum(term.astype(jnp.float32) for term in terms)


def line_reduce(parts, row, wait=()):
    right = send_row(parts[2], (0, 1), (1, 2))
    left = send_row(parts[2], (3, 2), (2, 1))
    far = send_row(parts[3], (0, 2), (3, 1))
    right, left, far = first = after((right, left, far), wait)
    none = jnp.zeros_like(far)
    right = add(jnp.where(row == 1, parts[3], parts[1]), right, jnp.where(row == 2, far, none))
    left = add(jnp.where(row == 2, parts[3], parts[1]), left, jnp.where(row == 1, far, none))
    right = send_row(right.astype(jnp.bfloat16), (0, 1), (1, 2), (2, 3))
    left = send_row(left.astype(jnp.bfloat16), (3, 2), (2, 1), (1, 0))
    return (parts[0], right, left), first


def line_gather(x):
    return [x] + [swap_row(x, t) for t in range(1, 4)]


def finish_col(even, odd):
    pairs = add(even, swap_col(odd, 1)).astype(jnp.bfloat16)
    sums = [pairs[0]] + [swap_col(pairs[m], 2 * m) for m in range(1, even.shape[0])]
    return add(*sums).astype(jnp.bfloat16)


def rows_first(total):
    return jnp.swapaxes(total, 0, 1).reshape(total.shape[1], -1).astype(jnp.bfloat16)


def finish_row(sums):
    return rows_first(add(sums[0], *[swap_row(sums[t], t) for t in range(1, 4)]))


def activations(hidden, grad_activ):
    sigmoid = jax.nn.sigmoid(hidden)
    slope = sigmoid * (1.0 + hidden * (1.0 - sigmoid))
    return (grad_activ * slope).astype(jnp.bfloat16)


def silu(hidden):
    return (hidden * jax.nn.sigmoid(hidden)).astype(jnp.bfloat16)


def per_device(tokens, upstream, w_in, in_codes, w_out, out_codes):
    tile = w_in.shape[3]
    slots = w_in.shape[1]
    devices = lax.axis_size("col")
    cols = FF // (tile * devices)
    row, col = lax.axis_index("row"), lax.axis_index("col")

    def slot_info(codes):
        own = lax.dynamic_slice_in_dim(codes[0], row * slots, slots)
        place = jnp.stack([row, col]).astype(jnp.int32)
        return jnp.concatenate([place, own])

    info_in, info_out = slot_info(in_codes), slot_info(out_codes)
    w_in, w_out = w_in[0], w_out[0]
    tokens, upstream = own_pieces(tokens, tile), own_pieces(upstream, tile)
    args = (info_in, info_out, tokens, upstream, w_in, w_out, cols, devices)
    results = on_long_row(*args) if long_row() else on_line(*args)
    layer_out, grad_tokens, grad_w_in, grad_w_out = results
    return layer_out, grad_tokens, grad_w_in[None], grad_w_out[None]


def on_line(info_in, info_out, tokens, upstream, w_in, w_out, cols, devices):
    row, slots = info_in[0], w_in.shape[0]
    token_blocks, up_blocks = line_gather(tokens), line_gather(upstream)
    token_even = across(jnp.stack(token_blocks))
    up_mine = jnp.stack(up_blocks)
    all_tokens = with_odd(after(token_even, up_mine))
    up_even = across(after(up_mine, token_even[1:]))
    parts = to_hidden(info_in, all_tokens, w_in, cols, False)
    all_up = with_odd(after(up_even, parts))
    terms, first = line_reduce(parts, row, up_even)
    parts = to_hidden(info_out, after(all_up, first), w_out, cols, True)
    hidden = add(*after(terms, parts))
    activ = silu(hidden)
    terms, _ = line_reduce(after(parts, activ), row)
    all_activ = lax.all_gather(activ, "row")
    grad_hidden = activations(hidden, add(*terms))
    all_grad = lax.all_gather(grad_hidden, "row")

    def column_sums(info, hs, w, flip, labels):
        total = finish_col(*from_hidden(info, hs, w, cols, flip, labels, devices))
        return [total[g] for g in range(len(labels))]

    all_activ = after(all_activ, grad_hidden)
    layer_sums = column_sums(info_out, all_activ, w_out, False, (0, 1, 2, 3))
    grad_w_out = slot_grads(info_out, all_up, all_activ, slots, cols, False)
    held = (all_grad, layer_sums, grad_w_out)
    all_grad, layer_sums, grad_w_out = lax.optimization_barrier(held)
    input_sums = column_sums(info_in, all_grad, w_in, True, (0, 1, 2, 3))
    grad_w_in = slot_grads(info_in, all_tokens, all_grad, slots, cols, True)
    layer_out, grad_tokens = finish_row(layer_sums), finish_row(input_sums)
    return layer_out, grad_tokens, grad_w_in, grad_w_out


def on_long_row(info_in, info_out, tokens, upstream, w_in, w_out, cols, devices):
    slots, blocks = w_in.shape[0], lax.axis_size("row")

    def everywhere(x):
        return [lax.all_gather(lax.all_gather(x, "row"), "col")]

    def hidden_side(info, xs, w, flip):
        parts = jnp.stack(to_hidden(info, xs, w, cols, flip))
        return lax.psum_scatter(parts, "row", scatter_dimension=0).astype(jnp.float32)

    def wide_side(info, hs, w, flip):
        sums = []
        for chunk in chunks(blocks):
            if sums:
                hs, _ = lax.optimization_barrier((hs, sums[-1]))
            labels = range(blocks)[chunk]
            [parts] = from_hidden(info, hs, w, cols, flip, labels, devices)
            sums.append(lax.psum_scatter(parts, "col", scatter_dimension=0))
        total = lax.psum_scatter(jnp.concatenate(sums), "row", scatter_dimension=0)
        return rows_first(total)

    hidden = hidden_side(info_in, everywhere(tokens), w_in, False)
    upstream, hidden = lax.optimization_barrier((upstream, hidden))
    all_up = everywhere(upstream)
    grad_activ = hidden_side(info_out, all_up, w_out, True)
    all_activ = lax.all_gather(silu(hidden), "row")
    layer_out = wide_side(info_out, all_activ, w_out, False)
    grad_w_out = slot_grads(info_out, all_up, all_activ, slots, cols, False)
    held = (activations(hidden, grad_activ), tokens, layer_out, grad_w_out)
    grad_hidden, tokens, layer_out, grad_w_out = lax.optimization_barrier(held)
    all_grad = lax.all_gather(grad_hidden, "row")
    grad_tokens = wide_side(info_in, all_grad, w_in, True)
    grad_w_in = slot_grads(info_in, everywhere(tokens), all_grad, slots, cols, True)
    return layer_out, grad_tokens, grad_w_in, grad_w_out


def solution(mesh):
    placed = (
        P("row", "col"),
        P("row", "col"),
        P("col", "row", None, None),
        P("col", None),
        P("col", "row", None, None),
        P("col", None),
    )
    return jax.shard_map(
        per_device,
        mesh=mesh,
        in_specs=placed,
        out_specs=(
            P("row", "col"),
            P("row", "col"),
            P("col", "row", None, None),
            P("col", "row", None, None),
        ),
        check_vma=False,
    )
```

```python
import functools

import jax
import jax.numpy as jnp
from jax import lax
from jax.experimental import pallas as pl
from jax.experimental.pallas import tpu as pltpu
from jax.sharding import PartitionSpec as P

D = 4096
FF = 16384
VMEM = 56 * 1024 * 1024
GROUP = 4
ANY = pl.BlockSpec(memory_space=pl.ANY)


def matmul(a, b, a_dim, b_dim):
    return lax.dot_general(
        a, b, (((a_dim,), (b_dim,)), ((), ())), preferred_element_type=jnp.float32
    )


def flat(block):
    return block.reshape(block.shape[0] * block.shape[1], block.shape[2])


def chunks(blocks):
    group = min(blocks, GROUP)
    return [slice(at, at + group) for at in range(0, blocks, group)]


def tile_part(held, owner, q, pieces, unit):
    tile = held.shape[-1]
    if unit == tile:
        return owner * pieces + q, slice(None)
    parts = tile // unit
    lane = pl.multiple_of(lax.rem(owner, parts) * unit, unit)
    return lax.div(owner, parts), pl.ds(lane, unit)


def wide_copies(refs, labels, held, sems, col):
    copies = []
    if len(refs) == 1:
        pairs = [(m, refs[0].at[m]) for m in range(refs[0].shape[0])]
    else:
        pairs = [(lax.bitwise_xor(col, m), ref) for m, ref in enumerate(refs)]
    for owner, ref in pairs:
        blocks, pieces, _, unit = ref.shape
        whole = len(labels) == blocks
        for q in range(pieces):
            tile, lanes = tile_part(held, owner, q, pieces, unit)
            for g, t in [(slice(None), slice(None))] if whole else enumerate(labels):
                target = held.at[tile, g, :, lanes]
                copies.append(pltpu.make_async_copy(ref.at[t, q], target, sems.at[len(copies)]))
                copies[-1].start()
    return copies


def hidden_copies(refs, labels, held, sems, row):
    copies = []
    for g, t in enumerate(labels):
        source = refs[g] if len(refs) > 1 else refs[0].at[lax.bitwise_xor(row, t)]
        copies.append(pltpu.make_async_copy(source, held.at[:, g], sems.at[g]))
        copies[-1].start()
    return copies


def over_slots(info, first, slots, cols, body):
    def slot(s, carry):
        code = info[2 + first + s]

        @pl.when(code >= 0)
        def _():
            body(s, lax.div(code, cols), lax.rem(code, cols))

        return carry

    lax.fori_loop(0, slots, slot, 0)


def to_hidden_kernel(cols, flip, labels, wides, weights, info, *refs):
    w_refs, x_refs, refs = refs[:weights], refs[weights:weights + wides], refs[weights + wides:]
    *outs, x, acc, sems = refs
    copies = wide_copies(x_refs, labels, x, sems, info[1])
    acc[...] = jnp.zeros_like(acc)
    for copy in copies:
        copy.wait()

    for at, w_ref in enumerate(w_refs):
        def add(s, wide, hidden, w_ref=w_ref):
            for chunk in chunks(x.shape[1]):
                product = matmul(flat(x[wide, chunk]), w_ref[s], 1, 1 if flip else 0)
                acc[hidden, chunk] += product.reshape(-1, *acc.shape[2:])

        over_slots(info, at * w_ref.shape[0], w_ref.shape[0], cols, add)
    for part, out in enumerate(outs):
        out[...] = acc[:, part].astype(out.dtype)


def from_hidden_kernel(cols, flip, labels, hiddens, weights, info, *refs):
    w_refs, h_refs = refs[:weights], refs[weights:weights + hiddens]
    *outs, h, acc, sems = refs[weights + hiddens:]
    copies = hidden_copies(h_refs, labels, h, sems, info[0])
    acc[...] = jnp.zeros_like(acc)
    for copy in copies:
        copy.wait()

    for at, w_ref in enumerate(w_refs):
        def add(s, wide, hidden, w_ref=w_ref):
            for chunk in chunks(h.shape[1]):
                product = matmul(flat(h[hidden, chunk]), w_ref[s], 1, 1 if flip else 0)
                acc[wide, chunk] += product.reshape(-1, *acc.shape[2:])

        over_slots(info, at * w_ref.shape[0], w_ref.shape[0], cols, add)
    for at, out in enumerate(outs):
        pieces, unit = out.shape[-3], out.shape[-1]
        for m in range(out.shape[0]):
            owner = m if len(outs) == 1 else lax.bitwise_xor(info[1], 2 * m + at)
            for q in range(pieces):
                tile, lanes = tile_part(acc, owner, q, pieces, unit)
                out[m, :, q] = acc[tile, :, :, lanes].astype(out.dtype)


def grad_kernel(cols, flip, wides, labels, info, *refs):
    x_refs, h_refs = refs[:wides], refs[wides:-5]
    out, x, h, x_sems, h_sems = refs[-5:]
    copies = wide_copies(x_refs, labels, x, x_sems, info[1])
    copies += hidden_copies(h_refs, labels, h, h_sems, info[0])
    out[...] = jnp.zeros_like(out)
    for copy in copies:
        copy.wait()

    def add(s, wide, hidden):
        total = 0.0
        for chunk in chunks(x.shape[1]):
            a, b = flat(x[wide, chunk]), flat(h[hidden, chunk])
            a, b = (a, b) if flip else (b, a)
            total += matmul(a, b, 0, 0)
        out[s] = total.astype(out.dtype)

    over_slots(info, 0, out.shape[0], cols, add)


def call(kernel, out_shape, scratch, flops, moved, *args):
    return pl.pallas_call(
        kernel,
        out_shape=out_shape,
        in_specs=[pl.BlockSpec(memory_space=pltpu.SMEM)] + args[1],
        out_specs=jax.tree.map(lambda _: pl.BlockSpec(memory_space=pltpu.VMEM), out_shape),
        scratch_shapes=scratch,
        compiler_params=pltpu.CompilerParams(vmem_limit_bytes=VMEM),
        cost_estimate=pl.CostEstimate(flops=flops, bytes_accessed=moved, transcendentals=0),
    )(args[0], *args[2])


def wide_scratch(labels, rows, tile, unit):
    group = len(labels)
    held = pltpu.VMEM((D // tile, group, rows, tile), jnp.bfloat16)
    return [held, pltpu.SemaphoreType.DMA((D // unit * group,))]


def to_hidden(info, xs, ws, cols, flip, labels):
    rows, unit = xs[0].shape[-2:]
    slots, tile, _ = ws[0].shape
    group = len(labels)
    outs = [jax.ShapeDtypeStruct((cols, rows, tile), jnp.bfloat16)] * group
    held, sems = wide_scratch(labels, rows, tile, unit)
    scratch = [held, pltpu.VMEM((cols, group, rows, tile), jnp.float32), sems]
    kernel = functools.partial(to_hidden_kernel, cols, flip, labels, len(xs), len(ws))
    specs = [pl.BlockSpec(memory_space=pltpu.VMEM)] * len(ws) + [ANY] * len(xs)
    flops = 2 * len(ws) * slots * group * rows * tile * tile
    return call(kernel, outs, scratch, flops, 8 << 20, info, specs, [*ws, *xs])


def from_hidden(info, hs, ws, cols, flip, labels, devices):
    rows, tile = hs[0].shape[-2:]
    slots, group = ws[0].shape[0], len(labels)
    unit = min(tile, D // devices)
    pieces = D // devices // unit
    shape = (group, pieces, rows, unit)
    if long_row():
        outs = [jax.ShapeDtypeStruct((devices, *shape), jnp.bfloat16)]
    else:
        outs = [jax.ShapeDtypeStruct((devices // 2, *shape), jnp.bfloat16)] * 2
    scratch = [
        pltpu.VMEM((cols, group, rows, tile), jnp.bfloat16),
        pltpu.VMEM((D // tile, group, rows, tile), jnp.float32),
        pltpu.SemaphoreType.DMA((group,)),
    ]
    kernel = functools.partial(from_hidden_kernel, cols, flip, labels, len(hs), len(ws))
    specs = [pl.BlockSpec(memory_space=pltpu.VMEM)] * len(ws) + [ANY] * len(hs)
    flops = 2 * len(ws) * slots * group * rows * tile * tile
    return call(kernel, outs, scratch, flops, 8 << 20, info, specs, [*ws, *hs])


def slot_grads(info, xs, hs, slots, cols, flip):
    blocks = lax.axis_size("row")
    labels = range(blocks)
    rows, unit = xs[0].shape[-2:]
    tile = hs[0].shape[-1]
    out = jax.ShapeDtypeStruct((slots, tile, tile), jnp.bfloat16)
    held, sems = wide_scratch(labels, rows, tile, unit)
    scratch = [
        held,
        pltpu.VMEM((cols, blocks, rows, tile), jnp.bfloat16),
        sems,
        pltpu.SemaphoreType.DMA((blocks,)),
    ]
    kernel = functools.partial(grad_kernel, cols, flip, len(xs), labels)
    specs = [ANY] * (len(xs) + len(hs))
    flops = 2 * slots * blocks * rows * tile * tile
    return call(kernel, out, scratch, flops, 8 << 20, info, specs, [*xs, *hs])


def long_row():
    return lax.axis_size("row") != 4


def swap_col(x, m):
    count = lax.axis_size("col")
    return lax.ppermute(x, "col", [(s, s ^ m) for s in range(count)])


def swap_row(x, t):
    return lax.ppermute(x, "row", [(s, s ^ t) for s in range(4)])


def send_row(x, *pairs):
    return lax.ppermute(x, "row", pairs)


def own_pieces(x, tile):
    rows, width = x.shape
    unit = min(width, tile)
    return jnp.swapaxes(x.reshape(rows, width // unit, unit), 0, 1)


def after(values, *others):
    return lax.optimization_barrier((values, others))[0]


def across(mine):
    return [swap_col(mine, m) if m else mine for m in range(0, lax.axis_size("col"), 2)]


def with_odd(even):
    return [x for own in even for x in (own, swap_col(own, 1))]


def add(*terms):
    return sum(term.astype(jnp.float32) for term in terms)


def line_reduce(parts, row, wait=()):
    right = send_row(parts[2], (0, 1), (1, 2))
    left = send_row(parts[2], (3, 2), (2, 1))
    far = send_row(parts[3], (0, 2), (3, 1))
    right, left, far = first = after((right, left, far), wait)
    none = jnp.zeros_like(far)
    right = add(jnp.where(row == 1, parts[3], parts[1]), right, jnp.where(row == 2, far, none))
    left = add(jnp.where(row == 2, parts[3], parts[1]), left, jnp.where(row == 1, far, none))
    right = send_row(right.astype(jnp.bfloat16), (0, 1), (1, 2), (2, 3))
    left = send_row(left.astype(jnp.bfloat16), (3, 2), (2, 1), (1, 0))
    return (parts[0], right, left), first


def line_gather(x):
    return [x] + [swap_row(x, t) for t in range(1, 4)]


def finish_col(even, odd):
    pairs = add(even, swap_col(odd, 1)).astype(jnp.bfloat16)
    sums = [pairs[0]] + [swap_col(pairs[m], 2 * m) for m in range(1, even.shape[0])]
    return add(*sums).astype(jnp.bfloat16)


def rows_first(total):
    return jnp.swapaxes(total, 0, 1).reshape(total.shape[1], -1).astype(jnp.bfloat16)


def finish_row(sums):
    return rows_first(add(sums[0], *[swap_row(sums[t], t) for t in range(1, 4)]))


def activations(hidden, grad_activ):
    sigmoid = jax.nn.sigmoid(hidden)
    slope = sigmoid * (1.0 + hidden * (1.0 - sigmoid))
    return (grad_activ * slope).astype(jnp.bfloat16)


def silu(hidden):
    return (hidden * jax.nn.sigmoid(hidden)).astype(jnp.bfloat16)


def per_device(tokens, upstream, w_in, in_codes, w_out, out_codes):
    tile = w_in.shape[3]
    slots = w_in.shape[1]
    devices = lax.axis_size("col")
    cols = FF // (tile * devices)
    row, col = lax.axis_index("row"), lax.axis_index("col")

    def slot_info(codes):
        own = lax.dynamic_slice_in_dim(codes[0], row * slots, slots)
        mate = lax.dynamic_slice_in_dim(codes[0], (row ^ 1) * slots, slots)
        place = jnp.stack([row, col]).astype(jnp.int32)
        return jnp.concatenate([place, own, mate])

    info_in, info_out = slot_info(in_codes), slot_info(out_codes)
    w_in, w_out = w_in[0], w_out[0]
    tokens, upstream = own_pieces(tokens, tile), own_pieces(upstream, tile)
    args = (info_in, info_out, tokens, upstream, w_in, w_out, cols, devices)
    results = on_long_row(*args) if long_row() else on_line(*args)
    layer_out, grad_tokens, grad_w_in, grad_w_out = results
    return layer_out, grad_tokens, grad_w_in[None], grad_w_out[None]


def on_line(info_in, info_out, tokens, upstream, w_in, w_out, cols, devices):
    row, slots = info_in[0], w_in.shape[0]
    every, ends = range(4), (0, 3)
    w_pair = [w_in, swap_row(w_in, 1)]
    both = line_gather(jnp.stack([tokens, upstream]))
    token_even = across(jnp.stack([block[0] for block in both]))
    up_mine = after(jnp.stack([block[1] for block in both]), token_even[1:])
    up_even = across(up_mine)
    all_tokens = with_odd(token_even)
    own, far = to_hidden(info_in, all_tokens, w_pair, cols, False, ends)
    all_up = with_odd(after(up_even, own))
    parts = to_hidden(info_out, all_up, [w_out], cols, True, every)
    hidden = add(*after((own, swap_row(far, 3)), parts))
    activ = silu(hidden)
    all_activ = [lax.all_gather(activ, "row")]
    terms, _ = line_reduce(after(parts, activ), row)
    grad_hidden = activations(hidden, add(*terms))
    far_grad = swap_row(grad_hidden, 3)

    def column_sums(info, hs, ws, flip, labels):
        total = finish_col(*from_hidden(info, hs, ws, cols, flip, labels, devices))
        return [total[g] for g in range(len(labels))]

    all_activ = after(all_activ, grad_hidden)
    layer_sums = column_sums(info_out, all_activ, [w_out], False, every)
    grad_w_out = slot_grads(info_out, all_up, all_activ, slots, cols, False)
    ends_grad = after([grad_hidden, far_grad], grad_w_out)
    input_sums = column_sums(info_in, ends_grad, w_pair, True, ends)
    all_grad = [grad_hidden, swap_row(grad_hidden, 1), swap_row(far_grad, 1), far_grad]
    grad_w_in = slot_grads(info_in, all_tokens, all_grad, slots, cols, True)
    layer_out = finish_row(layer_sums)
    grad_tokens = rows_first(add(input_sums[0], swap_row(input_sums[1], 3)))
    return layer_out, grad_tokens, grad_w_in, grad_w_out


def on_long_row(info_in, info_out, tokens, upstream, w_in, w_out, cols, devices):
    slots, blocks = w_in.shape[0], lax.axis_size("row")

    def everywhere(x):
        return [lax.all_gather(lax.all_gather(x, "row"), "col")]

    def hidden_side(info, xs, w, flip):
        parts = jnp.stack(to_hidden(info, xs, [w], cols, flip, range(blocks)))
        return lax.psum_scatter(parts, "row", scatter_dimension=0).astype(jnp.float32)

    def wide_side(info, hs, w, flip):
        sums = []
        for chunk in chunks(blocks):
            if sums:
                hs, _ = lax.optimization_barrier((hs, sums[-1]))
            labels = range(blocks)[chunk]
            [parts] = from_hidden(info, [hs], [w], cols, flip, labels, devices)
            sums.append(lax.psum_scatter(parts, "col", scatter_dimension=0))
        total = lax.psum_scatter(jnp.concatenate(sums), "row", scatter_dimension=0)
        return rows_first(total)

    hidden = hidden_side(info_in, everywhere(tokens), w_in, False)
    upstream, hidden = lax.optimization_barrier((upstream, hidden))
    all_up = everywhere(upstream)
    grad_activ = hidden_side(info_out, all_up, w_out, True)
    all_activ = lax.all_gather(silu(hidden), "row")
    layer_out = wide_side(info_out, all_activ, w_out, False)
    grad_w_out = slot_grads(info_out, all_up, [all_activ], slots, cols, False)
    held = (activations(hidden, grad_activ), tokens, layer_out, grad_w_out)
    grad_hidden, tokens, layer_out, grad_w_out = lax.optimization_barrier(held)
    all_grad = lax.all_gather(grad_hidden, "row")
    grad_tokens = wide_side(info_in, all_grad, w_in, True)
    grad_w_in = slot_grads(info_in, everywhere(tokens), [all_grad], slots, cols, True)
    return layer_out, grad_tokens, grad_w_in, grad_w_out


def solution(mesh):
    placed = (
        P("row", "col"),
        P("row", "col"),
        P("col", "row", None, None),
        P("col", None),
        P("col", "row", None, None),
        P("col", None),
    )
    return jax.shard_map(
        per_device,
        mesh=mesh,
        in_specs=placed,
        out_specs=(
            P("row", "col"),
            P("row", "col"),
            P("col", "row", None, None),
            P("col", "row", None, None),
        ),
        check_vma=False,
    )
```

```python
import functools

import jax
import jax.numpy as jnp
from jax import lax
from jax.experimental import pallas as pl
from jax.experimental.pallas import tpu as pltpu
from jax.sharding import PartitionSpec as P

D = 4096
FF = 16384
VMEM = 56 * 1024 * 1024
GROUP = 4
ANY = pl.BlockSpec(memory_space=pl.ANY)


def matmul(a, b, a_dim, b_dim):
    return lax.dot_general(
        a, b, (((a_dim,), (b_dim,)), ((), ())), preferred_element_type=jnp.float32
    )


def flat(block):
    return block.reshape(block.shape[0] * block.shape[1], block.shape[2])


def chunks(blocks):
    group = min(blocks, GROUP)
    return [slice(at, at + group) for at in range(0, blocks, group)]


def tile_part(held, owner, q, pieces, unit):
    tile = held.shape[-1]
    if unit == tile:
        return owner * pieces + q, slice(None)
    parts = tile // unit
    lane = pl.multiple_of(lax.rem(owner, parts) * unit, unit)
    return lax.div(owner, parts), pl.ds(lane, unit)


def wide_copies(refs, labels, held, sems, col):
    copies = []
    if len(refs) == 1:
        pairs = [(m, refs[0].at[m]) for m in range(refs[0].shape[0])]
    else:
        pairs = [(lax.bitwise_xor(col, m), ref) for m, ref in enumerate(refs)]
    for owner, ref in pairs:
        blocks, pieces, _, unit = ref.shape
        whole = len(labels) == blocks
        for q in range(pieces):
            tile, lanes = tile_part(held, owner, q, pieces, unit)
            for g, t in [(slice(None), slice(None))] if whole else enumerate(labels):
                target = held.at[tile, g, :, lanes]
                copies.append(pltpu.make_async_copy(ref.at[t, q], target, sems.at[len(copies)]))
                copies[-1].start()
    return copies


def hidden_copies(refs, labels, held, sems, row):
    copies = []
    for g, t in enumerate(labels):
        source = refs[g] if len(refs) > 1 else refs[0].at[lax.bitwise_xor(row, t)]
        copies.append(pltpu.make_async_copy(source, held.at[:, g], sems.at[g]))
        copies[-1].start()
    return copies


def over_slots(info, first, slots, cols, body):
    def slot(s, carry):
        code = info[2 + first + s]

        @pl.when(code >= 0)
        def _():
            body(s, lax.div(code, cols), lax.rem(code, cols))

        return carry

    lax.fori_loop(0, slots, slot, 0)


def to_hidden_kernel(cols, flip, labels, wides, weights, info, *refs):
    w_refs, x_refs, refs = refs[:weights], refs[weights:weights + wides], refs[weights + wides:]
    *outs, x, acc, sems = refs
    copies = wide_copies(x_refs, labels, x, sems, info[1])
    acc[...] = jnp.zeros_like(acc)
    for copy in copies:
        copy.wait()

    for at, w_ref in enumerate(w_refs):
        def add(s, wide, hidden, w_ref=w_ref):
            for chunk in chunks(x.shape[1]):
                product = matmul(flat(x[wide, chunk]), w_ref[s], 1, 1 if flip else 0)
                acc[hidden, chunk] += product.reshape(-1, *acc.shape[2:])

        over_slots(info, at * w_ref.shape[0], w_ref.shape[0], cols, add)
    for part, out in enumerate(outs):
        out[...] = acc[:, part].astype(out.dtype)


def from_hidden_kernel(cols, flip, labels, hiddens, weights, info, *refs):
    w_refs, h_refs = refs[:weights], refs[weights:weights + hiddens]
    *outs, h, acc, sems = refs[weights + hiddens:]
    copies = hidden_copies(h_refs, labels, h, sems, info[0])
    acc[...] = jnp.zeros_like(acc)
    for copy in copies:
        copy.wait()

    for at, w_ref in enumerate(w_refs):
        def add(s, wide, hidden, w_ref=w_ref):
            for chunk in chunks(h.shape[1]):
                product = matmul(flat(h[hidden, chunk]), w_ref[s], 1, 1 if flip else 0)
                acc[wide, chunk] += product.reshape(-1, *acc.shape[2:])

        over_slots(info, at * w_ref.shape[0], w_ref.shape[0], cols, add)
    for at, out in enumerate(outs):
        pieces, unit = out.shape[-3], out.shape[-1]
        for m in range(out.shape[0]):
            owner = m if len(outs) == 1 else lax.bitwise_xor(info[1], 2 * m + at)
            for q in range(pieces):
                tile, lanes = tile_part(acc, owner, q, pieces, unit)
                out[m, :, q] = acc[tile, :, :, lanes].astype(out.dtype)


def grad_kernel(cols, flip, wides, labels, info, *refs):
    x_refs, h_refs = refs[:wides], refs[wides:-5]
    out, x, h, x_sems, h_sems = refs[-5:]
    copies = wide_copies(x_refs, labels, x, x_sems, info[1])
    copies += hidden_copies(h_refs, labels, h, h_sems, info[0])
    out[...] = jnp.zeros_like(out)
    for copy in copies:
        copy.wait()

    def add(s, wide, hidden):
        total = 0.0
        for chunk in chunks(x.shape[1]):
            a, b = flat(x[wide, chunk]), flat(h[hidden, chunk])
            a, b = (a, b) if flip else (b, a)
            total += matmul(a, b, 0, 0)
        out[s] = total.astype(out.dtype)

    over_slots(info, 0, out.shape[0], cols, add)


def call(kernel, out_shape, scratch, flops, moved, *args):
    return pl.pallas_call(
        kernel,
        out_shape=out_shape,
        in_specs=[pl.BlockSpec(memory_space=pltpu.SMEM)] + args[1],
        out_specs=jax.tree.map(lambda _: pl.BlockSpec(memory_space=pltpu.VMEM), out_shape),
        scratch_shapes=scratch,
        compiler_params=pltpu.CompilerParams(vmem_limit_bytes=VMEM),
        cost_estimate=pl.CostEstimate(flops=flops, bytes_accessed=moved, transcendentals=0),
    )(args[0], *args[2])


def wide_scratch(labels, rows, tile, unit):
    group = len(labels)
    held = pltpu.VMEM((D // tile, group, rows, tile), jnp.bfloat16)
    return [held, pltpu.SemaphoreType.DMA((D // unit * group,))]


def to_hidden(info, xs, ws, cols, flip, labels):
    rows, unit = xs[0].shape[-2:]
    slots, tile, _ = ws[0].shape
    group = len(labels)
    outs = [jax.ShapeDtypeStruct((cols, rows, tile), jnp.bfloat16)] * group
    held, sems = wide_scratch(labels, rows, tile, unit)
    scratch = [held, pltpu.VMEM((cols, group, rows, tile), jnp.float32), sems]
    kernel = functools.partial(to_hidden_kernel, cols, flip, labels, len(xs), len(ws))
    specs = [pl.BlockSpec(memory_space=pltpu.VMEM)] * len(ws) + [ANY] * len(xs)
    flops = 2 * len(ws) * slots * group * rows * tile * tile
    return call(kernel, outs, scratch, flops, 8 << 20, info, specs, [*ws, *xs])


def from_hidden(info, hs, ws, cols, flip, labels, devices):
    rows, tile = hs[0].shape[-2:]
    slots, group = ws[0].shape[0], len(labels)
    unit = min(tile, D // devices)
    pieces = D // devices // unit
    shape = (group, pieces, rows, unit)
    if long_row():
        outs = [jax.ShapeDtypeStruct((devices, *shape), jnp.bfloat16)]
    else:
        outs = [jax.ShapeDtypeStruct((devices // 2, *shape), jnp.bfloat16)] * 2
    scratch = [
        pltpu.VMEM((cols, group, rows, tile), jnp.bfloat16),
        pltpu.VMEM((D // tile, group, rows, tile), jnp.float32),
        pltpu.SemaphoreType.DMA((group,)),
    ]
    kernel = functools.partial(from_hidden_kernel, cols, flip, labels, len(hs), len(ws))
    specs = [pl.BlockSpec(memory_space=pltpu.VMEM)] * len(ws) + [ANY] * len(hs)
    flops = 2 * len(ws) * slots * group * rows * tile * tile
    return call(kernel, outs, scratch, flops, 8 << 20, info, specs, [*ws, *hs])


def slot_grads(info, xs, hs, slots, cols, flip):
    blocks = lax.axis_size("row")
    labels = range(blocks)
    rows, unit = xs[0].shape[-2:]
    tile = hs[0].shape[-1]
    out = jax.ShapeDtypeStruct((slots, tile, tile), jnp.bfloat16)
    held, sems = wide_scratch(labels, rows, tile, unit)
    scratch = [
        held,
        pltpu.VMEM((cols, blocks, rows, tile), jnp.bfloat16),
        sems,
        pltpu.SemaphoreType.DMA((blocks,)),
    ]
    kernel = functools.partial(grad_kernel, cols, flip, len(xs), labels)
    specs = [ANY] * (len(xs) + len(hs))
    flops = 2 * slots * blocks * rows * tile * tile
    return call(kernel, out, scratch, flops, 8 << 20, info, specs, [*xs, *hs])


def long_row():
    return lax.axis_size("row") != 4


def swap_col(x, m):
    count = lax.axis_size("col")
    return lax.ppermute(x, "col", [(s, s ^ m) for s in range(count)])


def swap_row(x, t):
    return lax.ppermute(x, "row", [(s, s ^ t) for s in range(4)])


def own_pieces(x, tile):
    rows, width = x.shape
    unit = min(width, tile)
    return jnp.swapaxes(x.reshape(rows, width // unit, unit), 0, 1)


def after(values, *others):
    return lax.optimization_barrier((values, others))[0]


def across(mine):
    return [swap_col(mine, m) if m else mine for m in range(0, lax.axis_size("col"), 2)]


def with_odd(even):
    return [x for own in even for x in (own, swap_col(own, 1))]


def add(*terms):
    return sum(term.astype(jnp.float32) for term in terms)


def line_gather(x):
    return [x] + [swap_row(x, t) for t in range(1, 4)]


def pair_sums(even, odd):
    return add(even, swap_col(odd, 1)).astype(jnp.bfloat16)


def finish_col(pairs):
    sums = [pairs[0]] + [swap_col(pairs[m], 2 * m) for m in range(1, pairs.shape[0])]
    return add(*sums).astype(jnp.bfloat16)


def rows_first(total):
    return jnp.swapaxes(total, 0, 1).reshape(total.shape[1], -1).astype(jnp.bfloat16)


def finish_row(sums):
    return rows_first(add(sums[0], swap_row(sums[1], 3)))


def activations(hidden, grad_activ):
    sigmoid = jax.nn.sigmoid(hidden)
    slope = sigmoid * (1.0 + hidden * (1.0 - sigmoid))
    return (grad_activ * slope).astype(jnp.bfloat16)


def silu(hidden):
    return (hidden * jax.nn.sigmoid(hidden)).astype(jnp.bfloat16)


def per_device(tokens, upstream, w_in, in_codes, w_out, out_codes):
    tile = w_in.shape[3]
    slots = w_in.shape[1]
    devices = lax.axis_size("col")
    cols = FF // (tile * devices)
    row, col = lax.axis_index("row"), lax.axis_index("col")

    def slot_info(codes):
        own = lax.dynamic_slice_in_dim(codes[0], row * slots, slots)
        mate = lax.dynamic_slice_in_dim(codes[0], (row ^ 1) * slots, slots)
        place = jnp.stack([row, col]).astype(jnp.int32)
        return jnp.concatenate([place, own, mate])

    info_in, info_out = slot_info(in_codes), slot_info(out_codes)
    w_in, w_out = w_in[0], w_out[0]
    tokens, upstream = own_pieces(tokens, tile), own_pieces(upstream, tile)
    args = (info_in, info_out, tokens, upstream, w_in, w_out, cols, devices)
    results = on_long_row(*args) if long_row() else on_line(*args)
    layer_out, grad_tokens, grad_w_in, grad_w_out = results
    return layer_out, grad_tokens, grad_w_in[None], grad_w_out[None]


def on_line(info_in, info_out, tokens, upstream, w_in, w_out, cols, devices):
    slots = w_in.shape[0]
    ends = (0, 3)
    in_pair = [w_in, swap_row(w_in, 1)]
    out_pair = [w_out, swap_row(after(w_out, in_pair[1]), 1)]
    both = line_gather(jnp.stack([tokens, upstream]))
    token_even = across(jnp.stack([block[0] for block in both]))
    up_mine = after(jnp.stack([block[1] for block in both]), token_even[1:])
    up_even = across(up_mine)
    all_tokens = with_odd(token_even)
    own, far = to_hidden(info_in, all_tokens, in_pair, cols, False, ends)
    far = swap_row(far, 3)
    hidden = add(own, far)
    activ = silu(hidden)
    all_up = with_odd(after(up_even, own))
    activ_far = swap_row(activ, 3)
    own, far = to_hidden(info_out, after(all_up, activ_far), out_pair, cols, True, ends)
    far, activ_near = swap_row(far, 3), swap_row(after(activ, own), 1)
    ends_activ = after([activ, activ_far], own)
    layer_parts = from_hidden(info_out, ends_activ, out_pair, cols, False, ends, devices)
    grad_hidden = activations(hidden, add(own, after(far, layer_parts, activ_near)))
    grad_far = swap_row(grad_hidden, 3)
    all_activ = [activ, activ_near, swap_row(after(activ_far, grad_hidden), 1), activ_far]
    layer_sums = finish_col(pair_sums(*after(layer_parts, grad_hidden)))
    ends_grad = after([grad_hidden, grad_far], all_activ[2], layer_sums)
    input_parts = from_hidden(info_in, ends_grad, in_pair, cols, True, ends, devices)
    grad_near, grad_next = swap_row(grad_hidden, 1), swap_row(grad_far, 1)
    all_grad = [grad_hidden, grad_near, grad_next, grad_far]
    input_pairs = pair_sums(*input_parts)
    input_sums = finish_col(input_pairs)
    all_activ, all_grad = after((all_activ, all_grad), input_pairs)
    grad_w_out = slot_grads(info_out, all_up, all_activ, slots, cols, False)
    grad_w_in = slot_grads(info_in, all_tokens, all_grad, slots, cols, True)
    layer_out, grad_tokens = finish_row(layer_sums), finish_row(input_sums)
    return layer_out, grad_tokens, grad_w_in, grad_w_out


def on_long_row(info_in, info_out, tokens, upstream, w_in, w_out, cols, devices):
    slots, blocks = w_in.shape[0], lax.axis_size("row")

    def everywhere(x):
        return [lax.all_gather(lax.all_gather(x, "row"), "col")]

    def hidden_side(info, xs, w, flip):
        parts = jnp.stack(to_hidden(info, xs, [w], cols, flip, range(blocks)))
        return lax.psum_scatter(parts, "row", scatter_dimension=0).astype(jnp.float32)

    def wide_side(info, hs, w, flip):
        sums = []
        for chunk in chunks(blocks):
            if sums:
                hs, _ = lax.optimization_barrier((hs, sums[-1]))
            labels = range(blocks)[chunk]
            [parts] = from_hidden(info, [hs], [w], cols, flip, labels, devices)
            sums.append(lax.psum_scatter(parts, "col", scatter_dimension=0))
        total = lax.psum_scatter(jnp.concatenate(sums), "row", scatter_dimension=0)
        return rows_first(total)

    hidden = hidden_side(info_in, everywhere(tokens), w_in, False)
    upstream, hidden = lax.optimization_barrier((upstream, hidden))
    all_up = everywhere(upstream)
    grad_activ = hidden_side(info_out, all_up, w_out, True)
    all_activ = lax.all_gather(silu(hidden), "row")
    layer_out = wide_side(info_out, all_activ, w_out, False)
    grad_w_out = slot_grads(info_out, all_up, [all_activ], slots, cols, False)
    held = (activations(hidden, grad_activ), tokens, layer_out, grad_w_out)
    grad_hidden, tokens, layer_out, grad_w_out = lax.optimization_barrier(held)
    all_grad = lax.all_gather(grad_hidden, "row")
    grad_tokens = wide_side(info_in, all_grad, w_in, True)
    grad_w_in = slot_grads(info_in, everywhere(tokens), [all_grad], slots, cols, True)
    return layer_out, grad_tokens, grad_w_in, grad_w_out


def solution(mesh):
    placed = (
        P("row", "col"),
        P("row", "col"),
        P("col", "row", None, None),
        P("col", None),
        P("col", "row", None, None),
        P("col", None),
    )
    return jax.shard_map(
        per_device,
        mesh=mesh,
        in_specs=placed,
        out_specs=(
            P("row", "col"),
            P("row", "col"),
            P("col", "row", None, None),
            P("col", "row", None, None),
        ),
        check_vma=False,
    )
```

```python
import functools

import jax
import jax.numpy as jnp
from jax import lax
from jax.experimental import pallas as pl
from jax.experimental.pallas import tpu as pltpu
from jax.sharding import PartitionSpec as P

D = 4096
FF = 16384
VMEM = 56 * 1024 * 1024
GROUP = 4
ANY = pl.BlockSpec(memory_space=pl.ANY)


def matmul(a, b, a_dim, b_dim):
    return lax.dot_general(
        a, b, (((a_dim,), (b_dim,)), ((), ())), preferred_element_type=jnp.float32
    )


def flat(block):
    return block.reshape(block.shape[0] * block.shape[1], block.shape[2])


def chunks(blocks):
    group = min(blocks, GROUP)
    return [slice(at, at + group) for at in range(0, blocks, group)]


def tile_part(held, owner, q, pieces, unit):
    tile = held.shape[-1]
    if unit == tile:
        return owner * pieces + q, slice(None)
    parts = tile // unit
    lane = pl.multiple_of(lax.rem(owner, parts) * unit, unit)
    return lax.div(owner, parts), pl.ds(lane, unit)


def wide_copies(refs, labels, held, sems, col):
    copies = []
    if len(refs) == 1:
        pairs = [(m, refs[0].at[m]) for m in range(refs[0].shape[0])]
    else:
        pairs = [(lax.bitwise_xor(col, m), ref) for m, ref in enumerate(refs)]
    for owner, ref in pairs:
        blocks, pieces, _, unit = ref.shape
        whole = len(labels) == blocks
        for q in range(pieces):
            tile, lanes = tile_part(held, owner, q, pieces, unit)
            for g, t in [(slice(None), slice(None))] if whole else enumerate(labels):
                target = held.at[tile, g, :, lanes]
                copies.append(pltpu.make_async_copy(ref.at[t, q], target, sems.at[len(copies)]))
                copies[-1].start()
    return copies


def hidden_copies(refs, labels, held, sems, row):
    copies = []
    for g, t in enumerate(labels):
        source = refs[g] if len(refs) > 1 else refs[0].at[lax.bitwise_xor(row, t)]
        copies.append(pltpu.make_async_copy(source, held.at[:, g], sems.at[g]))
        copies[-1].start()
    return copies


def over_slots(info, first, slots, cols, body):
    step = 4 if slots % 4 == 0 else 1

    def some(at, carry):
        for s in [at * step + i for i in range(step)]:
            code = info[2 + first + s]
            tile = jnp.maximum(code, 0)
            body(s, code >= 0, lax.div(tile, cols), lax.rem(tile, cols))
        return carry

    lax.fori_loop(0, slots // step, some, 0)


def to_hidden_kernel(cols, flip, labels, wides, weights, info, *refs):
    w_refs, x_refs, refs = refs[:weights], refs[weights:weights + wides], refs[weights + wides:]
    *outs, x, acc, sems = refs
    copies = wide_copies(x_refs, labels, x, sems, info[1])
    acc[...] = jnp.zeros_like(acc)
    for copy in copies:
        copy.wait()

    for at, w_ref in enumerate(w_refs):
        def add(s, filled, wide, hidden, w_ref=w_ref):
            target = jnp.where(filled, hidden, acc.shape[0] - 1)
            for chunk in chunks(x.shape[1]):
                product = matmul(flat(x[wide, chunk]), w_ref[s], 1, 1 if flip else 0)
                acc[target, chunk] += product.reshape(-1, *acc.shape[2:])

        over_slots(info, at * w_ref.shape[0], w_ref.shape[0], cols, add)
    for part, out in enumerate(outs):
        out[...] = acc[:out.shape[0], part].astype(out.dtype)


def from_hidden_kernel(cols, flip, labels, hiddens, weights, info, *refs):
    w_refs, h_refs = refs[:weights], refs[weights:weights + hiddens]
    *outs, h, acc, sems = refs[weights + hiddens:]
    copies = hidden_copies(h_refs, labels, h, sems, info[0])
    acc[...] = jnp.zeros_like(acc)
    for copy in copies:
        copy.wait()

    for at, w_ref in enumerate(w_refs):
        def add(s, filled, wide, hidden, w_ref=w_ref):
            target = jnp.where(filled, wide, acc.shape[0] - 1)
            for chunk in chunks(h.shape[1]):
                product = matmul(flat(h[hidden, chunk]), w_ref[s], 1, 1 if flip else 0)
                acc[target, chunk] += product.reshape(-1, *acc.shape[2:])

        over_slots(info, at * w_ref.shape[0], w_ref.shape[0], cols, add)
    for at, out in enumerate(outs):
        pieces, unit = out.shape[-3], out.shape[-1]
        for m in range(out.shape[0]):
            owner = m if len(outs) == 1 else lax.bitwise_xor(info[1], 2 * m + at)
            for q in range(pieces):
                tile, lanes = tile_part(acc, owner, q, pieces, unit)
                out[m, :, q] = acc[tile, :, :, lanes].astype(out.dtype)


def grad_kernel(cols, flip, wides, labels, info, *refs):
    x_refs, h_refs = refs[:wides], refs[wides:-5]
    out, x, h, x_sems, h_sems = refs[-5:]
    copies = wide_copies(x_refs, labels, x, x_sems, info[1])
    copies += hidden_copies(h_refs, labels, h, h_sems, info[0])
    for copy in copies:
        copy.wait()

    def add(s, filled, wide, hidden):
        total = 0.0
        for chunk in chunks(x.shape[1]):
            a, b = flat(x[wide, chunk]), flat(h[hidden, chunk])
            a, b = (a, b) if flip else (b, a)
            total += matmul(a, b, 0, 0)
        out[s] = jnp.where(filled, total, 0.0).astype(out.dtype)

    over_slots(info, 0, out.shape[0], cols, add)


def call(kernel, out_shape, scratch, flops, moved, *args):
    return pl.pallas_call(
        kernel,
        out_shape=out_shape,
        in_specs=[pl.BlockSpec(memory_space=pltpu.SMEM)] + args[1],
        out_specs=jax.tree.map(lambda _: pl.BlockSpec(memory_space=pltpu.VMEM), out_shape),
        scratch_shapes=scratch,
        compiler_params=pltpu.CompilerParams(vmem_limit_bytes=VMEM),
        cost_estimate=pl.CostEstimate(flops=flops, bytes_accessed=moved, transcendentals=0),
    )(args[0], *args[2])


def wide_scratch(labels, rows, tile, unit):
    group = len(labels)
    held = pltpu.VMEM((D // tile, group, rows, tile), jnp.bfloat16)
    return [held, pltpu.SemaphoreType.DMA((D // unit * group,))]


def to_hidden(info, xs, ws, cols, flip, labels):
    rows, unit = xs[0].shape[-2:]
    slots, tile, _ = ws[0].shape
    group = len(labels)
    outs = [jax.ShapeDtypeStruct((cols, rows, tile), jnp.bfloat16)] * group
    held, sems = wide_scratch(labels, rows, tile, unit)
    scratch = [held, pltpu.VMEM((cols + 1, group, rows, tile), jnp.float32), sems]
    kernel = functools.partial(to_hidden_kernel, cols, flip, labels, len(xs), len(ws))
    specs = [pl.BlockSpec(memory_space=pltpu.VMEM)] * len(ws) + [ANY] * len(xs)
    flops = 2 * len(ws) * slots * group * rows * tile * tile
    return call(kernel, outs, scratch, flops, 8 << 20, info, specs, [*ws, *xs])


def from_hidden(info, hs, ws, cols, flip, labels, devices):
    rows, tile = hs[0].shape[-2:]
    slots, group = ws[0].shape[0], len(labels)
    unit = min(tile, D // devices)
    pieces = D // devices // unit
    shape = (group, pieces, rows, unit)
    if long_row():
        outs = [jax.ShapeDtypeStruct((devices, *shape), jnp.bfloat16)]
    else:
        outs = [jax.ShapeDtypeStruct((devices // 2, *shape), jnp.bfloat16)] * 2
    scratch = [
        pltpu.VMEM((cols, group, rows, tile), jnp.bfloat16),
        pltpu.VMEM((D // tile + 1, group, rows, tile), jnp.float32),
        pltpu.SemaphoreType.DMA((group,)),
    ]
    kernel = functools.partial(from_hidden_kernel, cols, flip, labels, len(hs), len(ws))
    specs = [pl.BlockSpec(memory_space=pltpu.VMEM)] * len(ws) + [ANY] * len(hs)
    flops = 2 * len(ws) * slots * group * rows * tile * tile
    return call(kernel, outs, scratch, flops, 8 << 20, info, specs, [*ws, *hs])


def slot_grads(info, xs, hs, slots, cols, flip):
    blocks = lax.axis_size("row")
    labels = range(blocks)
    rows, unit = xs[0].shape[-2:]
    tile = hs[0].shape[-1]
    out = jax.ShapeDtypeStruct((slots, tile, tile), jnp.bfloat16)
    held, sems = wide_scratch(labels, rows, tile, unit)
    scratch = [
        held,
        pltpu.VMEM((cols, blocks, rows, tile), jnp.bfloat16),
        sems,
        pltpu.SemaphoreType.DMA((blocks,)),
    ]
    kernel = functools.partial(grad_kernel, cols, flip, len(xs), labels)
    specs = [ANY] * (len(xs) + len(hs))
    flops = 2 * slots * blocks * rows * tile * tile
    return call(kernel, out, scratch, flops, 8 << 20, info, specs, [*xs, *hs])


def long_row():
    return lax.axis_size("row") != 4


def swap_col(x, m):
    count = lax.axis_size("col")
    return lax.ppermute(x, "col", [(s, s ^ m) for s in range(count)])


def swap_row(x, t):
    return lax.ppermute(x, "row", [(s, s ^ t) for s in range(4)])


def own_pieces(x, tile):
    rows, width = x.shape
    unit = min(width, tile)
    return jnp.swapaxes(x.reshape(rows, width // unit, unit), 0, 1)


def after(values, *others):
    return lax.optimization_barrier((values, others))[0]


def across(mine):
    return [swap_col(mine, m) if m else mine for m in range(0, lax.axis_size("col"), 2)]


def with_odd(even):
    return [x for own in even for x in (own, swap_col(own, 1))]


def add(*terms):
    return sum(term.astype(jnp.float32) for term in terms)


def line_gather(x):
    return [x] + [swap_row(x, t) for t in range(1, 4)]


def pair_sums(even, odd):
    return add(even, swap_col(odd, 1)).astype(jnp.bfloat16)


def finish_col(pairs, *wait):
    sums = [pairs[0]] + [swap_col(pairs[m], 2 * m) for m in range(1, pairs.shape[0])]
    return add(*after(sums, *wait)).astype(jnp.bfloat16)


def rows_first(total):
    return jnp.swapaxes(total, 0, 1).reshape(total.shape[1], -1).astype(jnp.bfloat16)


def activations(hidden, grad_activ):
    sigmoid = jax.nn.sigmoid(hidden)
    slope = sigmoid * (1.0 + hidden * (1.0 - sigmoid))
    return (grad_activ * slope).astype(jnp.bfloat16)


def silu(hidden):
    return (hidden * jax.nn.sigmoid(hidden)).astype(jnp.bfloat16)


def per_device(tokens, upstream, w_in, in_codes, w_out, out_codes):
    tile = w_in.shape[3]
    slots = w_in.shape[1]
    devices = lax.axis_size("col")
    cols = FF // (tile * devices)
    row, col = lax.axis_index("row"), lax.axis_index("col")

    def slot_info(codes):
        own = lax.dynamic_slice_in_dim(codes[0], row * slots, slots)
        mate = lax.dynamic_slice_in_dim(codes[0], (row ^ 1) * slots, slots)
        place = jnp.stack([row, col]).astype(jnp.int32)
        return jnp.concatenate([place, own, mate])

    info_in, info_out = slot_info(in_codes), slot_info(out_codes)
    w_in, w_out = w_in[0], w_out[0]
    tokens, upstream = own_pieces(tokens, tile), own_pieces(upstream, tile)
    args = (info_in, info_out, tokens, upstream, w_in, w_out, cols, devices)
    results = on_long_row(*args) if long_row() else on_line(*args)
    layer_out, grad_tokens, grad_w_in, grad_w_out = results
    return layer_out, grad_tokens, grad_w_in[None], grad_w_out[None]


def on_line(info_in, info_out, tokens, upstream, w_in, w_out, cols, devices):
    slots = w_in.shape[0]
    ends = (0, 3)
    both = line_gather(jnp.stack([tokens, upstream]))
    in_pair = [w_in, swap_row(after(w_in, both), 1)]
    token_even = across(jnp.stack([block[0] for block in both]))
    up_even = across(after(jnp.stack([block[1] for block in both]), token_even[1:]))
    all_tokens = with_odd(token_even)
    out_pair = [w_out, swap_row(after(w_out, in_pair[1], all_tokens), 1)]
    own, far = to_hidden(info_in, all_tokens, in_pair, cols, False, ends)
    hidden = add(own, swap_row(far, 3))
    activ = silu(hidden)
    activ_far = swap_row(activ, 3)
    all_up = with_odd(after(up_even, own))
    own, far = to_hidden(info_out, after(all_up, activ), out_pair, cols, True, ends)
    far, activ_near = swap_row(far, 3), swap_row(after(activ, own), 1)
    ends_activ = after([activ, activ_far], own)
    layer_parts = from_hidden(info_out, ends_activ, out_pair, cols, False, ends, devices)
    grad_hidden = activations(hidden, add(own, after(far, layer_parts, activ_near)))
    grad_far = swap_row(grad_hidden, 3)
    all_activ = [activ, activ_near, swap_row(after(activ_far, grad_hidden), 1), activ_far]
    layer_sums = finish_col(pair_sums(*after(layer_parts, grad_hidden)))
    ends_grad = after([grad_hidden, grad_far], all_activ[2], layer_sums)
    input_parts = from_hidden(info_in, ends_grad, in_pair, cols, True, ends, devices)
    layer_far = swap_row(layer_sums[1], 3)
    input_pairs = pair_sums(*input_parts)
    all_activ = after(all_activ, input_pairs)
    grad_w_out = slot_grads(info_out, all_up, all_activ, slots, cols, False)
    near, far = swap_row(grad_hidden, 1), swap_row(grad_far, 1)
    input_sums = finish_col(input_pairs, grad_w_out, near, far)
    all_grad = after([grad_hidden, near, far, grad_far], input_sums)
    grad_w_in = slot_grads(info_in, all_tokens, all_grad, slots, cols, True)
    input_far = after(swap_row(input_sums[1], 3), grad_w_in)
    layer_out = rows_first(add(layer_sums[0], after(layer_far, input_sums)))
    grad_tokens = rows_first(add(input_sums[0], input_far))
    return layer_out, grad_tokens, grad_w_in, grad_w_out


def on_long_row(info_in, info_out, tokens, upstream, w_in, w_out, cols, devices):
    slots, blocks = w_in.shape[0], lax.axis_size("row")

    def everywhere(x):
        return [lax.all_gather(lax.all_gather(x, "row"), "col")]

    def hidden_side(info, xs, w, flip):
        parts = jnp.stack(to_hidden(info, xs, [w], cols, flip, range(blocks)))
        return lax.psum_scatter(parts, "row", scatter_dimension=0).astype(jnp.float32)

    def wide_side(info, hs, w, flip):
        sums = []
        for chunk in chunks(blocks):
            if sums:
                hs, _ = lax.optimization_barrier((hs, sums[-1]))
            labels = range(blocks)[chunk]
            [parts] = from_hidden(info, [hs], [w], cols, flip, labels, devices)
            sums.append(lax.psum_scatter(parts, "col", scatter_dimension=0))
        total = lax.psum_scatter(jnp.concatenate(sums), "row", scatter_dimension=0)
        return rows_first(total)

    hidden = hidden_side(info_in, everywhere(tokens), w_in, False)
    upstream, hidden = lax.optimization_barrier((upstream, hidden))
    all_up = everywhere(upstream)
    grad_activ = hidden_side(info_out, all_up, w_out, True)
    all_activ = lax.all_gather(silu(hidden), "row")
    layer_out = wide_side(info_out, all_activ, w_out, False)
    grad_w_out = slot_grads(info_out, all_up, [all_activ], slots, cols, False)
    held = (activations(hidden, grad_activ), tokens, layer_out, grad_w_out)
    grad_hidden, tokens, layer_out, grad_w_out = lax.optimization_barrier(held)
    all_grad = lax.all_gather(grad_hidden, "row")
    grad_tokens = wide_side(info_in, all_grad, w_in, True)
    grad_w_in = slot_grads(info_in, everywhere(tokens), [all_grad], slots, cols, True)
    return layer_out, grad_tokens, grad_w_in, grad_w_out


def solution(mesh):
    placed = (
        P("row", "col"),
        P("row", "col"),
        P("col", "row", None, None),
        P("col", None),
        P("col", "row", None, None),
        P("col", None),
    )
    return jax.shard_map(
        per_device,
        mesh=mesh,
        in_specs=placed,
        out_specs=(
            P("row", "col"),
            P("row", "col"),
            P("col", "row", None, None),
            P("col", "row", None, None),
        ),
        check_vma=False,
    )
```

```python
import functools

import jax
import jax.numpy as jnp
from jax import lax
from jax.experimental import pallas as pl
from jax.experimental.pallas import tpu as pltpu
from jax.sharding import PartitionSpec as P

D = 4096
FF = 16384
VMEM = 56 * 1024 * 1024
GROUP = 4
ANY = pl.BlockSpec(memory_space=pl.ANY)


def matmul(a, b, a_dim, b_dim):
    return lax.dot_general(
        a, b, (((a_dim,), (b_dim,)), ((), ())), preferred_element_type=jnp.float32
    )


def flat(block):
    return block.reshape(block.shape[0] * block.shape[1], block.shape[2])


def chunks(blocks):
    group = min(blocks, GROUP)
    return [slice(at, at + group) for at in range(0, blocks, group)]


def tile_part(held, owner, q, pieces, unit):
    tile = held.shape[-1]
    if unit == tile:
        return owner * pieces + q, slice(None)
    parts = tile // unit
    lane = pl.multiple_of(lax.rem(owner, parts) * unit, unit)
    return lax.div(owner, parts), pl.ds(lane, unit)


def wide_copies(refs, labels, held, sems, col):
    copies = []
    if len(refs) == 1:
        pairs = [(m, refs[0].at[m]) for m in range(refs[0].shape[0])]
    else:
        pairs = [(lax.bitwise_xor(col, m), ref) for m, ref in enumerate(refs)]
    for owner, ref in pairs:
        blocks, pieces, _, unit = ref.shape
        whole = len(labels) == blocks
        for q in range(pieces):
            tile, lanes = tile_part(held, owner, q, pieces, unit)
            for g, t in [(slice(None), slice(None))] if whole else enumerate(labels):
                target = held.at[tile, g, :, lanes]
                copies.append(pltpu.make_async_copy(ref.at[t, q], target, sems.at[len(copies)]))
                copies[-1].start()
    return copies


def hidden_copies(refs, labels, held, sems, row):
    copies = []
    for g, t in enumerate(labels):
        source = refs[g] if len(refs) > 1 else refs[0].at[lax.bitwise_xor(row, t)]
        copies.append(pltpu.make_async_copy(source, held.at[:, g], sems.at[g]))
        copies[-1].start()
    return copies


def over_slots(info, first, slots, cols, body):
    step = 4 if slots % 4 == 0 else 1

    def some(at, carry):
        for s in [at * step + i for i in range(step)]:
            code = info[2 + first + s]
            tile = jnp.maximum(code, 0)
            body(s, code >= 0, lax.div(tile, cols), lax.rem(tile, cols))
        return carry

    lax.fori_loop(0, slots // step, some, 0)


def to_hidden_kernel(cols, flip, labels, wides, weights, info, *refs):
    w_refs, x_refs, refs = refs[:weights], refs[weights:weights + wides], refs[weights + wides:]
    *outs, x, acc, sems = refs
    copies = wide_copies(x_refs, labels, x, sems, info[1])
    acc[...] = jnp.zeros_like(acc)
    for copy in copies:
        copy.wait()

    for at, w_ref in enumerate(w_refs):
        def add(s, filled, wide, hidden, w_ref=w_ref):
            target = jnp.where(filled, hidden, acc.shape[0] - 1)
            for chunk in chunks(x.shape[1]):
                product = matmul(flat(x[wide, chunk]), w_ref[s], 1, 1 if flip else 0)
                acc[target, chunk] += product.reshape(-1, *acc.shape[2:])

        over_slots(info, at * w_ref.shape[0], w_ref.shape[0], cols, add)
    for part, out in enumerate(outs):
        out[...] = acc[:out.shape[0], part].astype(out.dtype)


def from_hidden_kernel(cols, flip, labels, hiddens, weights, info, *refs):
    w_refs, h_refs = refs[:weights], refs[weights:weights + hiddens]
    *outs, h, acc, sems = refs[weights + hiddens:]
    copies = hidden_copies(h_refs, labels, h, sems, info[0])
    acc[...] = jnp.zeros_like(acc)
    for copy in copies:
        copy.wait()

    for at, w_ref in enumerate(w_refs):
        def add(s, filled, wide, hidden, w_ref=w_ref):
            target = jnp.where(filled, wide, acc.shape[0] - 1)
            for chunk in chunks(h.shape[1]):
                product = matmul(flat(h[hidden, chunk]), w_ref[s], 1, 1 if flip else 0)
                acc[target, chunk] += product.reshape(-1, *acc.shape[2:])

        over_slots(info, at * w_ref.shape[0], w_ref.shape[0], cols, add)
    for at, out in enumerate(outs):
        pieces, unit = out.shape[-3], out.shape[-1]
        for m in range(out.shape[0]):
            owner = m if len(outs) == 1 else lax.bitwise_xor(info[1], 2 * m + at)
            for q in range(pieces):
                tile, lanes = tile_part(acc, owner, q, pieces, unit)
                out[m, :, q] = acc[tile, :, :, lanes].astype(out.dtype)


def grad_kernel(cols, flip, wides, labels, info, *refs):
    x_refs, h_refs = refs[:wides], refs[wides:-5]
    out, x, h, x_sems, h_sems = refs[-5:]
    copies = wide_copies(x_refs, labels, x, x_sems, info[1])
    copies += hidden_copies(h_refs, labels, h, h_sems, info[0])
    for copy in copies:
        copy.wait()

    def add(s, filled, wide, hidden):
        total = 0.0
        for chunk in chunks(x.shape[1]):
            a, b = flat(x[wide, chunk]), flat(h[hidden, chunk])
            a, b = (a, b) if flip else (b, a)
            total += matmul(a, b, 0, 0)
        out[s] = jnp.where(filled, total, 0.0).astype(out.dtype)

    over_slots(info, 0, out.shape[0], cols, add)


def call(kernel, out_shape, scratch, flops, moved, *args):
    return pl.pallas_call(
        kernel,
        out_shape=out_shape,
        in_specs=[pl.BlockSpec(memory_space=pltpu.SMEM)] + args[1],
        out_specs=jax.tree.map(lambda _: pl.BlockSpec(memory_space=pltpu.VMEM), out_shape),
        scratch_shapes=scratch,
        compiler_params=pltpu.CompilerParams(vmem_limit_bytes=VMEM),
        cost_estimate=pl.CostEstimate(flops=flops, bytes_accessed=moved, transcendentals=0),
    )(args[0], *args[2])


def wide_scratch(labels, rows, tile, unit):
    group = len(labels)
    held = pltpu.VMEM((D // tile, group, rows, tile), jnp.bfloat16)
    return [held, pltpu.SemaphoreType.DMA((D // unit * group,))]


def to_hidden(info, xs, ws, cols, flip, labels):
    rows, unit = xs[0].shape[-2:]
    slots, tile, _ = ws[0].shape
    group = len(labels)
    outs = [jax.ShapeDtypeStruct((cols, rows, tile), jnp.bfloat16)] * group
    held, sems = wide_scratch(labels, rows, tile, unit)
    scratch = [held, pltpu.VMEM((cols + 1, group, rows, tile), jnp.float32), sems]
    kernel = functools.partial(to_hidden_kernel, cols, flip, labels, len(xs), len(ws))
    specs = [pl.BlockSpec(memory_space=pltpu.VMEM)] * len(ws) + [ANY] * len(xs)
    flops = 2 * len(ws) * slots * group * rows * tile * tile
    return call(kernel, outs, scratch, flops, 8 << 20, info, specs, [*ws, *xs])


def from_hidden(info, hs, ws, cols, flip, labels, devices):
    rows, tile = hs[0].shape[-2:]
    slots, group = ws[0].shape[0], len(labels)
    unit = min(tile, D // devices)
    pieces = D // devices // unit
    shape = (group, pieces, rows, unit)
    if long_row():
        outs = [jax.ShapeDtypeStruct((devices, *shape), jnp.bfloat16)]
    else:
        outs = [jax.ShapeDtypeStruct((devices // 2, *shape), jnp.bfloat16)] * 2
    scratch = [
        pltpu.VMEM((cols, group, rows, tile), jnp.bfloat16),
        pltpu.VMEM((D // tile + 1, group, rows, tile), jnp.float32),
        pltpu.SemaphoreType.DMA((group,)),
    ]
    kernel = functools.partial(from_hidden_kernel, cols, flip, labels, len(hs), len(ws))
    specs = [pl.BlockSpec(memory_space=pltpu.VMEM)] * len(ws) + [ANY] * len(hs)
    flops = 2 * len(ws) * slots * group * rows * tile * tile
    return call(kernel, outs, scratch, flops, 8 << 20, info, specs, [*ws, *hs])


def slot_grads(info, xs, hs, slots, cols, flip):
    blocks = lax.axis_size("row")
    labels = range(blocks)
    rows, unit = xs[0].shape[-2:]
    tile = hs[0].shape[-1]
    out = jax.ShapeDtypeStruct((slots, tile, tile), jnp.bfloat16)
    held, sems = wide_scratch(labels, rows, tile, unit)
    scratch = [
        held,
        pltpu.VMEM((cols, blocks, rows, tile), jnp.bfloat16),
        sems,
        pltpu.SemaphoreType.DMA((blocks,)),
    ]
    kernel = functools.partial(grad_kernel, cols, flip, len(xs), labels)
    specs = [ANY] * (len(xs) + len(hs))
    flops = 2 * slots * blocks * rows * tile * tile
    return call(kernel, out, scratch, flops, 8 << 20, info, specs, [*xs, *hs])


def long_row():
    return lax.axis_size("row") != 4


def swap_col(x, m):
    count = lax.axis_size("col")
    return lax.ppermute(x, "col", [(s, s ^ m) for s in range(count)])


def swap_row(x, t):
    return lax.ppermute(x, "row", [(s, s ^ t) for s in range(4)])


def own_pieces(x, tile):
    rows, width = x.shape
    unit = min(width, tile)
    return jnp.swapaxes(x.reshape(rows, width // unit, unit), 0, 1)


def after(values, *others):
    return lax.optimization_barrier((values, others))[0]


def across(mine):
    return [swap_col(mine, m) if m else mine for m in range(0, lax.axis_size("col"), 2)]


def with_odd(even):
    return [x for own in even for x in (own, swap_col(own, 1))]


def add(*terms):
    return sum(term.astype(jnp.float32) for term in terms)


def line_gather(x):
    return [x] + [swap_row(x, t) for t in range(1, 4)]


def pair_sums(even, odd):
    return add(even, swap_col(odd, 1)).astype(jnp.bfloat16)


def finish_col(pairs, *wait):
    sums = [pairs[0]] + [swap_col(pairs[m], 2 * m) for m in range(1, pairs.shape[0])]
    return add(*after(sums, *wait)).astype(jnp.bfloat16)


def rows_first(total):
    return jnp.swapaxes(total, 0, 1).reshape(total.shape[1], -1).astype(jnp.bfloat16)


def activations(hidden, grad_activ):
    sigmoid = jax.nn.sigmoid(hidden)
    slope = sigmoid * (1.0 + hidden * (1.0 - sigmoid))
    return (grad_activ * slope).astype(jnp.bfloat16)


def silu(hidden):
    return (hidden * jax.nn.sigmoid(hidden)).astype(jnp.bfloat16)


def per_device(tokens, upstream, w_in, in_codes, w_out, out_codes):
    tile = w_in.shape[3]
    slots = w_in.shape[1]
    devices = lax.axis_size("col")
    cols = FF // (tile * devices)
    row, col = lax.axis_index("row"), lax.axis_index("col")

    def slot_info(codes):
        own = lax.dynamic_slice_in_dim(codes[0], row * slots, slots)
        mate = lax.dynamic_slice_in_dim(codes[0], (row ^ 1) * slots, slots)
        place = jnp.stack([row, col]).astype(jnp.int32)
        return jnp.concatenate([place, own, mate])

    info_in, info_out = slot_info(in_codes), slot_info(out_codes)
    w_in, w_out = w_in[0], w_out[0]
    tokens, upstream = own_pieces(tokens, tile), own_pieces(upstream, tile)
    args = (info_in, info_out, tokens, upstream, w_in, w_out, cols, devices)
    results = on_long_row(*args) if long_row() else on_line(*args)
    layer_out, grad_tokens, grad_w_in, grad_w_out = results
    return layer_out, grad_tokens, grad_w_in[None], grad_w_out[None]


def on_line(info_in, info_out, tokens, upstream, w_in, w_out, cols, devices):
    slots = w_in.shape[0]
    ends = (0, 3)
    mine = jnp.stack([tokens, upstream])
    both = line_gather(mine)
    in_pair = [w_in, swap_row(after(w_in, mine), 1)]
    token_even = across(jnp.stack([block[0] for block in both]))
    up_even = across(after(jnp.stack([block[1] for block in both]), token_even[1:]))
    all_tokens = with_odd(token_even)
    out_pair = [w_out, swap_row(after(w_out, all_tokens), 1)]
    own, far = to_hidden(info_in, all_tokens, in_pair, cols, False, ends)
    hidden = add(own, swap_row(far, 3))
    activ = silu(hidden)
    activ_far = swap_row(activ, 3)
    all_up = with_odd(after(up_even, own))
    own, far = to_hidden(info_out, after(all_up, activ), out_pair, cols, True, ends)
    far = swap_row(far, 3)
    ends_activ = after([activ, activ_far], own)
    layer_parts = from_hidden(info_out, ends_activ, out_pair, cols, False, ends, devices)
    grad_hidden = activations(hidden, add(own, after(far, layer_parts)))
    grad_far = swap_row(grad_hidden, 3)
    activ, activ_far = after((activ, activ_far), grad_hidden)
    all_activ = [activ, swap_row(activ, 1), swap_row(activ_far, 1), activ_far]
    layer_sums = finish_col(pair_sums(*after(layer_parts, grad_hidden)))
    ends_grad = after([grad_hidden, grad_far], layer_sums)
    input_parts = from_hidden(info_in, ends_grad, in_pair, cols, True, ends, devices)
    layer_far = swap_row(layer_sums[1], 3)
    input_pairs = pair_sums(*input_parts)
    all_activ = after(all_activ, input_pairs)
    grad_w_out = slot_grads(info_out, all_up, all_activ, slots, cols, False)
    near, far = swap_row(grad_hidden, 1), swap_row(grad_far, 1)
    input_sums = finish_col(input_pairs, grad_w_out)
    all_grad = after([grad_hidden, near, far, grad_far], input_sums)
    grad_w_in = slot_grads(info_in, all_tokens, all_grad, slots, cols, True)
    input_far = after(swap_row(input_sums[1], 3), grad_w_in)
    layer_out = rows_first(add(layer_sums[0], after(layer_far, input_sums)))
    grad_tokens = rows_first(add(input_sums[0], input_far))
    return layer_out, grad_tokens, grad_w_in, grad_w_out


def on_long_row(info_in, info_out, tokens, upstream, w_in, w_out, cols, devices):
    slots, blocks = w_in.shape[0], lax.axis_size("row")

    def everywhere(x):
        return [lax.all_gather(lax.all_gather(x, "row"), "col")]

    def hidden_side(info, xs, w, flip):
        parts = jnp.stack(to_hidden(info, xs, [w], cols, flip, range(blocks)))
        return lax.psum_scatter(parts, "row", scatter_dimension=0).astype(jnp.float32)

    def wide_side(info, hs, w, flip):
        sums = []
        for chunk in chunks(blocks):
            if sums:
                hs, _ = lax.optimization_barrier((hs, sums[-1]))
            labels = range(blocks)[chunk]
            [parts] = from_hidden(info, [hs], [w], cols, flip, labels, devices)
            sums.append(lax.psum_scatter(parts, "col", scatter_dimension=0))
        total = lax.psum_scatter(jnp.concatenate(sums), "row", scatter_dimension=0)
        return rows_first(total)

    hidden = hidden_side(info_in, everywhere(tokens), w_in, False)
    upstream, hidden = lax.optimization_barrier((upstream, hidden))
    all_up = everywhere(upstream)
    grad_activ = hidden_side(info_out, all_up, w_out, True)
    all_activ = lax.all_gather(silu(hidden), "row")
    layer_out = wide_side(info_out, all_activ, w_out, False)
    grad_w_out = slot_grads(info_out, all_up, [all_activ], slots, cols, False)
    held = (activations(hidden, grad_activ), tokens, layer_out, grad_w_out)
    grad_hidden, tokens, layer_out, grad_w_out = lax.optimization_barrier(held)
    all_grad = lax.all_gather(grad_hidden, "row")
    grad_tokens = wide_side(info_in, all_grad, w_in, True)
    grad_w_in = slot_grads(info_in, everywhere(tokens), [all_grad], slots, cols, True)
    return layer_out, grad_tokens, grad_w_in, grad_w_out


def solution(mesh):
    placed = (
        P("row", "col"),
        P("row", "col"),
        P("col", "row", None, None),
        P("col", None),
        P("col", "row", None, None),
        P("col", None),
    )
    return jax.shard_map(
        per_device,
        mesh=mesh,
        in_specs=placed,
        out_specs=(
            P("row", "col"),
            P("row", "col"),
            P("col", "row", None, None),
            P("col", "row", None, None),
        ),
        check_vma=False,
    )
```

```python
import functools

import jax
import jax.numpy as jnp
from jax import lax
from jax.experimental import pallas as pl
from jax.experimental.pallas import tpu as pltpu
from jax.sharding import PartitionSpec as P

D = 4096
FF = 16384
VMEM = 56 * 1024 * 1024
GROUP = 4
ANY = pl.BlockSpec(memory_space=pl.ANY)


def matmul(a, b, a_dim, b_dim):
    return lax.dot_general(
        a, b, (((a_dim,), (b_dim,)), ((), ())), preferred_element_type=jnp.float32
    )


def flat(block):
    return block.reshape(block.shape[0] * block.shape[1], block.shape[2])


def chunks(blocks):
    group = min(blocks, GROUP)
    return [slice(at, at + group) for at in range(0, blocks, group)]


def tile_part(held, owner, q, pieces, unit):
    tile = held.shape[-1]
    if unit == tile:
        return owner * pieces + q, slice(None)
    parts = tile // unit
    lane = pl.multiple_of(lax.rem(owner, parts) * unit, unit)
    return lax.div(owner, parts), pl.ds(lane, unit)


def wide_copies(refs, labels, held, sems, col):
    copies = []
    if len(refs) == 1:
        pairs = [(m, refs[0].at[m]) for m in range(refs[0].shape[0])]
    else:
        pairs = [(lax.bitwise_xor(col, m), ref) for m, ref in enumerate(refs)]
    for owner, ref in pairs:
        blocks, pieces, _, unit = ref.shape
        whole = len(labels) == blocks
        for q in range(pieces):
            tile, lanes = tile_part(held, owner, q, pieces, unit)
            for g, t in [(slice(None), slice(None))] if whole else enumerate(labels):
                target = held.at[tile, g, :, lanes]
                copies.append(pltpu.make_async_copy(ref.at[t, q], target, sems.at[len(copies)]))
                copies[-1].start()
    return copies


def hidden_copies(refs, labels, held, sems, row):
    copies = []
    for g, t in enumerate(labels):
        source = refs[g] if len(refs) > 1 else refs[0].at[lax.bitwise_xor(row, t)]
        copies.append(pltpu.make_async_copy(source, held.at[:, g], sems.at[g]))
        copies[-1].start()
    return copies


def over_slots(info, first, slots, cols, body):
    step = 4 if slots % 4 == 0 else 1

    def some(at, carry):
        for s in [at * step + i for i in range(step)]:
            code = info[2 + first + s]
            tile = jnp.maximum(code, 0)
            body(s, code >= 0, lax.div(tile, cols), lax.rem(tile, cols))
        return carry

    lax.fori_loop(0, slots // step, some, 0)


def to_hidden_kernel(cols, flip, labels, wides, weights, info, *refs):
    w_refs, x_refs, refs = refs[:weights], refs[weights:weights + wides], refs[weights + wides:]
    *outs, x, acc, sems = refs
    copies = wide_copies(x_refs, labels, x, sems, info[1])
    acc[...] = jnp.zeros_like(acc)
    for copy in copies:
        copy.wait()

    for at, w_ref in enumerate(w_refs):
        def add(s, filled, wide, hidden, w_ref=w_ref):
            target = jnp.where(filled, hidden, acc.shape[0] - 1)
            for chunk in chunks(x.shape[1]):
                product = matmul(flat(x[wide, chunk]), w_ref[s], 1, 1 if flip else 0)
                acc[target, chunk] += product.reshape(-1, *acc.shape[2:])

        over_slots(info, at * w_ref.shape[0], w_ref.shape[0], cols, add)
    for part, out in enumerate(outs):
        out[...] = acc[:out.shape[0], part].astype(out.dtype)


def from_hidden_kernel(cols, flip, labels, hiddens, weights, info, *refs):
    w_refs, h_refs = refs[:weights], refs[weights:weights + hiddens]
    *outs, h, acc, sems = refs[weights + hiddens:]
    copies = hidden_copies(h_refs, labels, h, sems, info[0])
    acc[...] = jnp.zeros_like(acc)
    for copy in copies:
        copy.wait()

    for at, w_ref in enumerate(w_refs):
        def add(s, filled, wide, hidden, w_ref=w_ref):
            target = jnp.where(filled, wide, acc.shape[0] - 1)
            for chunk in chunks(h.shape[1]):
                product = matmul(flat(h[hidden, chunk]), w_ref[s], 1, 1 if flip else 0)
                acc[target, chunk] += product.reshape(-1, *acc.shape[2:])

        over_slots(info, at * w_ref.shape[0], w_ref.shape[0], cols, add)
    for at, out in enumerate(outs):
        pieces, unit = out.shape[-3], out.shape[-1]
        for m in range(out.shape[0]):
            owner = m if len(outs) == 1 else lax.bitwise_xor(info[1], 2 * m + at)
            for q in range(pieces):
                tile, lanes = tile_part(acc, owner, q, pieces, unit)
                out[m, :, q] = acc[tile, :, :, lanes].astype(out.dtype)


def grad_kernel(cols, flip, wides, labels, info, *refs):
    x_refs, h_refs = refs[:wides], refs[wides:-5]
    out, x, h, x_sems, h_sems = refs[-5:]
    copies = wide_copies(x_refs, labels, x, x_sems, info[1])
    copies += hidden_copies(h_refs, labels, h, h_sems, info[0])
    for copy in copies:
        copy.wait()

    def add(s, filled, wide, hidden):
        total = 0.0
        for chunk in chunks(x.shape[1]):
            a, b = flat(x[wide, chunk]), flat(h[hidden, chunk])
            a, b = (a, b) if flip else (b, a)
            total += matmul(a, b, 0, 0)
        out[s] = jnp.where(filled, total, 0.0).astype(out.dtype)

    over_slots(info, 0, out.shape[0], cols, add)


def call(kernel, out_shape, scratch, flops, moved, *args):
    return pl.pallas_call(
        kernel,
        out_shape=out_shape,
        in_specs=[pl.BlockSpec(memory_space=pltpu.SMEM)] + args[1],
        out_specs=jax.tree.map(lambda _: pl.BlockSpec(memory_space=pltpu.VMEM), out_shape),
        scratch_shapes=scratch,
        compiler_params=pltpu.CompilerParams(vmem_limit_bytes=VMEM),
        cost_estimate=pl.CostEstimate(flops=flops, bytes_accessed=moved, transcendentals=0),
    )(args[0], *args[2])


def wide_scratch(labels, rows, tile, unit):
    group = len(labels)
    held = pltpu.VMEM((D // tile, group, rows, tile), jnp.bfloat16)
    return [held, pltpu.SemaphoreType.DMA((D // unit * group,))]


def to_hidden(info, xs, ws, cols, flip, labels):
    rows, unit = xs[0].shape[-2:]
    slots, tile, _ = ws[0].shape
    group = len(labels)
    outs = [jax.ShapeDtypeStruct((cols, rows, tile), jnp.bfloat16)] * group
    held, sems = wide_scratch(labels, rows, tile, unit)
    scratch = [held, pltpu.VMEM((cols + 1, group, rows, tile), jnp.float32), sems]
    kernel = functools.partial(to_hidden_kernel, cols, flip, labels, len(xs), len(ws))
    specs = [pl.BlockSpec(memory_space=pltpu.VMEM)] * len(ws) + [ANY] * len(xs)
    flops = 2 * len(ws) * slots * group * rows * tile * tile
    return call(kernel, outs, scratch, flops, 8 << 20, info, specs, [*ws, *xs])


def from_hidden(info, hs, ws, cols, flip, labels, devices):
    rows, tile = hs[0].shape[-2:]
    slots, group = ws[0].shape[0], len(labels)
    unit = min(tile, D // devices)
    pieces = D // devices // unit
    shape = (group, pieces, rows, unit)
    if long_row():
        outs = [jax.ShapeDtypeStruct((devices, *shape), jnp.bfloat16)]
    else:
        outs = [jax.ShapeDtypeStruct((devices // 2, *shape), jnp.bfloat16)] * 2
    scratch = [
        pltpu.VMEM((cols, group, rows, tile), jnp.bfloat16),
        pltpu.VMEM((D // tile + 1, group, rows, tile), jnp.float32),
        pltpu.SemaphoreType.DMA((group,)),
    ]
    kernel = functools.partial(from_hidden_kernel, cols, flip, labels, len(hs), len(ws))
    specs = [pl.BlockSpec(memory_space=pltpu.VMEM)] * len(ws) + [ANY] * len(hs)
    flops = 2 * len(ws) * slots * group * rows * tile * tile
    return call(kernel, outs, scratch, flops, 8 << 20, info, specs, [*ws, *hs])


def slot_grads(info, xs, hs, slots, cols, flip):
    blocks = lax.axis_size("row")
    labels = range(blocks)
    rows, unit = xs[0].shape[-2:]
    tile = hs[0].shape[-1]
    out = jax.ShapeDtypeStruct((slots, tile, tile), jnp.bfloat16)
    held, sems = wide_scratch(labels, rows, tile, unit)
    scratch = [
        held,
        pltpu.VMEM((cols, blocks, rows, tile), jnp.bfloat16),
        sems,
        pltpu.SemaphoreType.DMA((blocks,)),
    ]
    kernel = functools.partial(grad_kernel, cols, flip, len(xs), labels)
    specs = [ANY] * (len(xs) + len(hs))
    flops = 2 * slots * blocks * rows * tile * tile
    return call(kernel, out, scratch, flops, 8 << 20, info, specs, [*xs, *hs])


def long_row():
    return lax.axis_size("row") != 4


def swap_col(x, m):
    count = lax.axis_size("col")
    return lax.ppermute(x, "col", [(s, s ^ m) for s in range(count)])


def swap_row(x, t):
    return lax.ppermute(x, "row", [(s, s ^ t) for s in range(4)])


def own_pieces(x, tile):
    rows, width = x.shape
    unit = min(width, tile)
    return jnp.swapaxes(x.reshape(rows, width // unit, unit), 0, 1)


def after(values, *others):
    return lax.optimization_barrier((values, others))[0]


def across(mine):
    return [swap_col(mine, m) if m else mine for m in range(0, lax.axis_size("col"), 2)]


def with_odd(even):
    return [x for own in even for x in (own, swap_col(own, 1))]


def add(*terms):
    return sum(term.astype(jnp.float32) for term in terms)


def line_gather(x):
    return [x] + [swap_row(x, t) for t in range(1, 4)]


def pair_sums(even, odd):
    return add(even, swap_col(odd, 1)).astype(jnp.bfloat16)


def finish_col(pairs, *wait):
    sums = [pairs[0]] + [swap_col(pairs[m], 2 * m) for m in range(1, pairs.shape[0])]
    return add(*after(sums, *wait)).astype(jnp.bfloat16)


def rows_first(total):
    return jnp.swapaxes(total, 0, 1).reshape(total.shape[1], -1).astype(jnp.bfloat16)


def activations(hidden, grad_activ):
    sigmoid = jax.nn.sigmoid(hidden)
    slope = sigmoid * (1.0 + hidden * (1.0 - sigmoid))
    return (grad_activ * slope).astype(jnp.bfloat16)


def silu(hidden):
    return (hidden * jax.nn.sigmoid(hidden)).astype(jnp.bfloat16)


def per_device(tokens, upstream, w_in, in_codes, w_out, out_codes):
    tile = w_in.shape[3]
    slots = w_in.shape[1]
    devices = lax.axis_size("col")
    cols = FF // (tile * devices)
    row, col = lax.axis_index("row"), lax.axis_index("col")

    def slot_info(codes):
        own = lax.dynamic_slice_in_dim(codes[0], row * slots, slots)
        mate = lax.dynamic_slice_in_dim(codes[0], (row ^ 1) * slots, slots)
        place = jnp.stack([row, col]).astype(jnp.int32)
        return jnp.concatenate([place, own, mate])

    info_in, info_out = slot_info(in_codes), slot_info(out_codes)
    w_in, w_out = w_in[0], w_out[0]
    tokens, upstream = own_pieces(tokens, tile), own_pieces(upstream, tile)
    args = (info_in, info_out, tokens, upstream, w_in, w_out, cols, devices)
    results = on_long_row(*args) if long_row() else on_line(*args)
    layer_out, grad_tokens, grad_w_in, grad_w_out = results
    return layer_out, grad_tokens, grad_w_in[None], grad_w_out[None]


def on_line(info_in, info_out, tokens, upstream, w_in, w_out, cols, devices):
    slots = w_in.shape[0]
    ends = (0, 3)
    mine = jnp.stack([tokens, upstream])
    both = line_gather(mine)
    in_pair = [w_in, swap_row(after(w_in, mine), 1)]
    token_even = across(jnp.stack([block[0] for block in both]))
    up_even = across(after(jnp.stack([block[1] for block in both]), token_even[1:]))
    all_tokens = with_odd(token_even)
    out_pair = [w_out, swap_row(after(w_out, all_tokens), 1)]
    own, far = to_hidden(info_in, all_tokens, in_pair, cols, False, ends)
    hidden = add(own, swap_row(far, 3))
    activ = silu(hidden)
    activ_far = swap_row(activ, 3)
    all_up = with_odd(after(up_even, own))
    own, far = to_hidden(info_out, after(all_up, activ), out_pair, cols, True, ends)
    far = swap_row(far, 3)
    ends_activ = after([activ, activ_far], own)
    layer_parts = from_hidden(info_out, ends_activ, out_pair, cols, False, ends, devices)
    grad_hidden = activations(hidden, add(own, after(far, layer_parts)))
    grad_far = swap_row(grad_hidden, 3)
    activ, activ_far = after((activ, activ_far), grad_hidden)
    all_activ = [activ, swap_row(activ, 1), swap_row(activ_far, 1), activ_far]
    layer_sums = finish_col(pair_sums(*after(layer_parts, grad_hidden)))
    ends_grad = after([grad_hidden, grad_far], layer_sums, all_activ[1])
    input_parts = from_hidden(info_in, ends_grad, in_pair, cols, True, ends, devices)
    layer_far = swap_row(layer_sums[1], 3)
    input_pairs = pair_sums(*input_parts)
    all_activ = after(all_activ, input_pairs)
    grad_w_out = slot_grads(info_out, all_up, all_activ, slots, cols, False)
    near, far = swap_row(grad_hidden, 1), swap_row(grad_far, 1)
    input_sums = finish_col(input_pairs, grad_w_out, near, far)
    all_grad = after([grad_hidden, near, far, grad_far], input_sums)
    grad_w_in = slot_grads(info_in, all_tokens, all_grad, slots, cols, True)
    input_far = after(swap_row(input_sums[1], 3), grad_w_in)
    layer_out = rows_first(add(layer_sums[0], after(layer_far, input_sums)))
    grad_tokens = rows_first(add(input_sums[0], input_far))
    return layer_out, grad_tokens, grad_w_in, grad_w_out


def on_long_row(info_in, info_out, tokens, upstream, w_in, w_out, cols, devices):
    slots, blocks = w_in.shape[0], lax.axis_size("row")

    def everywhere(x):
        return [lax.all_gather(lax.all_gather(x, "row"), "col")]

    def hidden_side(info, xs, w, flip):
        parts = jnp.stack(to_hidden(info, xs, [w], cols, flip, range(blocks)))
        return lax.psum_scatter(parts, "row", scatter_dimension=0).astype(jnp.float32)

    def wide_side(info, hs, w, flip):
        sums = []
        for chunk in chunks(blocks):
            if sums:
                hs, _ = lax.optimization_barrier((hs, sums[-1]))
            labels = range(blocks)[chunk]
            [parts] = from_hidden(info, [hs], [w], cols, flip, labels, devices)
            sums.append(lax.psum_scatter(parts, "col", scatter_dimension=0))
        total = lax.psum_scatter(jnp.concatenate(sums), "row", scatter_dimension=0)
        return rows_first(total)

    hidden = hidden_side(info_in, everywhere(tokens), w_in, False)
    upstream, hidden = lax.optimization_barrier((upstream, hidden))
    all_up = everywhere(upstream)
    grad_activ = hidden_side(info_out, all_up, w_out, True)
    all_activ = lax.all_gather(silu(hidden), "row")
    layer_out = wide_side(info_out, all_activ, w_out, False)
    grad_w_out = slot_grads(info_out, all_up, [all_activ], slots, cols, False)
    held = (activations(hidden, grad_activ), tokens, layer_out, grad_w_out)
    grad_hidden, tokens, layer_out, grad_w_out = lax.optimization_barrier(held)
    all_grad = lax.all_gather(grad_hidden, "row")
    grad_tokens = wide_side(info_in, all_grad, w_in, True)
    grad_w_in = slot_grads(info_in, everywhere(tokens), [all_grad], slots, cols, True)
    return layer_out, grad_tokens, grad_w_in, grad_w_out


def solution(mesh):
    placed = (
        P("row", "col"),
        P("row", "col"),
        P("col", "row", None, None),
        P("col", None),
        P("col", "row", None, None),
        P("col", None),
    )
    return jax.shard_map(
        per_device,
        mesh=mesh,
        in_specs=placed,
        out_specs=(
            P("row", "col"),
            P("row", "col"),
            P("col", "row", None, None),
            P("col", "row", None, None),
        ),
        check_vma=False,
    )
```

```python
import functools

import jax
import jax.numpy as jnp
from jax import lax
from jax.experimental import pallas as pl
from jax.experimental.pallas import tpu as pltpu
from jax.sharding import PartitionSpec as P

D = 4096
FF = 16384
VMEM = 56 * 1024 * 1024
GROUP = 4
ANY = pl.BlockSpec(memory_space=pl.ANY)


def matmul(a, b, a_dim, b_dim):
    return lax.dot_general(
        a, b, (((a_dim,), (b_dim,)), ((), ())), preferred_element_type=jnp.float32
    )


def flat(block):
    return block.reshape(block.shape[0] * block.shape[1], block.shape[2])


def chunks(blocks):
    group = min(blocks, GROUP)
    return [slice(at, at + group) for at in range(0, blocks, group)]


def tile_part(held, owner, q, pieces, unit):
    tile = held.shape[-1]
    if unit == tile:
        return owner * pieces + q, slice(None)
    parts = tile // unit
    lane = pl.multiple_of(lax.rem(owner, parts) * unit, unit)
    return lax.div(owner, parts), pl.ds(lane, unit)


def wide_copies(refs, labels, held, sems, col):
    copies = []
    if len(refs) == 1:
        pairs = [(m, refs[0].at[m]) for m in range(refs[0].shape[0])]
    else:
        pairs = [(lax.bitwise_xor(col, m), ref) for m, ref in enumerate(refs)]
    for owner, ref in pairs:
        blocks, pieces, _, unit = ref.shape
        whole = len(labels) == blocks
        for q in range(pieces):
            tile, lanes = tile_part(held, owner, q, pieces, unit)
            for g, t in [(slice(None), slice(None))] if whole else enumerate(labels):
                target = held.at[tile, g, :, lanes]
                copies.append(pltpu.make_async_copy(ref.at[t, q], target, sems.at[len(copies)]))
                copies[-1].start()
    return copies


def hidden_copies(refs, labels, held, sems, row):
    copies = []
    for g, t in enumerate(labels):
        source = refs[g] if len(refs) > 1 else refs[0].at[lax.bitwise_xor(row, t)]
        copies.append(pltpu.make_async_copy(source, held.at[:, g], sems.at[g]))
        copies[-1].start()
    return copies


def over_slots(info, first, slots, cols, body):
    step = 4 if slots % 4 == 0 else 1

    def some(at, carry):
        for s in [at * step + i for i in range(step)]:
            code = info[2 + first + s]
            tile = jnp.maximum(code, 0)
            body(s, code >= 0, lax.div(tile, cols), lax.rem(tile, cols))
        return carry

    lax.fori_loop(0, slots // step, some, 0)


def to_hidden_kernel(cols, flip, labels, wides, weights, info, *refs):
    w_refs, x_refs, refs = refs[:weights], refs[weights:weights + wides], refs[weights + wides:]
    *outs, x, acc, sems = refs
    copies = wide_copies(x_refs, labels, x, sems, info[1])
    acc[...] = jnp.zeros_like(acc)
    for copy in copies:
        copy.wait()

    for at, w_ref in enumerate(w_refs):
        def add(s, filled, wide, hidden, w_ref=w_ref):
            target = jnp.where(filled, hidden, acc.shape[0] - 1)
            for chunk in chunks(x.shape[1]):
                product = matmul(flat(x[wide, chunk]), w_ref[s], 1, 1 if flip else 0)
                acc[target, chunk] += product.reshape(-1, *acc.shape[2:])

        over_slots(info, at * w_ref.shape[0], w_ref.shape[0], cols, add)
    for part, out in enumerate(outs):
        out[...] = acc[:out.shape[0], part].astype(out.dtype)


def from_hidden_kernel(cols, flip, labels, hiddens, weights, info, *refs):
    w_refs, h_refs = refs[:weights], refs[weights:weights + hiddens]
    *outs, h, acc, sems = refs[weights + hiddens:]
    copies = hidden_copies(h_refs, labels, h, sems, info[0])
    acc[...] = jnp.zeros_like(acc)
    for copy in copies:
        copy.wait()

    for at, w_ref in enumerate(w_refs):
        def add(s, filled, wide, hidden, w_ref=w_ref):
            target = jnp.where(filled, wide, acc.shape[0] - 1)
            for chunk in chunks(h.shape[1]):
                product = matmul(flat(h[hidden, chunk]), w_ref[s], 1, 1 if flip else 0)
                acc[target, chunk] += product.reshape(-1, *acc.shape[2:])

        over_slots(info, at * w_ref.shape[0], w_ref.shape[0], cols, add)
    for at, out in enumerate(outs):
        pieces, unit = out.shape[-3], out.shape[-1]
        for m in range(out.shape[0]):
            owner = m if len(outs) == 1 else lax.bitwise_xor(info[1], 2 * m + at)
            for q in range(pieces):
                tile, lanes = tile_part(acc, owner, q, pieces, unit)
                out[m, :, q] = acc[tile, :, :, lanes].astype(out.dtype)


def grad_kernel(cols, flip, wides, labels, info, *refs):
    x_refs, h_refs = refs[:wides], refs[wides:-5]
    out, x, h, x_sems, h_sems = refs[-5:]
    copies = wide_copies(x_refs, labels, x, x_sems, info[1])
    copies += hidden_copies(h_refs, labels, h, h_sems, info[0])
    for copy in copies:
        copy.wait()

    def add(s, filled, wide, hidden):
        total = 0.0
        for chunk in chunks(x.shape[1]):
            a, b = flat(x[wide, chunk]), flat(h[hidden, chunk])
            a, b = (a, b) if flip else (b, a)
            total += matmul(a, b, 0, 0)
        out[s] = jnp.where(filled, total, 0.0).astype(out.dtype)

    over_slots(info, 0, out.shape[0], cols, add)


def call(kernel, out_shape, scratch, flops, moved, *args):
    return pl.pallas_call(
        kernel,
        out_shape=out_shape,
        in_specs=[pl.BlockSpec(memory_space=pltpu.SMEM)] + args[1],
        out_specs=jax.tree.map(lambda _: pl.BlockSpec(memory_space=pltpu.VMEM), out_shape),
        scratch_shapes=scratch,
        compiler_params=pltpu.CompilerParams(vmem_limit_bytes=VMEM),
        cost_estimate=pl.CostEstimate(flops=flops, bytes_accessed=moved, transcendentals=0),
    )(args[0], *args[2])


def wide_scratch(labels, rows, tile, unit):
    group = len(labels)
    held = pltpu.VMEM((D // tile, group, rows, tile), jnp.bfloat16)
    return [held, pltpu.SemaphoreType.DMA((D // unit * group,))]


def to_hidden(info, xs, ws, cols, flip, labels):
    rows, unit = xs[0].shape[-2:]
    slots, tile, _ = ws[0].shape
    group = len(labels)
    outs = [jax.ShapeDtypeStruct((cols, rows, tile), jnp.bfloat16)] * group
    held, sems = wide_scratch(labels, rows, tile, unit)
    scratch = [held, pltpu.VMEM((cols + 1, group, rows, tile), jnp.float32), sems]
    kernel = functools.partial(to_hidden_kernel, cols, flip, labels, len(xs), len(ws))
    specs = [pl.BlockSpec(memory_space=pltpu.VMEM)] * len(ws) + [ANY] * len(xs)
    flops = 2 * len(ws) * slots * group * rows * tile * tile
    return call(kernel, outs, scratch, flops, 8 << 20, info, specs, [*ws, *xs])


def from_hidden(info, hs, ws, cols, flip, labels, devices):
    rows, tile = hs[0].shape[-2:]
    slots, group = ws[0].shape[0], len(labels)
    unit = min(tile, D // devices)
    pieces = D // devices // unit
    shape = (group, pieces, rows, unit)
    if long_row():
        outs = [jax.ShapeDtypeStruct((devices, *shape), jnp.bfloat16)]
    else:
        outs = [jax.ShapeDtypeStruct((devices // 2, *shape), jnp.bfloat16)] * 2
    scratch = [
        pltpu.VMEM((cols, group, rows, tile), jnp.bfloat16),
        pltpu.VMEM((D // tile + 1, group, rows, tile), jnp.float32),
        pltpu.SemaphoreType.DMA((group,)),
    ]
    kernel = functools.partial(from_hidden_kernel, cols, flip, labels, len(hs), len(ws))
    specs = [pl.BlockSpec(memory_space=pltpu.VMEM)] * len(ws) + [ANY] * len(hs)
    flops = 2 * len(ws) * slots * group * rows * tile * tile
    return call(kernel, outs, scratch, flops, 8 << 20, info, specs, [*ws, *hs])


def slot_grads(info, xs, hs, slots, cols, flip):
    blocks = lax.axis_size("row")
    labels = range(blocks)
    rows, unit = xs[0].shape[-2:]
    tile = hs[0].shape[-1]
    out = jax.ShapeDtypeStruct((slots, tile, tile), jnp.bfloat16)
    held, sems = wide_scratch(labels, rows, tile, unit)
    scratch = [
        held,
        pltpu.VMEM((cols, blocks, rows, tile), jnp.bfloat16),
        sems,
        pltpu.SemaphoreType.DMA((blocks,)),
    ]
    kernel = functools.partial(grad_kernel, cols, flip, len(xs), labels)
    specs = [ANY] * (len(xs) + len(hs))
    flops = 2 * slots * blocks * rows * tile * tile
    return call(kernel, out, scratch, flops, 8 << 20, info, specs, [*xs, *hs])


def long_row():
    return lax.axis_size("row") != 4


def swap_col(x, m):
    count = lax.axis_size("col")
    return lax.ppermute(x, "col", [(s, s ^ m) for s in range(count)])


def swap_row(x, t):
    return lax.ppermute(x, "row", [(s, s ^ t) for s in range(4)])


def own_pieces(x, tile):
    rows, width = x.shape
    unit = min(width, tile)
    return jnp.swapaxes(x.reshape(rows, width // unit, unit), 0, 1)


def after(values, *others):
    return lax.optimization_barrier((values, others))[0]


def across(mine):
    return [swap_col(mine, m) if m else mine for m in range(0, lax.axis_size("col"), 2)]


def with_odd(even):
    return [x for own in even for x in (own, swap_col(own, 1))]


def add(*terms):
    return sum(term.astype(jnp.float32) for term in terms)


def line_gather(x):
    return [x] + [swap_row(x, t) for t in range(1, 4)]


def pair_sums(even, odd):
    return add(even, swap_col(odd, 1)).astype(jnp.bfloat16)


def col_terms(pairs):
    return [pairs[0]] + [swap_col(pairs[m], 2 * m) for m in range(1, pairs.shape[0])]


def rows_first(total):
    return jnp.swapaxes(total, 0, 1).reshape(total.shape[1], -1).astype(jnp.bfloat16)


def activations(hidden, grad_activ):
    sigmoid = jax.nn.sigmoid(hidden)
    slope = sigmoid * (1.0 + hidden * (1.0 - sigmoid))
    return (grad_activ * slope).astype(jnp.bfloat16)


def silu(hidden):
    return (hidden * jax.nn.sigmoid(hidden)).astype(jnp.bfloat16)


def per_device(tokens, upstream, w_in, in_codes, w_out, out_codes):
    tile = w_in.shape[3]
    slots = w_in.shape[1]
    devices = lax.axis_size("col")
    cols = FF // (tile * devices)
    row, col = lax.axis_index("row"), lax.axis_index("col")

    def slot_info(codes):
        own = lax.dynamic_slice_in_dim(codes[0], row * slots, slots)
        mate = lax.dynamic_slice_in_dim(codes[0], (row ^ 1) * slots, slots)
        place = jnp.stack([row, col]).astype(jnp.int32)
        return jnp.concatenate([place, own, mate])

    info_in, info_out = slot_info(in_codes), slot_info(out_codes)
    w_in, w_out = w_in[0], w_out[0]
    tokens, upstream = own_pieces(tokens, tile), own_pieces(upstream, tile)
    args = (info_in, info_out, tokens, upstream, w_in, w_out, cols, devices)
    results = on_long_row(*args) if long_row() else on_line(*args)
    layer_out, grad_tokens, grad_w_in, grad_w_out = results
    return layer_out, grad_tokens, grad_w_in[None], grad_w_out[None]


def on_line(info_in, info_out, tokens, upstream, w_in, w_out, cols, devices):
    slots = w_in.shape[0]
    ends = (0, 3)
    mine = jnp.stack([tokens, upstream])
    both = line_gather(mine)
    in_pair = [w_in, swap_row(after(w_in, mine), 1)]
    token_even = across(jnp.stack([block[0] for block in both]))
    up_even = across(after(jnp.stack([block[1] for block in both]), token_even[1:]))
    all_tokens = with_odd(token_even)
    out_pair = [w_out, swap_row(after(w_out, all_tokens), 1)]
    own, far = to_hidden(info_in, all_tokens, in_pair, cols, False, ends)
    hidden = add(own, swap_row(far, 3))
    activ = silu(hidden)
    activ_far = swap_row(activ, 3)
    all_up = with_odd(after(up_even, own))
    own, far = to_hidden(info_out, after(all_up, activ), out_pair, cols, True, ends)
    far = swap_row(far, 3)
    ends_activ = after([activ, activ_far], own)
    layer_parts = from_hidden(info_out, ends_activ, out_pair, cols, False, ends, devices)
    grad_hidden = activations(hidden, add(own, after(far, layer_parts)))
    grad_far = swap_row(grad_hidden, 3)
    activ, activ_far = after((activ, activ_far), grad_hidden)
    all_activ = [activ, swap_row(activ, 1), swap_row(activ_far, 1), activ_far]
    layer_terms = col_terms(pair_sums(*after(layer_parts, grad_hidden)))
    layer_sums = add(*layer_terms).astype(jnp.bfloat16)
    ends_grad = after([grad_hidden, grad_far], layer_sums, all_activ[1])
    input_parts = from_hidden(info_in, ends_grad, in_pair, cols, True, ends, devices)
    layer_far = swap_row(layer_sums[1], 3)
    input_pairs = pair_sums(*input_parts)
    input_terms = col_terms(input_pairs)
    all_activ = after(all_activ, input_terms)
    grad_w_out = slot_grads(info_out, all_up, all_activ, slots, cols, False)
    grad_hidden, grad_far = after((grad_hidden, grad_far), input_pairs)
    near, far = swap_row(grad_hidden, 1), swap_row(grad_far, 1)
    input_sums = add(*after(input_terms, grad_w_out, near, far)).astype(jnp.bfloat16)
    all_grad = after([grad_hidden, near, far, grad_far], input_sums)
    grad_w_in = slot_grads(info_in, all_tokens, all_grad, slots, cols, True)
    input_far = after(swap_row(input_sums[1], 3), grad_w_in)
    layer_out = rows_first(add(layer_sums[0], after(layer_far, grad_w_in)))
    grad_tokens = rows_first(add(input_sums[0], input_far))
    return layer_out, grad_tokens, grad_w_in, grad_w_out


def on_long_row(info_in, info_out, tokens, upstream, w_in, w_out, cols, devices):
    slots, blocks = w_in.shape[0], lax.axis_size("row")

    def everywhere(x):
        return [lax.all_gather(lax.all_gather(x, "row"), "col")]

    def hidden_side(info, xs, w, flip):
        parts = jnp.stack(to_hidden(info, xs, [w], cols, flip, range(blocks)))
        return lax.psum_scatter(parts, "row", scatter_dimension=0).astype(jnp.float32)

    def wide_side(info, hs, w, flip):
        sums = []
        for chunk in chunks(blocks):
            if sums:
                hs, _ = lax.optimization_barrier((hs, sums[-1]))
            labels = range(blocks)[chunk]
            [parts] = from_hidden(info, [hs], [w], cols, flip, labels, devices)
            sums.append(lax.psum_scatter(parts, "col", scatter_dimension=0))
        total = lax.psum_scatter(jnp.concatenate(sums), "row", scatter_dimension=0)
        return rows_first(total)

    hidden = hidden_side(info_in, everywhere(tokens), w_in, False)
    upstream, hidden = lax.optimization_barrier((upstream, hidden))
    all_up = everywhere(upstream)
    grad_activ = hidden_side(info_out, all_up, w_out, True)
    all_activ = lax.all_gather(silu(hidden), "row")
    layer_out = wide_side(info_out, all_activ, w_out, False)
    grad_w_out = slot_grads(info_out, all_up, [all_activ], slots, cols, False)
    held = (activations(hidden, grad_activ), tokens, layer_out, grad_w_out)
    grad_hidden, tokens, layer_out, grad_w_out = lax.optimization_barrier(held)
    all_grad = lax.all_gather(grad_hidden, "row")
    grad_tokens = wide_side(info_in, all_grad, w_in, True)
    grad_w_in = slot_grads(info_in, everywhere(tokens), [all_grad], slots, cols, True)
    return layer_out, grad_tokens, grad_w_in, grad_w_out


def solution(mesh):
    placed = (
        P("row", "col"),
        P("row", "col"),
        P("col", "row", None, None),
        P("col", None),
        P("col", "row", None, None),
        P("col", None),
    )
    return jax.shard_map(
        per_device,
        mesh=mesh,
        in_specs=placed,
        out_specs=(
            P("row", "col"),
            P("row", "col"),
            P("col", "row", None, None),
            P("col", "row", None, None),
        ),
        check_vma=False,
    )
```

```python
import functools

import jax
import jax.numpy as jnp
from jax import lax
from jax.experimental import pallas as pl
from jax.experimental.pallas import tpu as pltpu
from jax.sharding import PartitionSpec as P

D = 4096
FF = 16384
VMEM = 56 * 1024 * 1024
GROUP = 4
ANY = pl.BlockSpec(memory_space=pl.ANY)


def matmul(a, b, a_dim, b_dim):
    return lax.dot_general(
        a, b, (((a_dim,), (b_dim,)), ((), ())), preferred_element_type=jnp.float32
    )


def flat(block):
    return block.reshape(block.shape[0] * block.shape[1], block.shape[2])


def chunks(blocks):
    group = min(blocks, GROUP)
    return [slice(at, at + group) for at in range(0, blocks, group)]


def tile_part(held, owner, q, pieces, unit):
    tile = held.shape[-1]
    if unit == tile:
        return owner * pieces + q, slice(None)
    parts = tile // unit
    lane = pl.multiple_of(lax.rem(owner, parts) * unit, unit)
    return lax.div(owner, parts), pl.ds(lane, unit)


def wide_copies(refs, labels, held, sems, col):
    copies = []
    if len(refs) == 1:
        pairs = [(m, refs[0].at[m]) for m in range(refs[0].shape[0])]
    else:
        pairs = [(lax.bitwise_xor(col, m), ref) for m, ref in enumerate(refs)]
    for owner, ref in pairs:
        blocks, pieces, _, unit = ref.shape
        whole = len(labels) == blocks
        for q in range(pieces):
            tile, lanes = tile_part(held, owner, q, pieces, unit)
            for g, t in [(slice(None), slice(None))] if whole else enumerate(labels):
                target = held.at[tile, g, :, lanes]
                copies.append(pltpu.make_async_copy(ref.at[t, q], target, sems.at[len(copies)]))
                copies[-1].start()
    return copies


def hidden_copies(refs, labels, held, sems, row):
    copies = []
    for g, t in enumerate(labels):
        source = refs[g] if len(refs) > 1 else refs[0].at[lax.bitwise_xor(row, t)]
        copies.append(pltpu.make_async_copy(source, held.at[:, g], sems.at[g]))
        copies[-1].start()
    return copies


def over_slots(info, first, slots, cols, body):
    step = 4 if slots % 4 == 0 else 1

    def some(at, carry):
        for s in [at * step + i for i in range(step)]:
            code = info[2 + first + s]
            tile = jnp.maximum(code, 0)
            body(s, code >= 0, lax.div(tile, cols), lax.rem(tile, cols))
        return carry

    lax.fori_loop(0, slots // step, some, 0)


def to_hidden_kernel(cols, flip, labels, wides, weights, info, *refs):
    w_refs, x_refs, refs = refs[:weights], refs[weights:weights + wides], refs[weights + wides:]
    *outs, x, acc, sems = refs
    copies = wide_copies(x_refs, labels, x, sems, info[1])
    acc[...] = jnp.zeros_like(acc)
    for copy in copies:
        copy.wait()

    for at, w_ref in enumerate(w_refs):
        def add(s, filled, wide, hidden, w_ref=w_ref):
            target = jnp.where(filled, hidden, acc.shape[0] - 1)
            for chunk in chunks(x.shape[1]):
                product = matmul(flat(x[wide, chunk]), w_ref[s], 1, 1 if flip else 0)
                acc[target, chunk] += product.reshape(-1, *acc.shape[2:])

        over_slots(info, at * w_ref.shape[0], w_ref.shape[0], cols, add)
    for part, out in enumerate(outs):
        out[...] = acc[:out.shape[0], part].astype(out.dtype)


def from_hidden_kernel(cols, flip, labels, hiddens, weights, info, *refs):
    w_refs, h_refs = refs[:weights], refs[weights:weights + hiddens]
    *outs, h, acc, sems = refs[weights + hiddens:]
    copies = hidden_copies(h_refs, labels, h, sems, info[0])
    acc[...] = jnp.zeros_like(acc)
    for copy in copies:
        copy.wait()

    for at, w_ref in enumerate(w_refs):
        def add(s, filled, wide, hidden, w_ref=w_ref):
            target = jnp.where(filled, wide, acc.shape[0] - 1)
            for chunk in chunks(h.shape[1]):
                product = matmul(flat(h[hidden, chunk]), w_ref[s], 1, 1 if flip else 0)
                acc[target, chunk] += product.reshape(-1, *acc.shape[2:])

        over_slots(info, at * w_ref.shape[0], w_ref.shape[0], cols, add)
    for at, out in enumerate(outs):
        pieces, unit = out.shape[-3], out.shape[-1]
        for m in range(out.shape[0]):
            owner = m if len(outs) == 1 else lax.bitwise_xor(info[1], 2 * m + at)
            for q in range(pieces):
                tile, lanes = tile_part(acc, owner, q, pieces, unit)
                out[m, :, q] = acc[tile, :, :, lanes].astype(out.dtype)


def grad_kernel(cols, flip, wides, labels, info, *refs):
    x_refs, h_refs = refs[:wides], refs[wides:-5]
    out, x, h, x_sems, h_sems = refs[-5:]
    copies = wide_copies(x_refs, labels, x, x_sems, info[1])
    copies += hidden_copies(h_refs, labels, h, h_sems, info[0])
    for copy in copies:
        copy.wait()

    def add(s, filled, wide, hidden):
        total = 0.0
        for chunk in chunks(x.shape[1]):
            a, b = flat(x[wide, chunk]), flat(h[hidden, chunk])
            a, b = (a, b) if flip else (b, a)
            total += matmul(a, b, 0, 0)
        out[s] = jnp.where(filled, total, 0.0).astype(out.dtype)

    over_slots(info, 0, out.shape[0], cols, add)


def call(kernel, out_shape, scratch, flops, moved, *args):
    return pl.pallas_call(
        kernel,
        out_shape=out_shape,
        in_specs=[pl.BlockSpec(memory_space=pltpu.SMEM)] + args[1],
        out_specs=jax.tree.map(lambda _: pl.BlockSpec(memory_space=pltpu.VMEM), out_shape),
        scratch_shapes=scratch,
        compiler_params=pltpu.CompilerParams(vmem_limit_bytes=VMEM),
        cost_estimate=pl.CostEstimate(flops=flops, bytes_accessed=moved, transcendentals=0),
    )(args[0], *args[2])


def wide_scratch(labels, rows, tile, unit):
    group = len(labels)
    held = pltpu.VMEM((D // tile, group, rows, tile), jnp.bfloat16)
    return [held, pltpu.SemaphoreType.DMA((D // unit * group,))]


def to_hidden(info, xs, ws, cols, flip, labels):
    rows, unit = xs[0].shape[-2:]
    slots, tile, _ = ws[0].shape
    group = len(labels)
    outs = [jax.ShapeDtypeStruct((cols, rows, tile), jnp.bfloat16)] * group
    held, sems = wide_scratch(labels, rows, tile, unit)
    scratch = [held, pltpu.VMEM((cols + 1, group, rows, tile), jnp.float32), sems]
    kernel = functools.partial(to_hidden_kernel, cols, flip, labels, len(xs), len(ws))
    specs = [pl.BlockSpec(memory_space=pltpu.VMEM)] * len(ws) + [ANY] * len(xs)
    flops = 2 * len(ws) * slots * group * rows * tile * tile
    return call(kernel, outs, scratch, flops, 8 << 20, info, specs, [*ws, *xs])


def from_hidden(info, hs, ws, cols, flip, labels, devices):
    rows, tile = hs[0].shape[-2:]
    slots, group = ws[0].shape[0], len(labels)
    unit = min(tile, D // devices)
    pieces = D // devices // unit
    shape = (group, pieces, rows, unit)
    if long_row():
        outs = [jax.ShapeDtypeStruct((devices, *shape), jnp.bfloat16)]
    else:
        outs = [jax.ShapeDtypeStruct((devices // 2, *shape), jnp.bfloat16)] * 2
    scratch = [
        pltpu.VMEM((cols, group, rows, tile), jnp.bfloat16),
        pltpu.VMEM((D // tile + 1, group, rows, tile), jnp.float32),
        pltpu.SemaphoreType.DMA((group,)),
    ]
    kernel = functools.partial(from_hidden_kernel, cols, flip, labels, len(hs), len(ws))
    specs = [pl.BlockSpec(memory_space=pltpu.VMEM)] * len(ws) + [ANY] * len(hs)
    flops = 2 * len(ws) * slots * group * rows * tile * tile
    return call(kernel, outs, scratch, flops, 8 << 20, info, specs, [*ws, *hs])


def slot_grads(info, xs, hs, slots, cols, flip):
    blocks = lax.axis_size("row")
    labels = range(blocks)
    rows, unit = xs[0].shape[-2:]
    tile = hs[0].shape[-1]
    out = jax.ShapeDtypeStruct((slots, tile, tile), jnp.bfloat16)
    held, sems = wide_scratch(labels, rows, tile, unit)
    scratch = [
        held,
        pltpu.VMEM((cols, blocks, rows, tile), jnp.bfloat16),
        sems,
        pltpu.SemaphoreType.DMA((blocks,)),
    ]
    kernel = functools.partial(grad_kernel, cols, flip, len(xs), labels)
    specs = [ANY] * (len(xs) + len(hs))
    flops = 2 * slots * blocks * rows * tile * tile
    return call(kernel, out, scratch, flops, 8 << 20, info, specs, [*xs, *hs])


def long_row():
    return lax.axis_size("row") != 4


def swap_col(x, m):
    count = lax.axis_size("col")
    return lax.ppermute(x, "col", [(s, s ^ m) for s in range(count)])


def swap_row(x, t):
    return lax.ppermute(x, "row", [(s, s ^ t) for s in range(4)])


def own_pieces(x, tile):
    rows, width = x.shape
    unit = min(width, tile)
    return jnp.swapaxes(x.reshape(rows, width // unit, unit), 0, 1)


def after(values, *others):
    return lax.optimization_barrier((values, others))[0]


def across(mine):
    return [swap_col(mine, m) if m else mine for m in range(0, lax.axis_size("col"), 2)]


def with_odd(even):
    return [x for own in even for x in (own, swap_col(own, 1))]


def add(*terms):
    return sum(term.astype(jnp.float32) for term in terms)


def line_gather(x):
    return [x] + [swap_row(x, t) for t in range(1, 4)]


def pair_sums(even, odd):
    return add(even, swap_col(odd, 1)).astype(jnp.bfloat16)


def col_terms(pairs):
    return [pairs[0]] + [swap_col(pairs[m], 2 * m) for m in range(1, pairs.shape[0])]


def rows_first(total):
    return jnp.swapaxes(total, 0, 1).reshape(total.shape[1], -1).astype(jnp.bfloat16)


def activations(hidden, grad_activ):
    sigmoid = jax.nn.sigmoid(hidden)
    slope = sigmoid * (1.0 + hidden * (1.0 - sigmoid))
    return (grad_activ * slope).astype(jnp.bfloat16)


def silu(hidden):
    return (hidden * jax.nn.sigmoid(hidden)).astype(jnp.bfloat16)


def per_device(tokens, upstream, w_in, in_codes, w_out, out_codes):
    tile = w_in.shape[3]
    slots = w_in.shape[1]
    devices = lax.axis_size("col")
    cols = FF // (tile * devices)
    row, col = lax.axis_index("row"), lax.axis_index("col")

    def slot_info(codes):
        own = lax.dynamic_slice_in_dim(codes[0], row * slots, slots)
        mate = lax.dynamic_slice_in_dim(codes[0], (row ^ 1) * slots, slots)
        place = jnp.stack([row, col]).astype(jnp.int32)
        return jnp.concatenate([place, own, mate])

    info_in, info_out = slot_info(in_codes), slot_info(out_codes)
    w_in, w_out = w_in[0], w_out[0]
    tokens, upstream = own_pieces(tokens, tile), own_pieces(upstream, tile)
    args = (info_in, info_out, tokens, upstream, w_in, w_out, cols, devices)
    results = on_long_row(*args) if long_row() else on_line(*args)
    layer_out, grad_tokens, grad_w_in, grad_w_out = results
    return layer_out, grad_tokens, grad_w_in[None], grad_w_out[None]


def on_line(info_in, info_out, tokens, upstream, w_in, w_out, cols, devices):
    slots = w_in.shape[0]
    ends = (0, 3)
    mine = jnp.stack([tokens, upstream])
    both = line_gather(mine)
    in_pair = [w_in, swap_row(after(w_in, mine), 1)]
    token_even = across(jnp.stack([block[0] for block in both]))
    up_even = across(after(jnp.stack([block[1] for block in both]), token_even[1:]))
    all_tokens = with_odd(token_even)
    out_pair = [w_out, swap_row(after(w_out, all_tokens), 1)]
    own, far = to_hidden(info_in, all_tokens, in_pair, cols, False, ends)
    hidden = add(own, swap_row(far, 3))
    activ = silu(hidden)
    activ_far = swap_row(activ, 3)
    all_up = with_odd(after(up_even, own))
    own, far = to_hidden(info_out, after(all_up, activ), out_pair, cols, True, ends)
    far = swap_row(far, 3)
    ends_activ = after([activ, activ_far], own)
    layer_parts = from_hidden(info_out, ends_activ, out_pair, cols, False, ends, devices)
    grad_hidden = activations(hidden, add(own, after(far, layer_parts)))
    grad_far = swap_row(grad_hidden, 3)
    activ, activ_far = after((activ, activ_far), grad_hidden)
    all_activ = [activ, swap_row(activ, 1), swap_row(activ_far, 1), activ_far]
    layer_terms = col_terms(pair_sums(*after(layer_parts, grad_hidden)))
    layer_sums = add(*layer_terms).astype(jnp.bfloat16)
    ends_grad = after([grad_hidden, grad_far], layer_sums, all_activ[1])
    input_parts = from_hidden(info_in, ends_grad, in_pair, cols, True, ends, devices)
    layer_far = swap_row(layer_sums[1], 3)
    input_pairs = pair_sums(*input_parts)
    input_terms = col_terms(input_pairs)
    all_activ = after(all_activ, input_terms)
    grad_w_out = slot_grads(info_out, all_up, all_activ, slots, cols, False)
    grad_hidden, grad_far = after((grad_hidden, grad_far), input_pairs)
    near, far = swap_row(grad_hidden, 1), swap_row(grad_far, 1)
    input_sums = add(*after(input_terms, grad_w_out, near, far)).astype(jnp.bfloat16)
    all_grad = after([grad_hidden, near, far, grad_far], input_sums)
    grad_w_in = slot_grads(info_in, all_tokens, all_grad, slots, cols, True)
    input_far = after(swap_row(input_sums[1], 3), grad_w_in)
    layer_out = rows_first(add(layer_sums[0], after(layer_far, input_sums)))
    grad_tokens = rows_first(add(input_sums[0], input_far))
    return layer_out, grad_tokens, grad_w_in, grad_w_out


def on_long_row(info_in, info_out, tokens, upstream, w_in, w_out, cols, devices):
    slots, blocks = w_in.shape[0], lax.axis_size("row")

    def everywhere(x):
        return [lax.all_gather(lax.all_gather(x, "row"), "col")]

    def hidden_side(info, xs, w, flip):
        parts = jnp.stack(to_hidden(info, xs, [w], cols, flip, range(blocks)))
        return lax.psum_scatter(parts, "row", scatter_dimension=0).astype(jnp.float32)

    def wide_side(info, hs, w, flip):
        sums = []
        for chunk in chunks(blocks):
            if sums:
                hs, _ = lax.optimization_barrier((hs, sums[-1]))
            labels = range(blocks)[chunk]
            [parts] = from_hidden(info, [hs], [w], cols, flip, labels, devices)
            sums.append(lax.psum_scatter(parts, "col", scatter_dimension=0))
        total = lax.psum_scatter(jnp.concatenate(sums), "row", scatter_dimension=0)
        return rows_first(total)

    hidden = hidden_side(info_in, everywhere(tokens), w_in, False)
    upstream, hidden = lax.optimization_barrier((upstream, hidden))
    all_up = everywhere(upstream)
    grad_activ = hidden_side(info_out, all_up, w_out, True)
    all_activ = lax.all_gather(silu(hidden), "row")
    layer_out = wide_side(info_out, all_activ, w_out, False)
    grad_w_out = slot_grads(info_out, all_up, [all_activ], slots, cols, False)
    held = (activations(hidden, grad_activ), tokens, layer_out, grad_w_out)
    grad_hidden, tokens, layer_out, grad_w_out = lax.optimization_barrier(held)
    all_grad = lax.all_gather(grad_hidden, "row")
    grad_tokens = wide_side(info_in, all_grad, w_in, True)
    grad_w_in = slot_grads(info_in, everywhere(tokens), [all_grad], slots, cols, True)
    return layer_out, grad_tokens, grad_w_in, grad_w_out


def solution(mesh):
    placed = (
        P("row", "col"),
        P("row", "col"),
        P("col", "row", None, None),
        P("col", None),
        P("col", "row", None, None),
        P("col", None),
    )
    return jax.shard_map(
        per_device,
        mesh=mesh,
        in_specs=placed,
        out_specs=(
            P("row", "col"),
            P("row", "col"),
            P("col", "row", None, None),
            P("col", "row", None, None),
        ),
        check_vma=False,
    )
```
